512 devices in a mesh: expert: 8 (over z), blk: 32 (over y, x_lo, core), dp: 2 (over x_hi).
Axes of the slice: x: 4 (x_hi: 2, x_lo: 2; x = x_hi * 2 + x_lo), y: 8, z: 8, core: 2. Of those that a mesh axis runs over, the one named last changes fastest.
Arguments:
- cotangent: bfloat16 [2, 1536, 6144], P('dp', 'expert', 'blk'), may hold values from -6 to 6
- expert_ids: int32 [2, 1536, 2], P('dp', 'expert'), may hold values from 0 to 7, all different within a row; in each aligned block of 192 rows (0 to 191, 192 to 383, ..., all dimensions but the last counted through in order) at most 96 rows name the same one
- combine: float32 [2, 8, 768], P('dp', 'expert'), may hold values from 0.1 to 0.9
- gate_saved: bfloat16 [2, 8, 768, 8192], P('dp', 'expert', None, 'blk'), may hold values from -6 to 6
- up_saved: bfloat16 [2, 8, 768, 8192], P('dp', 'expert', None, 'blk'), may hold values from -6 to 6
- w_down: bfloat16 [8, 6144, 8192], P('expert', 'dp', 'blk'), may hold values from -0.0625 to 0.0625
Outputs:
- grad_gate: bfloat16 [2, 8, 768, 8192], P('dp', 'expert', None, 'blk')
- grad_up: bfloat16 [2, 8, 768, 8192], P('dp', 'expert', None, 'blk')
- grad_weight: bfloat16 [8, 6144, 8192], P('expert', 'dp', 'blk')
- grad_combine: float32 [2, 8, 768], P('dp', 'expert', 'blk')
The draws below stay inside these ranges and needn't reach their ends.
Inputs may be any that keep to these rules, and one draw needn't show every extreme that they name: `expert_ids`: each token names 2 different experts. In each aligned block of 192 tokens (the tokens of one owner) no expert is named by more than 96 tokens, and in some block some expert is named by exactly 96.
All inputs are finite; a program needn't handle non-finite values.
Results may differ from the reference program's by a relative error of at most 0.01.
Values may be sent and summed in bfloat16 or wider, within the bound.
No kernel may reach another device: no remote copies, remote signals or barrier semaphores. Data moves between devices by JAX's collectives and lax.ppermute only.
A program may use at most 128 MiB of HBM per device.

```python
import math
import jax
import jax.numpy as jnp
import numpy as np
from jax import lax

D = 6144
FF = 8192
TOP = 2
TOK_DEV = 192
EXPERTS = 8
CAP = 96
COPIES = 2
GROUP_TOKENS = 1536
ROWS = 768
N_EXPERT = 8


def with_spikes(values, rng, source, target, shards_of, factor):
    owner, partner = [(jnp.arange(values.shape[dim]) // (values.shape[dim] // shards_of)).reshape([-1 if axis == dim else 1 for axis in range(values.ndim)]) for dim in (source, target)]
    chosen = jax.random.permutation(rng, shards_of)[partner]
    strong = (owner == chosen) | (owner == (partner + shards_of // 2) % shards_of)
    return jnp.where(strong, factor * values, values)


def block_levels(key, shape, split, smallest, top_value):
    loudness, own = 1.0, jax.random.fold_in(key, 6)
    for dim, blocks in split:
        heights = jnp.exp(jax.random.uniform(jax.random.fold_in(own, dim), (blocks,), jnp.float32, smallest / len(split), top_value / len(split)))
        loudness = loudness * jnp.repeat(heights, shape[dim] // blocks).reshape([-1 if axis == dim else 1 for axis in range(len(shape))])
    return loudness


def deal_out(own_key, own, number, rows, amount, top, bound, skew):
    sequence = jax.random.permutation(own_key, amount)
    heavy_load, common = shares(amount, rows * top, bound, skew, True), shares(amount, rows * top, bound, skew, False)
    places = jnp.arange(amount)

    def named(tallies, offset_by):
        used = int((tallies > 0).sum())
        fixed = max(1, used // 4)
        shifted = fixed + (places - fixed + offset_by * (used - fixed)) % max(1, amount - fixed)
        return jnp.zeros((amount,), jnp.int32).at[sequence[jnp.where(places < fixed, places, shifted)]].set(jnp.asarray(tallies, jnp.int32))

    tallies = jnp.where(number % 4 == 0, named(heavy_load, number // 4), named(common, number - number // 4 - 1))
    mixed = jax.random.permutation(jax.random.fold_in(own, 3), amount)
    source_of, receiver = mixed[0:amount // 2 * 2:2], mixed[1:amount // 2 * 2:2]
    slack = jnp.minimum(tallies[source_of] - 1, bound - tallies[receiver]) // 2
    slack = jnp.where((source_of == sequence[0]) | (receiver == sequence[0]) | (tallies[receiver] == 0), 0, jnp.maximum(slack, 0))
    shifted = jax.random.randint(jax.random.fold_in(own, 4), (amount // 2,), 0, 1 << 20) % (slack + 1)
    tallies = tallies.at[source_of].add(-shifted).at[receiver].add(shifted)
    members = jnp.searchsorted(jnp.cumsum(tallies), jnp.arange(rows * top), side="right").astype(jnp.int32)
    grid = members.reshape(top, rows).T
    grid = grid[jax.random.permutation(jax.random.fold_in(own, 1), rows)]
    offset_by = jax.random.randint(jax.random.fold_in(own, 2), (rows, 1), 0, top)
    return jnp.take_along_axis(grid, (jnp.arange(top)[None, :] + offset_by) % top, axis=1)


def shares(count, total, bound, lean, full):
    portions = [(1 << 20) // math.isqrt(standing ** lean) + 1 for standing in range(1, count + 1)]
    largest = bound if full else min(bound, max(-(-total // count), total * portions[0] // sum(portions)))
    least = 1 if total - largest >= count - 1 else 0
    holding, surplus = [largest] + [least] * (count - 1), total - largest - least * (count - 1)
    while surplus > 0:
        movable = [i for i in range(1, count) if holding[i] < largest] or [i for i in range(1, count) if holding[i] < bound]
        pool, left = sum([portions[i] for i in movable]), surplus
        for i in movable:
            more = min(bound - holding[i], max(1, left * portions[i] // pool), surplus)
            holding[i] = holding[i] + more
            surplus = surplus - more
    return np.array(holding)


def normal_values(key, extent, deviation, bound, cuts=(), kind=jnp.bfloat16):
    values = jax.random.normal(key, extent, jnp.float32) * deviation
    if len(cuts) > 0:
        values = block_levels(key, extent, cuts, -0.22, 0.18) * values
    return jnp.clip(values, min=-bound, max=bound).astype(kind)


def gaussian_with(stream_key, shape, spread, reach, shards, heavy, kind=jnp.bfloat16):
    values = spread * jax.random.normal(stream_key, shape, jnp.float32)
    if shards:
        values = values * block_levels(stream_key, shape, shards, -0.22, 0.18)
    return jnp.clip(with_spikes(values, jax.random.fold_in(stream_key, 3), *heavy), -reach, reach).astype(kind)


def setup_inputs(seed: int = 0) -> dict:
    streams_of = jax.random.split(jax.random.key(seed), 7)
    cotangent = normal_values(streams_of[0], (COPIES, GROUP_TOKENS, D), 1.0, 6.0, ((0, 2), (1, 8), (2, 32)))
    expert_ids_keys = jax.random.split(jax.random.fold_in(streams_of[1], 1), COPIES * GROUP_TOKENS // TOK_DEV)
    expert_ids_turns = jax.random.permutation(jax.random.fold_in(streams_of[1], 3), COPIES * GROUP_TOKENS // TOK_DEV)
    expert_ids = jax.vmap(lambda own, number: deal_out(jax.random.fold_in(streams_of[1], 2), own, number, TOK_DEV, EXPERTS, TOP, CAP, 2))(expert_ids_keys, expert_ids_turns).reshape((COPIES, GROUP_TOKENS, TOP))
    combine = jnp.clip(0.1 + 0.79999997 * jax.random.uniform(streams_of[2], (COPIES, EXPERTS, ROWS), jnp.float32) ** block_levels(streams_of[2], (COPIES, EXPERTS, ROWS), ((0, 2), (1, 8)), -0.2, 0.2), 0.1, 0.9)
    gate_saved = gaussian_with(streams_of[3], (COPIES, EXPERTS, ROWS, FF), 1.0, 6.0, ((0, 2), (1, 8), (3, 32)), (3, 2, 32, 2.75))
    up_saved = normal_values(streams_of[4], (COPIES, EXPERTS, ROWS, FF), 1.0, 6.0, ((0, 2), (1, 8), (3, 32)))
    w_down = normal_values(streams_of[5], (EXPERTS, D, FF), FF ** -0.5, 0.0625, ((0, 8), (1, 2), (2, 32)))
    return dict(cotangent=cotangent, expert_ids=expert_ids, combine=combine, gate_saved=gate_saved, up_saved=up_saved, w_down=w_down)


def dispatch_tables(routing, expert_count, capacity):
    experts = jnp.arange(expert_count, dtype=jnp.int32)
    chosen = (routing[..., None] == experts).astype(jnp.int32)
    per_token = jnp.sum(chosen, axis=-2)
    earlier = jnp.cumsum(per_token, axis=-2) - per_token
    position = jnp.sum(chosen * earlier[..., None, :], axis=-1)
    target = jnp.sum(chosen * experts, axis=-1) * capacity + position
    columns = jnp.arange(expert_count * capacity, dtype=jnp.int32)
    matches = target[..., None, :, :] == columns[:, None, None]
    return jnp.sum(matches.astype(jnp.float32), axis=-1)


def reference(cotangent, expert_ids, combine, gate_saved, up_saved, w_down):
    copies = cotangent.shape[0]
    owners = N_EXPERT
    tokens = cotangent.reshape(copies, owners, TOK_DEV, D).astype(jnp.float32)
    routing = expert_ids.reshape(copies, owners, TOK_DEV, TOP).astype(jnp.int32)
    tables = dispatch_tables(routing, EXPERTS, CAP)
    filled = jnp.einsum("cost,cotw->cosw", tables, tokens)
    filled = filled.reshape(copies, owners, EXPERTS, CAP, D)
    dispatched = jnp.transpose(filled, (0, 2, 1, 3, 4)).reshape(copies, EXPERTS, ROWS, D).astype(jnp.bfloat16)

    def one_expert(operands):
        slot_rows, gate_rows, upper_rows, weights, combine_rows = operands
        gate_out = []
        upper_out = []
        mixing_out = []
        total = jnp.zeros((D, FF), jnp.float32)
        for member in range(copies):
            grad_hidden = jnp.dot(slot_rows[member], weights, preferred_element_type=jnp.float32)
            gate_float = gate_rows[member].astype(jnp.float32)
            upper_float = upper_rows[member].astype(jnp.float32)
            sigmoid_gate = jax.nn.sigmoid(gate_float)
            activated = gate_float * sigmoid_gate
            hidden = activated * upper_float
            weighted = combine_rows[member][:, None] * grad_hidden
            gate_out.append((weighted * upper_float * sigmoid_gate * (1.0 + gate_float * (1.0 - sigmoid_gate))).astype(jnp.bfloat16))
            upper_out.append((weighted * activated).astype(jnp.bfloat16))
            scaled = (combine_rows[member][:, None] * hidden).astype(jnp.bfloat16)
            partial_value = jnp.dot(slot_rows[member].T, scaled, preferred_element_type=jnp.float32).astype(jnp.bfloat16)
            partial_value = lax.optimization_barrier(partial_value)
            total = total + partial_value.astype(jnp.float32)
            mixing_out.append(jnp.sum(hidden * grad_hidden, axis=1))
        return jnp.stack(gate_out), jnp.stack(upper_out), total.astype(jnp.bfloat16), jnp.stack(mixing_out)

    operands = (jnp.transpose(dispatched, (1, 0, 2, 3)), jnp.transpose(gate_saved, (1, 0, 2, 3)), jnp.transpose(up_saved, (1, 0, 2, 3)), w_down, jnp.transpose(combine, (1, 0, 2)))
    grad_gate, grad_up, grad_weight, grad_combine = lax.map(one_expert, operands)
    return (jnp.transpose(grad_gate, (1, 0, 2, 3)), jnp.transpose(grad_up, (1, 0, 2, 3)), grad_weight, jnp.transpose(grad_combine, (1, 0, 2)))
```

```python
import jax
import jax.numpy as jnp
from jax import lax
from jax.sharding import Mesh, PartitionSpec as P

BF = jnp.bfloat16
F32 = jnp.float32


def one_hot_table(ids, expert_count, capacity, core):
    half = capacity // 2
    experts = jnp.arange(expert_count, dtype=jnp.int32)
    chosen = (ids[:, :, None] == experts).astype(F32)
    per_token = jnp.sum(chosen, axis=1)
    count = ids.shape[0]
    before = (jnp.arange(count)[:, None] > jnp.arange(count)[None, :]).astype(BF)
    earlier = jnp.dot(before, per_token.astype(BF), preferred_element_type=F32)
    position = jnp.sum(chosen * earlier[:, None, :], axis=-1).astype(jnp.int32)
    target = ids * capacity + position
    rows = jnp.arange(expert_count * half, dtype=jnp.int32)
    columns = (rows // half) * capacity + core * half + rows % half
    hit = (target[:, 0][None, :] == columns[:, None]) | (target[:, 1][None, :] == columns[:, None])
    return hit.astype(BF)


def make_local(ny):
    half_y = ny // 2

    def token_moves(other_core):
        def flat(y, x, c, d):
            return ((y * 2 + x) * 2 + c) * 2 + d

        pairs = []
        for y in range(ny):
            for x in range(2):
                for c in range(2):
                    for d in range(2):
                        h = y // half_y
                        to_y = (y % half_y) * 2 + x
                        to_x = 0 if d == h else 1
                        to_c = 1 - c if other_core else c
                        pairs.append((flat(y, x, c, d), flat(to_y, to_x, to_c, h)))
        return pairs

    ring = [(y * 2, ((y + 1) % ny) * 2) for y in range(ny)] + [
        (y * 2 + 1, ((y - 1) % ny) * 2 + 1) for y in range(ny)
    ]
    swap = [(0, 1), (1, 0)]

    def on_ring(x):
        return lax.ppermute(x, ("y", "core"), ring)

    def on_core(x):
        return lax.ppermute(x, "core", swap)

    def local(cotangent, expert_ids, combine, gate_saved, up_saved, w_down):
        expert_count = lax.axis_size("expert")
        y = lax.axis_index("y")
        core = lax.axis_index("core")
        xlo = lax.axis_index("xlo")
        dp = lax.axis_index("dp")
        rows = gate_saved.shape[2]
        width = gate_saved.shape[3]
        capacity = rows // expert_count
        half = capacity // 2
        lanes = cotangent.shape[2]
        chip = 2 * lanes

        ids = expert_ids[0].astype(BF)
        moved = lax.ppermute(
            jnp.concatenate([cotangent[0], ids], axis=1), ("y", "xlo", "core", "dp"), token_moves(False)
        )
        across = lax.ppermute(cotangent[0], ("y", "xlo", "core", "dp"), token_moves(True))
        mine = moved[:, :lanes]
        first = jnp.where(core == 0, mine, across)
        second = jnp.where(core == 0, across, mine)
        tokens = jnp.concatenate([first, second], axis=1)
        table = one_hot_table(moved[:, lanes:].astype(jnp.int32), expert_count, capacity, core)
        outgoing = jnp.dot(table, tokens, preferred_element_type=F32).astype(BF)
        outgoing = outgoing.reshape(expert_count, half, chip)
        part = lax.all_to_all(outgoing, "expert", split_axis=0, concat_axis=0, tiled=True)

        gate = gate_saved[0, 0].astype(F32)
        upper = up_saved[0, 0].astype(F32)
        weight_rows = combine[0, 0][:, None]
        sigma = jax.nn.sigmoid(gate)
        active = gate * sigma
        scaled = (weight_rows * (active * upper)).astype(BF)
        scaled_other = lax.ppermute(scaled, "dp", swap)

        def whole(a, b):
            lo = jnp.where(core == 0, a, b)
            hi = jnp.where(core == 0, b, a)
            return jnp.stack([lo, hi], axis=1).reshape(rows, chip)

        part_x = lax.ppermute(part, "xlo", swap)
        mine_rows = whole(part, on_core(part))
        x_rows = whole(part_x, on_core(part_x))
        own = jnp.where(xlo == 0, mine_rows, x_rows)
        other = jnp.where(xlo == 0, x_rows, mine_rows)

        w = w_down[0]
        state = dict(own=jnp.zeros((rows, width), F32), other=jnp.zeros((rows, width), F32))
        grad_weight = jnp.zeros((w.shape[0], width), BF)

        def use(state, grad_weight, block, own, other):
            w_block = lax.dynamic_slice_in_dim(w, block * chip, chip, 0)
            state = dict(
                own=state["own"] + jnp.dot(own, w_block, preferred_element_type=F32),
                other=state["other"] + jnp.dot(other, w_block, preferred_element_type=F32),
            )
            dims = (((0,), (0,)), ((), ()))
            piece = lax.dot_general(own, scaled, dims, preferred_element_type=F32) + lax.dot_general(
                other, scaled_other, dims, preferred_element_type=F32
            )
            return state, lax.dynamic_update_slice_in_dim(grad_weight, piece.astype(BF), block * chip, 0)

        state, grad_weight = use(state, grad_weight, y, own, other)
        turn = jnp.where(core == 0, -1, 1)
        for step in range(1, half_y):
            other = on_ring(other)
            own = on_ring(own)
            other_c = on_core(other)
            own_c = on_core(own)
            state, grad_weight = use(state, grad_weight, (y + turn * step + ny) % ny, own, other)
            state, grad_weight = use(state, grad_weight, (y - turn * step + ny) % ny, own_c, other_c)
        mid = rows // 2
        cut = lambda a: on_ring(lax.dynamic_slice_in_dim(a, core * mid, mid, 0))
        other = cut(other)
        own = cut(own)

        def join(a):
            b = on_core(a)
            return jnp.concatenate([jnp.where(core == 0, a, b), jnp.where(core == 0, b, a)], axis=0)

        state, grad_weight = use(state, grad_weight, (y + half_y) % ny, join(own), join(other))

        arrived = lax.ppermute(state["other"].astype(BF), "dp", swap)
        mix_own = jnp.sum(scaled.astype(F32) * state["own"], axis=1)
        mix_other = jnp.sum(scaled_other.astype(F32) * state["other"], axis=1)
        mix = jnp.stack([jnp.where(dp == 0, mix_own, mix_other), jnp.where(dp == 0, mix_other, mix_own)])
        group = ("dp", "y", "xlo", "core")
        members = 2 * ny * 4
        share = rows // (ny * 4)
        mix = lax.all_to_all(mix.reshape(members, share), group, 0, 0, tiled=True)
        mix = jnp.sum(mix, axis=0)
        blk = (y * 2 + xlo) * 2 + core
        mix = mix / lax.dynamic_slice_in_dim(combine[0, 0], blk * share, share, 0)

        grad_hidden = state["own"] + arrived.astype(F32)
        weighted = weight_rows * grad_hidden
        grad_gate = (weighted * upper * sigma * (1.0 + gate * (1.0 - sigma))).astype(BF)
        grad_upper = (weighted * active).astype(BF)
        return grad_gate[None, None], grad_upper[None, None], grad_weight[None], mix[None, None]

    return local


def solution(mesh):
    ne, nb, nd = mesh.devices.shape
    fine = Mesh(mesh.devices.reshape(ne, nb // 4, 2, 2, nd), ("expert", "y", "xlo", "core", "dp"))
    blk = ("y", "xlo", "core")
    return jax.shard_map(
        make_local(nb // 4),
        mesh=fine,
        in_specs=(
            P("dp", "expert", blk),
            P("dp", "expert", None),
            P("dp", "expert", None),
            P("dp", "expert", None, blk),
            P("dp", "expert", None, blk),
            P("expert", "dp", blk),
        ),
        out_specs=(
            P("dp", "expert", None, blk),
            P("dp", "expert", None, blk),
            P("expert", "dp", blk),
            P("dp", "expert", blk),
        ),
        check_vma=False,
    )
```

```python
import functools

import jax
import jax.numpy as jnp
from jax import lax
from jax.experimental import pallas as pl
from jax.experimental.pallas import tpu as pltpu
from jax.sharding import Mesh, PartitionSpec as P

BF = jnp.bfloat16
F32 = jnp.float32
VMEM_LIMIT = 32 * 1024 * 1024


def one_hot_table(ids, expert_count, capacity, part):
    half = capacity // 2
    experts = jnp.arange(expert_count, dtype=jnp.int32)
    chosen = (ids[:, :, None] == experts).astype(F32)
    per_token = jnp.sum(chosen, axis=1)
    count = ids.shape[0]
    before = (jnp.arange(count)[:, None] > jnp.arange(count)[None, :]).astype(BF)
    earlier = jnp.dot(before, per_token.astype(BF), preferred_element_type=F32)
    position = jnp.sum(chosen * earlier[:, None, :], axis=-1).astype(jnp.int32)
    target = ids * capacity + position
    rows = jnp.arange(expert_count * half, dtype=jnp.int32)
    columns = (rows // half) * capacity + part * half + rows % half
    hit = (target[:, 0][None, :] == columns[:, None]) | (target[:, 1][None, :] == columns[:, None])
    return hit.astype(BF)


def use_kernel(layout, first, *refs):
    pieces = sum(len(b) for b in layout)
    blocks = len(layout)
    it = iter(refs[1:])
    x_refs = [next(it) for _ in range(pieces)]
    w_mine = [next(it) for _ in range(blocks)]
    w_theirs = [next(it) for _ in range(blocks)]
    s_mine, s_theirs = next(it), next(it)
    acc_in = None if first else next(it)
    acc, g_mine, g_theirs = next(it), next(it), next(it)
    width = s_mine.shape[1]
    touched = set()
    n = 0
    for b in range(blocks):
        w = jnp.concatenate([w_mine[b][0], w_theirs[b][0]], axis=1)
        total = None
        for _, start, rows in layout[b]:
            x = x_refs[n][...]
            n += 1
            span = pl.ds(start, rows)
            product = jnp.dot(x, w, preferred_element_type=F32)
            if start not in touched:
                touched.add(start)
                if not first:
                    product = product + acc_in[span, :]
            else:
                product = product + acc[span, :]
            acc[span, :] = product
            s = jnp.concatenate([s_mine[span, :], s_theirs[span, :]], axis=1)
            outer = lax.dot_general(x, s, (((0,), (0,)), ((), ())), preferred_element_type=F32)
            total = outer if total is None else total + outer
        g_mine[b] = total[:, :width].astype(BF)
        g_theirs[b] = total[:, width:].astype(BF)


def use(layout, pieces, index, w_mine, w_theirs, s_mine, s_theirs, acc):
    first = acc is None
    blocks = len(layout)
    rows, width = s_mine.shape
    chip = pieces[0].shape[1]

    def whole(a):
        return pl.BlockSpec(a.shape, lambda i, idx: (0,) * a.ndim)

    def pick(j):
        return pl.BlockSpec((1, chip, width), lambda i, idx: (idx[j], 0, 0))

    ins = list(pieces) + [w_mine] * blocks + [w_theirs] * blocks + [s_mine, s_theirs]
    specs = [whole(a) for a in pieces] + [pick(j) for j in range(blocks)] * 2 + [whole(s_mine), whole(s_theirs)]
    aliases = {}
    if not first:
        aliases = {1 + len(ins): 0}
        ins.append(acc)
        specs.append(whole(acc))
    outs = [
        jax.ShapeDtypeStruct((rows, 2 * width), F32),
        jax.ShapeDtypeStruct((blocks, chip, width), BF),
        jax.ShapeDtypeStruct((blocks, chip, width), BF),
    ]
    return pl.pallas_call(
        functools.partial(use_kernel, layout, first),
        grid_spec=pltpu.PrefetchScalarGridSpec(
            num_scalar_prefetch=1,
            grid=(1,),
            in_specs=specs,
            out_specs=[pl.BlockSpec(o.shape, lambda i, idx, n=len(o.shape): (0,) * n) for o in outs],
        ),
        out_shape=outs,
        input_output_aliases=aliases,
        compiler_params=pltpu.CompilerParams(vmem_limit_bytes=VMEM_LIMIT),
        cost_estimate=pl.CostEstimate(
            flops=8 * blocks * rows * chip * width, bytes_accessed=blocks * 5000000, transcendentals=0
        ),
    )(index, *ins)


def place_kernel(counts, index, *refs):
    n = sum(counts)
    k = len(counts)
    mine, theirs, out = refs[:k], refs[k:-1], refs[-1]
    where = [(a, j) for a in range(k) for j in range(counts[a])]
    spots = []
    for ref in theirs:
        spots += [(ref, j) for j in range(ref.shape[0])]
    for i in range(n):
        a, j = where[i]
        ref, r = spots[i]
        out[index[i]] = (mine[a][j].astype(F32) + ref[r].astype(F32)).astype(BF)


def place(index, mine, theirs):
    counts = tuple(a.shape[0] for a in mine)
    n = sum(counts)
    shape = (n,) + mine[0].shape[1:]
    return pl.pallas_call(
        functools.partial(place_kernel, counts),
        grid_spec=pltpu.PrefetchScalarGridSpec(
            num_scalar_prefetch=1,
            grid=(1,),
            in_specs=[pl.BlockSpec(a.shape, lambda i, idx: (0, 0, 0)) for a in (*mine, *theirs)],
            out_specs=pl.BlockSpec(shape, lambda i, idx: (0, 0, 0)),
        ),
        out_shape=jax.ShapeDtypeStruct(shape, BF),
        compiler_params=pltpu.CompilerParams(vmem_limit_bytes=VMEM_LIMIT),
        cost_estimate=pl.CostEstimate(flops=1000000, bytes_accessed=5000000, transcendentals=0),
    )(index, *mine, *theirs)


def make_local(ny):
    half_y = ny // 2
    swap = [(0, 1), (1, 0)]

    def flat4(y, x, c, d):
        return ((y * 2 + x) * 2 + c) * 2 + d

    def token_moves(cross):
        pairs = []
        for y in range(ny):
            for x in range(2):
                for c in range(2):
                    for d in range(2):
                        to_y = (y % half_y) * 2 + x
                        to_x = 1 - c if cross else c
                        pairs.append((flat4(y, x, c, d), flat4(to_y, to_x, d, y // half_y)))
        return pairs

    def flat2(c, d):
        return c * 2 + d

    scaled_a = [(flat2(c, k), flat2(k, c)) for c in range(2) for k in range(2)]
    scaled_b = [(flat2(c, k), flat2(k, 1 - c)) for c in range(2) for k in range(2)]
    sums_a = [(flat2(1 - g, g), flat2(1 - g, 1 - g)) for g in range(2)] + [
        (flat2(g, g), flat2(1 - g, g)) for g in range(2)
    ]
    sums_b = [(flat2(1 - g, g), flat2(g, 1 - g)) for g in range(2)]
    up_ring = [(y, (y + 1) % ny) for y in range(ny)]
    down_ring = [(y, (y - 1) % ny) for y in range(ny)]

    def local(cotangent, expert_ids, combine, gate_saved, up_saved, w_down):
        expert_count = lax.axis_size("expert")
        y = lax.axis_index("y")
        core = lax.axis_index("core")
        xlo = lax.axis_index("xlo")
        dp = lax.axis_index("dp")
        rows = gate_saved.shape[2]
        width = gate_saved.shape[3]
        capacity = rows // expert_count
        half = capacity // 2
        lanes = cotangent.shape[2]
        chip = 2 * lanes
        every = ("y", "xlo", "core", "dp")

        ids = expert_ids[0].astype(BF)
        moved = lax.ppermute(jnp.concatenate([cotangent[0], ids], axis=1), every, token_moves(False))
        across = lax.ppermute(cotangent[0], every, token_moves(True))
        mine = moved[:, :lanes]
        tokens = jnp.concatenate([jnp.where(xlo == 0, mine, across), jnp.where(xlo == 0, across, mine)], axis=1)
        table = one_hot_table(moved[:, lanes:].astype(jnp.int32), expert_count, capacity, xlo)
        outgoing = jnp.dot(table, tokens, preferred_element_type=F32).astype(BF)
        outgoing = outgoing.reshape(expert_count, half, chip)
        part = lax.all_to_all(outgoing, "expert", split_axis=0, concat_axis=0, tiled=True)

        gate = gate_saved[0, 0].astype(F32)
        upper = up_saved[0, 0].astype(F32)
        weight_rows = combine[0, 0][:, None]
        sigma = jax.nn.sigmoid(gate)
        active = gate * sigma
        scaled = (weight_rows * (active * upper)).astype(BF)
        s_a = lax.ppermute(scaled, ("core", "dp"), scaled_a)
        s_b = lax.ppermute(scaled, ("core", "dp"), scaled_b)
        w_moved = lax.ppermute(w_down[0], "core", swap)

        from_x = lax.ppermute(part, "xlo", swap)
        from_x, s_a, s_b, w_moved = lax.optimization_barrier((from_x, s_a, s_b, w_moved))
        s_mine = jnp.where(dp == core, s_a, s_b)
        s_theirs = jnp.where(dp == core, s_b, s_a)
        w_mine = w_down[0].reshape(ny, chip, width)
        w_theirs = w_moved.reshape(ny, chip, width)
        block = jnp.stack([jnp.where(xlo == 0, part, from_x), jnp.where(xlo == 0, from_x, part)], axis=1)
        block = block.reshape(rows, chip)

        spot = lambda *offsets: jnp.stack([(y + o + ny) % ny for o in offsets]).astype(jnp.int32)
        full = (0, 0, rows)
        mid = rows // 2
        share_args = (w_mine, w_theirs, s_mine, s_theirs)
        g_mine, g_theirs, order = [], [], [0]
        up = down = block
        pending = (((full,),), [block], spot(0))
        acc = None

        def run(pending, acc):
            acc, gm, gt = use(*pending, *share_args, acc)
            g_mine.append(gm)
            g_theirs.append(gt)
            return acc

        for step in range(1, half_y + 1):
            if acc is not None:
                if step < half_y:
                    up, acc = lax.optimization_barrier((up, acc))
                    down, acc = lax.optimization_barrier((down, acc))
                else:
                    up, acc = lax.optimization_barrier((up, acc))
                    down, acc, sent = lax.optimization_barrier((down, acc, tuple(g_theirs)))
            if step < half_y:
                up_next = lax.ppermute(up, "y", up_ring)
                down_next = lax.ppermute(down, "y", down_ring)
                coming = (((full,), (full,)), [up_next, down_next], spot(-step, step))
                order += [-step, step]
            else:
                up_next = lax.ppermute(up[:mid], "y", up_ring)
                down_next = lax.ppermute(down[mid:], "y", down_ring)
                coming = ((((0, 0, mid), (0, mid, mid)),), [up_next, down_next], spot(half_y))
                order.append(half_y)
                early = lax.ppermute(jnp.concatenate(sent, axis=0), "core", swap)
            acc = run(pending, acc)
            up, down, pending = up_next, down_next, coming
        acc, early = lax.optimization_barrier((acc, early))
        acc = run(pending, acc)

        sum_mine, sum_theirs = acc[:, :width].astype(BF), acc[:, width:].astype(BF)
        held_own = dp == core
        got_a = lax.ppermute(jnp.where(held_own, sum_theirs, sum_mine), ("core", "dp"), sums_a)
        got_b = lax.ppermute(sum_theirs, ("core", "dp"), sums_b)

        late = lax.ppermute(jnp.concatenate(g_theirs[3:], axis=0), "core", swap)
        grad_weight = place(spot(*order), g_mine, [early, late]).reshape(ny * chip, width)

        mix = jnp.sum(
            s_mine.astype(F32) * acc[:, :width] + s_theirs.astype(F32) * acc[:, width:], axis=1
        )
        got_a, got_b, _ = lax.optimization_barrier((got_a, got_b, mix))
        members = 2 * ny * 4
        share = rows // (ny * 4)
        mix = jnp.stack([jnp.where(core == 0, mix, 0.0), jnp.where(core == 1, mix, 0.0)])
        mix = lax.all_to_all(mix.reshape(members, share), ("dp", "y", "xlo", "core"), 0, 0, tiled=True)
        mix = jnp.sum(mix, axis=0)
        blk = (y * 2 + xlo) * 2 + core
        mix = mix / lax.dynamic_slice_in_dim(combine[0, 0], blk * share, share, 0)

        grad_hidden = jnp.where(held_own, acc[:, :width], got_b.astype(F32)) + got_a.astype(F32)
        weighted = weight_rows * grad_hidden
        grad_gate = (weighted * upper * sigma * (1.0 + gate * (1.0 - sigma))).astype(BF)
        grad_upper = (weighted * active).astype(BF)
        return grad_gate[None, None], grad_upper[None, None], grad_weight[None], mix[None, None]

    return local


def solution(mesh):
    ne, nb, nd = mesh.devices.shape
    fine = Mesh(mesh.devices.reshape(ne, nb // 4, 2, 2, nd), ("expert", "y", "xlo", "core", "dp"))
    blk = ("y", "xlo", "core")
    return jax.shard_map(
        make_local(nb // 4),
        mesh=fine,
        in_specs=(
            P("dp", "expert", blk),
            P("dp", "expert", None),
            P("dp", "expert", None),
            P("dp", "expert", None, blk),
            P("dp", "expert", None, blk),
            P("expert", "dp", blk),
        ),
        out_specs=(
            P("dp", "expert", None, blk),
            P("dp", "expert", None, blk),
            P("expert", "dp", blk),
            P("dp", "expert", blk),
        ),
        check_vma=False,
    )
```

```python
import functools

import jax
import jax.numpy as jnp
from jax import lax
from jax.experimental import pallas as pl
from jax.experimental.pallas import tpu as pltpu
from jax.sharding import Mesh, PartitionSpec as P

BF = jnp.bfloat16
F32 = jnp.float32
VMEM_LIMIT = 60 * 1024 * 1024


def one_hot_table(ids, expert_count, capacity):
    experts = jnp.arange(expert_count, dtype=jnp.int32)
    chosen = (ids[:, :, None] == experts).astype(F32)
    per_token = jnp.sum(chosen, axis=1)
    count = ids.shape[0]
    before = (jnp.arange(count)[:, None] > jnp.arange(count)[None, :]).astype(BF)
    earlier = jnp.dot(before, per_token.astype(BF), preferred_element_type=F32)
    position = jnp.sum(chosen * earlier[:, None, :], axis=-1).astype(jnp.int32)
    target = ids * capacity + position
    columns = jnp.arange(expert_count * capacity, dtype=jnp.int32)
    hit = (target[:, 0][None, :] == columns[:, None]) | (target[:, 1][None, :] == columns[:, None])
    return hit.astype(BF)


def use_kernel(parts, first, carried, *refs):
    blocks = len(parts)
    it = iter(refs[1:])
    x_refs = [[next(it) for _ in range(n)] for n in parts]
    w_mine = [next(it) for _ in range(blocks)]
    w_theirs = [next(it) for _ in range(blocks)]
    s_mine, s_theirs = next(it), next(it)
    carry = next(it) if carried else None
    acc_in = None if first else next(it)
    acc, g_mine, g_theirs = next(it), next(it), next(it)
    width = s_mine.shape[1]
    s = jnp.concatenate([s_mine[...], s_theirs[...]], axis=1)
    for b in range(blocks):
        x = x_refs[b][0][...]
        for more in x_refs[b][1:]:
            x = x + more[...]
        w = jnp.concatenate([w_mine[b][0], w_theirs[b][0]], axis=1)
        product = jnp.dot(x, w, preferred_element_type=F32)
        if b == 0:
            acc[...] = product if first else product + acc_in[...]
        else:
            acc[...] += product
        outer = lax.dot_general(x, s, (((0,), (0,)), ((), ())), preferred_element_type=F32)
        g_mine[b] = outer[:, :width].astype(BF)
        g_theirs[carried + b] = outer[:, width:].astype(BF)
    if carried:
        g_theirs[:carried] = carry[...]


def use(pieces, index, w_mine, w_theirs, s_mine, s_theirs, acc, carry=None):
    first = acc is None
    parts = tuple(len(p) for p in pieces)
    blocks = len(parts)
    carried = 0 if carry is None else carry.shape[0]
    rows, width = s_mine.shape
    chip = pieces[0][0].shape[1]

    def whole(a):
        return pl.BlockSpec(a.shape, lambda i, idx: (0,) * len(a.shape))

    def pick(j):
        return pl.BlockSpec((1, chip, width), lambda i, idx: (idx[j], 0, 0))

    flat = [a for p in pieces for a in p]
    ins = flat + [w_mine] * blocks + [w_theirs] * blocks + [s_mine, s_theirs]
    specs = [whole(a) for a in flat] + [pick(j) for j in range(blocks)] * 2 + [whole(s_mine), whole(s_theirs)]
    if carried:
        ins.append(carry)
        specs.append(whole(carry))
    aliases = {}
    if not first:
        aliases = {1 + len(ins): 0}
        ins.append(acc)
        specs.append(whole(acc))
    outs = [
        jax.ShapeDtypeStruct((rows, 2 * width), F32),
        jax.ShapeDtypeStruct((blocks, chip, width), BF),
        jax.ShapeDtypeStruct((carried + blocks, chip, width), BF),
    ]
    return pl.pallas_call(
        functools.partial(use_kernel, parts, first, carried),
        grid_spec=pltpu.PrefetchScalarGridSpec(
            num_scalar_prefetch=1,
            grid=(1,),
            in_specs=specs,
            out_specs=[whole(o) for o in outs],
        ),
        out_shape=outs,
        input_output_aliases=aliases,
        compiler_params=pltpu.CompilerParams(vmem_limit_bytes=VMEM_LIMIT),
        cost_estimate=pl.CostEstimate(
            flops=8 * blocks * rows * chip * width, bytes_accessed=blocks * 4000000, transcendentals=0
        ),
    )(index, *ins)


def place_kernel(counts, index, *refs):
    n = sum(counts)
    k = len(counts)
    mine, theirs, out = refs[:k], refs[k:-1], refs[-1]
    where = [(a, j) for a in range(k) for j in range(counts[a])]
    spots = []
    for ref in theirs:
        spots += [(ref, j) for j in range(ref.shape[0])]
    for i in range(n):
        a, j = where[i]
        ref, r = spots[i]
        out[index[i]] = (mine[a][j].astype(F32) + ref[r].astype(F32)).astype(BF)


def place(index, mine, theirs):
    counts = tuple(a.shape[0] for a in mine)
    n = sum(counts)
    shape = (n,) + mine[0].shape[1:]
    return pl.pallas_call(
        functools.partial(place_kernel, counts),
        grid_spec=pltpu.PrefetchScalarGridSpec(
            num_scalar_prefetch=1,
            grid=(1,),
            in_specs=[pl.BlockSpec(a.shape, lambda i, idx: (0, 0, 0)) for a in (*mine, *theirs)],
            out_specs=pl.BlockSpec(shape, lambda i, idx: (0, 0, 0)),
        ),
        out_shape=jax.ShapeDtypeStruct(shape, BF),
        compiler_params=pltpu.CompilerParams(vmem_limit_bytes=VMEM_LIMIT),
        cost_estimate=pl.CostEstimate(flops=1000000, bytes_accessed=5000000, transcendentals=0),
    )(index, *mine, *theirs)


def make_local(ny):
    half_y = ny // 2
    swap = [(0, 1), (1, 0)]

    def flat4(y, x, c, d):
        return ((y * 2 + x) * 2 + c) * 2 + d

    def token_moves(cross):
        pairs = []
        for y in range(ny):
            for x in range(2):
                for c in range(2):
                    for d in range(2):
                        to_y = (y % half_y) * 2 + x
                        to_x = 1 - c if cross else c
                        pairs.append((flat4(y, x, c, d), flat4(to_y, to_x, d, y // half_y)))
        return pairs

    def flat2(c, d):
        return c * 2 + d

    scaled_a = [(flat2(c, k), flat2(k, c)) for c in range(2) for k in range(2)]
    scaled_b = [(flat2(c, k), flat2(k, 1 - c)) for c in range(2) for k in range(2)]
    sums_a = [(flat2(1 - g, g), flat2(1 - g, 1 - g)) for g in range(2)] + [
        (flat2(g, g), flat2(1 - g, g)) for g in range(2)
    ]
    sums_b = [(flat2(1 - g, g), flat2(g, 1 - g)) for g in range(2)]
    up_ring = [(y, (y + 1) % ny) for y in range(ny)]
    down_ring = [(y, (y - 1) % ny) for y in range(ny)]

    def local(cotangent, expert_ids, combine, gate_saved, up_saved, w_down):
        expert_count = lax.axis_size("expert")
        y = lax.axis_index("y")
        core = lax.axis_index("core")
        xlo = lax.axis_index("xlo")
        dp = lax.axis_index("dp")
        rows = gate_saved.shape[2]
        width = gate_saved.shape[3]
        capacity = rows // expert_count
        lanes = cotangent.shape[2]
        chip = 2 * lanes
        every = ("y", "xlo", "core", "dp")

        ids = expert_ids[0].astype(BF)
        moved = lax.ppermute(jnp.concatenate([cotangent[0], ids], axis=1), every, token_moves(False))
        across = lax.ppermute(cotangent[0], every, token_moves(True))
        mine = moved[:, :lanes]
        tokens = jnp.concatenate([jnp.where(xlo == 0, mine, across), jnp.where(xlo == 0, across, mine)], axis=1)
        table = one_hot_table(moved[:, lanes:].astype(jnp.int32), expert_count, capacity)
        outgoing = jnp.dot(table, tokens, preferred_element_type=F32).astype(BF)
        outgoing = outgoing.reshape(expert_count, capacity, chip)
        part = lax.all_to_all(outgoing, "expert", split_axis=0, concat_axis=0, tiled=True)

        gate = gate_saved[0, 0].astype(F32)
        upper = up_saved[0, 0].astype(F32)
        weight_rows = combine[0, 0][:, None]
        sigma = jax.nn.sigmoid(gate)
        active = gate * sigma
        scaled = (weight_rows * (active * upper)).astype(BF)
        w_sent, scaled = lax.optimization_barrier((w_down[0], scaled))
        s_a = lax.ppermute(scaled, ("core", "dp"), scaled_a)
        s_b = lax.ppermute(scaled, ("core", "dp"), scaled_b)
        w_moved = lax.ppermute(w_sent, "core", swap)

        spot = lambda *offsets: jnp.stack([(y + o + ny) % ny for o in offsets]).astype(jnp.int32)
        block = part.reshape(rows, chip)
        up = lax.ppermute(block, "y", up_ring)
        down = lax.ppermute(block, "y", down_ring)
        waiting, offsets, order = [[block], [up], [down]], (0, -1, 1), [0, -1, 1]
        acc, share_args, theirs = None, None, None
        g_mine, g_moved = [], []
        for step in range(2, half_y + 1):
            if acc is None:
                up, s_a, s_b, w_moved = lax.optimization_barrier((up, s_a, s_b, w_moved))
                share_args = (
                    w_down[0].reshape(ny, chip, width),
                    w_moved.reshape(ny, chip, width),
                    jnp.where(dp == core, s_a, s_b),
                    jnp.where(dp == core, s_b, s_a),
                )
            else:
                up, acc = lax.optimization_barrier((up, acc))
                down, acc, theirs = lax.optimization_barrier((down, acc, theirs))
                g_moved.append(lax.ppermute(theirs, "core", swap))
            if step < half_y:
                up = lax.ppermute(up, "y", up_ring)
                down = lax.ppermute(down, "y", down_ring)
                arriving = [[up], [down]]
            else:
                up = lax.ppermute(up, ("y", "core"), [(2 * a, 2 * b) for a, b in up_ring])
                down = lax.ppermute(down, ("y", "core"), [(2 * a + 1, 2 * b + 1) for a, b in down_ring])
                arriving = [[up, down]]
            acc, gm, theirs = use(waiting, spot(*offsets), *share_args, acc)
            g_mine.append(gm)
            waiting = arriving
            offsets = (-step, step) if step < half_y else (half_y,)
            order += list(offsets)
        acc, *g_moved = lax.optimization_barrier((acc, *g_moved))
        acc, gm, theirs = use(waiting, spot(*offsets), *share_args, acc, theirs)
        g_mine.append(gm)
        share_s = share_args[2:]

        sum_mine, sum_theirs = acc[:, :width].astype(BF), acc[:, width:].astype(BF)
        held_own = dp == core
        got_a = lax.ppermute(jnp.where(held_own, sum_theirs, sum_mine), ("core", "dp"), sums_a)
        got_b = lax.ppermute(sum_theirs, ("core", "dp"), sums_b)

        mix = jnp.sum(
            share_s[0].astype(F32) * acc[:, :width] + share_s[1].astype(F32) * acc[:, width:], axis=1
        )
        late = lax.ppermute(theirs, "core", swap)
        grad_weight = place(spot(*order), g_mine, [*g_moved, late]).reshape(ny * chip, width)
        got_a, got_b, _ = lax.optimization_barrier((got_a, got_b, mix))
        members = 2 * ny * 4
        share = rows // (ny * 4)
        mix = jnp.stack([jnp.where(core == 0, mix, 0.0), jnp.where(core == 1, mix, 0.0)])
        mix = lax.all_to_all(mix.reshape(members, share), ("dp", "y", "xlo", "core"), 0, 0, tiled=True)
        grad_hidden = jnp.where(held_own, acc[:, :width], got_b.astype(F32)) + got_a.astype(F32)
        weighted = weight_rows * grad_hidden
        grad_gate = (weighted * upper * sigma * (1.0 + gate * (1.0 - sigma))).astype(BF)
        grad_upper = (weighted * active).astype(BF)
        mix, grad_gate, grad_upper, grad_weight = lax.optimization_barrier((mix, grad_gate, grad_upper, grad_weight))
        mix = jnp.sum(mix, axis=0)
        blk = (y * 2 + xlo) * 2 + core
        mix = mix / lax.dynamic_slice_in_dim(combine[0, 0], blk * share, share, 0)
        return grad_gate[None, None], grad_upper[None, None], grad_weight[None], mix[None, None]

    return local


def solution(mesh):
    ne, nb, nd = mesh.devices.shape
    fine = Mesh(mesh.devices.reshape(ne, nb // 4, 2, 2, nd), ("expert", "y", "xlo", "core", "dp"))
    blk = ("y", "xlo", "core")
    return jax.shard_map(
        make_local(nb // 4),
        mesh=fine,
        in_specs=(
            P("dp", "expert", blk),
            P("dp", "expert", None),
            P("dp", "expert", None),
            P("dp", "expert", None, blk),
            P("dp", "expert", None, blk),
            P("expert", "dp", blk),
        ),
        out_specs=(
            P("dp", "expert", None, blk),
            P("dp", "expert", None, blk),
            P("expert", "dp", blk),
            P("dp", "expert", blk),
        ),
        check_vma=False,
    )
```

```python
import functools

import jax
import jax.numpy as jnp
from jax import lax
from jax.experimental import pallas as pl
from jax.experimental.pallas import tpu as pltpu
from jax.sharding import Mesh, PartitionSpec as P

BF = jnp.bfloat16
F32 = jnp.float32
VMEM_LIMIT = 60 * 1024 * 1024


def one_hot_table(ids, expert_count, capacity):
    experts = jnp.arange(expert_count, dtype=jnp.int32)
    chosen = (ids[:, :, None] == experts).astype(F32)
    per_token = jnp.sum(chosen, axis=1)
    count = ids.shape[0]
    before = (jnp.arange(count)[:, None] > jnp.arange(count)[None, :]).astype(BF)
    earlier = jnp.dot(before, per_token.astype(BF), preferred_element_type=F32)
    position = jnp.sum(chosen * earlier[:, None, :], axis=-1).astype(jnp.int32)
    target = ids * capacity + position
    columns = jnp.arange(expert_count * capacity, dtype=jnp.int32)
    hit = (target[:, 0][None, :] == columns[:, None]) | (target[:, 1][None, :] == columns[:, None])
    return hit.astype(BF)


def use_kernel(blocks, first, last, carried, index, *refs):
    it = iter(refs)
    x_refs = [next(it) for _ in range(blocks)]
    w_mine = [next(it) for _ in range(blocks)]
    w_theirs = [next(it) for _ in range(blocks)]
    s_a, s_b = next(it), next(it)
    carry = next(it) if carried else None
    acc_in = None if first else next(it)
    acc, g_mine, g_theirs = next(it), next(it), next(it)
    width = s_a.shape[1]
    flags = index.shape[0] - 2
    own = index[flags] == 1
    s_mine = jnp.where(own, s_a[...], s_b[...])
    s_theirs = jnp.where(own, s_b[...], s_a[...])
    s = jnp.concatenate([s_mine, s_theirs], axis=1)
    for b in range(blocks):
        x = x_refs[b][...]
        w = jnp.concatenate([w_mine[b][0], w_theirs[b][0]], axis=1)
        product = jnp.dot(x, w, preferred_element_type=F32)
        if last:
            total = product + acc_in[...]
        elif b == 0:
            acc[...] = product if first else product + acc_in[...]
        else:
            acc[...] += product
        outer = lax.dot_general(x, s, (((0,), (0,)), ((), ())), preferred_element_type=F32)
        g_mine[b] = outer[:, :width].astype(BF)
        g_theirs[carried + b] = outer[:, width:].astype(BF)
    if last:
        sum_a, sum_b, mix = next(it), next(it), next(it)
        mine, theirs = total[:, :width], total[:, width:]
        acc[...] = mine
        sum_b[...] = theirs.astype(BF)
        sum_a[...] = jnp.where(own, theirs, mine).astype(BF)
        terms = s_mine.astype(F32) * mine + s_theirs.astype(F32) * theirs
        line = lax.dot_general(
            jnp.ones((8, width), F32),
            terms,
            (((1,), (1,)), ((), ())),
            precision=lax.Precision.HIGHEST,
            preferred_element_type=F32,
        )
        row = lax.broadcasted_iota(jnp.int32, (2, line.shape[1]), 0)
        mix[...] = jnp.where(row == index[flags + 1], line[:2], 0.0)
    if carried:
        g_theirs[:carried] = carry[...]


def use(pieces, index, start, w_mine, w_theirs, s_a, s_b, acc, last=False, carry=None):
    first = acc is None
    blocks = len(pieces)
    carried = 0 if carry is None else carry.shape[0]
    rows, width = s_a.shape
    chip = pieces[0].shape[1]

    def whole(a):
        return pl.BlockSpec(a.shape, lambda i, idx: (0,) * len(a.shape))

    def pick(j):
        return pl.BlockSpec((1, chip, width), lambda i, idx: (idx[start + j], 0, 0))

    ins = list(pieces) + [w_mine] * blocks + [w_theirs] * blocks + [s_a, s_b]
    specs = [whole(a) for a in pieces] + [pick(j) for j in range(blocks)] * 2 + [whole(s_a), whole(s_b)]
    if carried:
        ins.append(carry)
        specs.append(whole(carry))
    aliases = {}
    if not first:
        if not last:
            aliases = {1 + len(ins): 0}
        ins.append(acc)
        specs.append(whole(acc))
    outs = [
        jax.ShapeDtypeStruct((rows, width if last else 2 * width), F32),
        jax.ShapeDtypeStruct((blocks, chip, width), BF),
        jax.ShapeDtypeStruct((carried + blocks, chip, width), BF),
    ]
    if last:
        outs += [jax.ShapeDtypeStruct((rows, width), BF)] * 2 + [jax.ShapeDtypeStruct((2, rows), F32)]
    return pl.pallas_call(
        functools.partial(use_kernel, blocks, first, last, carried),
        grid_spec=pltpu.PrefetchScalarGridSpec(
            num_scalar_prefetch=1,
            grid=(1,),
            in_specs=specs,
            out_specs=[whole(o) for o in outs],
        ),
        out_shape=outs,
        input_output_aliases=aliases,
        compiler_params=pltpu.CompilerParams(vmem_limit_bytes=VMEM_LIMIT),
        cost_estimate=pl.CostEstimate(
            flops=8 * blocks * rows * chip * width, bytes_accessed=blocks * 4000000, transcendentals=0
        ),
    )(index, *ins)


def place_kernel(counts, index, *refs):
    n = sum(counts)
    k = len(counts)
    mine, theirs, out = refs[:k], refs[k:-1], refs[-1]
    where = [(a, j) for a in range(k) for j in range(counts[a])]
    spots = []
    for ref in theirs:
        spots += [(ref, j) for j in range(ref.shape[0])]
    for i in range(n):
        a, j = where[i]
        partner = i if i in (0, n - 1) else i + 1 - 2 * ((i - 1) % 2)
        ref, r = spots[partner]
        out[index[i]] = (mine[a][j].astype(F32) + ref[r].astype(F32)).astype(BF)


def place(index, mine, theirs):
    counts = tuple(a.shape[0] for a in mine)
    n = sum(counts)
    shape = (n,) + mine[0].shape[1:]
    return pl.pallas_call(
        functools.partial(place_kernel, counts),
        grid_spec=pltpu.PrefetchScalarGridSpec(
            num_scalar_prefetch=1,
            grid=(1,),
            in_specs=[pl.BlockSpec(a.shape, lambda i, idx: (0, 0, 0)) for a in (*mine, *theirs)],
            out_specs=pl.BlockSpec(shape, lambda i, idx: (0, 0, 0)),
        ),
        out_shape=jax.ShapeDtypeStruct(shape, BF),
        compiler_params=pltpu.CompilerParams(vmem_limit_bytes=VMEM_LIMIT),
        cost_estimate=pl.CostEstimate(flops=1000000, bytes_accessed=5000000, transcendentals=0),
    )(index, *mine, *theirs)


def make_local(ny):
    half_y = ny // 2
    swap = [(0, 1), (1, 0)]

    def flat4(y, x, c, d):
        return ((y * 2 + x) * 2 + c) * 2 + d

    def token_moves(cross):
        pairs = []
        for y in range(ny):
            for x in range(2):
                for c in range(2):
                    for d in range(2):
                        to_y = (y % half_y) * 2 + x
                        to_x = 1 - c if cross else c
                        pairs.append((flat4(y, x, c, d), flat4(to_y, to_x, d, y // half_y)))
        return pairs

    def flat2(c, d):
        return c * 2 + d

    scaled_a = [(flat2(c, k), flat2(k, c)) for c in range(2) for k in range(2)]
    scaled_b = [(flat2(c, k), flat2(k, 1 - c)) for c in range(2) for k in range(2)]
    sums_a = [(flat2(1 - g, g), flat2(1 - g, 1 - g)) for g in range(2)] + [
        (flat2(g, g), flat2(1 - g, g)) for g in range(2)
    ]
    sums_b = [(flat2(1 - g, g), flat2(g, 1 - g)) for g in range(2)]
    ring_a = [(y * 2 + c, ((y + 1 - 2 * c) % ny) * 2 + c) for y in range(ny) for c in range(2)]
    ring_b = [(y * 2 + c, ((y - 1 + 2 * c) % ny) * 2 + c) for y in range(ny) for c in range(2)]

    def local(cotangent, expert_ids, combine, gate_saved, up_saved, w_down):
        expert_count = lax.axis_size("expert")
        y = lax.axis_index("y")
        core = lax.axis_index("core")
        xlo = lax.axis_index("xlo")
        dp = lax.axis_index("dp")
        rows = gate_saved.shape[2]
        width = gate_saved.shape[3]
        capacity = rows // expert_count
        lanes = cotangent.shape[2]
        chip = 2 * lanes
        every = ("y", "xlo", "core", "dp")

        ids = expert_ids[0].astype(BF)
        moved = lax.ppermute(jnp.concatenate([cotangent[0], ids], axis=1), every, token_moves(False))
        across = lax.ppermute(cotangent[0], every, token_moves(True))
        mine = moved[:, :lanes]
        tokens = jnp.concatenate([jnp.where(xlo == 0, mine, across), jnp.where(xlo == 0, across, mine)], axis=1)
        table = one_hot_table(moved[:, lanes:].astype(jnp.int32), expert_count, capacity)
        outgoing = jnp.dot(table, tokens, preferred_element_type=F32).astype(BF)
        outgoing = outgoing.reshape(expert_count, capacity, chip)
        part = lax.all_to_all(outgoing, "expert", split_axis=0, concat_axis=0, tiled=True)

        gate = gate_saved[0, 0].astype(F32)
        upper = up_saved[0, 0].astype(F32)
        weight_rows = combine[0, 0][:, None]
        sigma = jax.nn.sigmoid(gate)
        active = gate * sigma
        scaled = (weight_rows * (active * upper)).astype(BF)
        w_sent, scaled = lax.optimization_barrier((w_down[0], scaled))
        s_a = lax.ppermute(scaled, ("core", "dp"), scaled_a)
        s_b = lax.ppermute(scaled, ("core", "dp"), scaled_b)
        w_moved = lax.ppermute(w_sent, "core", swap)

        held_own = dp == core
        turn = jnp.where(core == 0, -1, 1)
        order = [0] + [sign * step for step in range(1, half_y) for sign in (1, -1)] + [half_y]
        index = jnp.stack(
            [(y + turn * o + ny) % ny for o in order] + [held_own.astype(jnp.int32), core]
        ).astype(jnp.int32)
        on_a = lambda v: lax.ppermute(v, ("y", "core"), ring_a)
        on_b = lambda v: lax.ppermute(v, ("y", "core"), ring_b)
        block = part.reshape(rows, chip)
        a = on_a(block)
        block_b, s_a, s_b, w_moved = lax.optimization_barrier((block, s_a, s_b, w_moved))
        b = on_b(block_b)
        args = (w_down[0].reshape(ny, chip, width), w_moved.reshape(ny, chip, width), s_a, s_b)
        waiting, start, acc, theirs = [block_b, a, b], 0, None, None
        g_mine, g_moved = [], []
        for step in range(2, half_y + 1):
            if acc is not None:
                a, acc = lax.optimization_barrier((a, acc))
                b, acc, theirs = lax.optimization_barrier((b, acc, theirs))
                g_moved.append(lax.ppermute(theirs, "core", swap))
            a = on_a(a)
            arriving = [a]
            if step < half_y:
                b = on_b(b)
                arriving.append(b)
            acc, gm, theirs = use(waiting, index, start, *args, acc)
            g_mine.append(gm)
            start += len(waiting)
            waiting = arriving
        acc, *g_moved = lax.optimization_barrier((acc, *g_moved))
        acc, gm, theirs, sum_a, sum_b, mix = use(waiting, index, start, *args, acc, last=True, carry=theirs)
        g_mine.append(gm)

        got_a = lax.ppermute(sum_a, ("core", "dp"), sums_a)
        got_b = lax.ppermute(sum_b, ("core", "dp"), sums_b)
        members = 2 * ny * 4
        share = rows // (ny * 4)
        mix = lax.all_to_all(mix.reshape(members, share), ("dp", "y", "xlo", "core"), 0, 0, tiled=True)
        late = lax.ppermute(theirs, "core", swap)
        grad_weight = place(index, g_mine, [*g_moved, late]).reshape(ny * chip, width)
        grad_hidden = jnp.where(held_own, acc, got_b.astype(F32)) + got_a.astype(F32)
        weighted = weight_rows * grad_hidden
        grad_gate = (weighted * upper * sigma * (1.0 + gate * (1.0 - sigma))).astype(BF)
        grad_upper = (weighted * active).astype(BF)
        mix, grad_gate, grad_upper, grad_weight = lax.optimization_barrier((mix, grad_gate, grad_upper, grad_weight))
        mix = jnp.sum(mix, axis=0)
        blk = (y * 2 + xlo) * 2 + core
        mix = mix / lax.dynamic_slice_in_dim(combine[0, 0], blk * share, share, 0)
        return grad_gate[None, None], grad_upper[None, None], grad_weight[None], mix[None, None]

    return local


def solution(mesh):
    ne, nb, nd = mesh.devices.shape
    fine = Mesh(mesh.devices.reshape(ne, nb // 4, 2, 2, nd), ("expert", "y", "xlo", "core", "dp"))
    blk = ("y", "xlo", "core")
    return jax.shard_map(
        make_local(nb // 4),
        mesh=fine,
        in_specs=(
            P("dp", "expert", blk),
            P("dp", "expert", None),
            P("dp", "expert", None),
            P("dp", "expert", None, blk),
            P("dp", "expert", None, blk),
            P("expert", "dp", blk),
        ),
        out_specs=(
            P("dp", "expert", None, blk),
            P("dp", "expert", None, blk),
            P("expert", "dp", blk),
            P("dp", "expert", blk),
        ),
        check_vma=False,
    )
```

```python
import functools

import jax
import jax.numpy as jnp
from jax import lax
from jax.experimental import pallas as pl
from jax.experimental.pallas import tpu as pltpu
from jax.sharding import Mesh, PartitionSpec as P

BF = jnp.bfloat16
F32 = jnp.float32
VMEM_LIMIT = 60 * 1024 * 1024


def one_hot_table(ids, expert_count, capacity):
    experts = jnp.arange(expert_count, dtype=jnp.int32)
    chosen = (ids[:, :, None] == experts).astype(F32)
    per_token = jnp.sum(chosen, axis=1)
    count = ids.shape[0]
    before = (jnp.arange(count)[:, None] > jnp.arange(count)[None, :]).astype(BF)
    earlier = jnp.dot(before, per_token.astype(BF), preferred_element_type=F32)
    position = jnp.sum(chosen * earlier[:, None, :], axis=-1).astype(jnp.int32)
    target = ids * capacity + position
    columns = jnp.arange(expert_count * capacity, dtype=jnp.int32)
    hit = (target[:, 0][None, :] == columns[:, None]) | (target[:, 1][None, :] == columns[:, None])
    return hit.astype(BF)


def use_kernel(blocks, first, last, carried, index, *refs):
    it = iter(refs)
    x_refs = [next(it) for _ in range(blocks)]
    w_mine = [next(it) for _ in range(blocks)]
    w_theirs = [next(it) for _ in range(blocks)]
    s_a, s_b = next(it), next(it)
    carry = next(it) if carried else None
    acc_in = None if first else next(it)
    acc, g_mine, g_theirs = next(it), next(it), next(it)
    width = s_a.shape[1]
    flags = index.shape[0] - 2
    own = index[flags] == 1
    s_mine = jnp.where(own, s_a[...], s_b[...])
    s_theirs = jnp.where(own, s_b[...], s_a[...])
    s = jnp.concatenate([s_mine, s_theirs], axis=1)
    for b in range(blocks):
        x = x_refs[b][...]
        w = jnp.concatenate([w_mine[b][0], w_theirs[b][0]], axis=1)
        product = jnp.dot(x, w, preferred_element_type=F32)
        if last:
            total = product + acc_in[...]
        elif b == 0:
            acc[...] = product if first else product + acc_in[...]
        else:
            acc[...] += product
        outer = lax.dot_general(x, s, (((0,), (0,)), ((), ())), preferred_element_type=F32)
        g_mine[b] = outer[:, :width].astype(BF)
        g_theirs[carried + b] = outer[:, width:].astype(BF)
    if last:
        sum_a, sum_b, mix = next(it), next(it), next(it)
        mine, theirs = total[:, :width], total[:, width:]
        acc[...] = mine
        sum_b[...] = theirs.astype(BF)
        sum_a[...] = jnp.where(own, theirs, mine).astype(BF)
        terms = s_mine.astype(F32) * mine + s_theirs.astype(F32) * theirs
        line = lax.dot_general(
            jnp.ones((8, width), F32),
            terms,
            (((1,), (1,)), ((), ())),
            precision=lax.Precision.HIGHEST,
            preferred_element_type=F32,
        )
        row = lax.broadcasted_iota(jnp.int32, (2, line.shape[1]), 0)
        mix[...] = jnp.where(row == index[flags + 1], line[:2], 0.0)
    if carried:
        g_theirs[:carried] = carry[...]


def use(pieces, index, start, w_mine, w_theirs, s_a, s_b, acc, last=False, carry=None):
    first = acc is None
    blocks = len(pieces)
    carried = 0 if carry is None else carry.shape[0]
    rows, width = s_a.shape
    chip = pieces[0].shape[1]

    def whole(a):
        return pl.BlockSpec(a.shape, lambda i, idx: (0,) * len(a.shape))

    def pick(j):
        return pl.BlockSpec((1, chip, width), lambda i, idx: (idx[start + j], 0, 0))

    ins = list(pieces) + [w_mine] * blocks + [w_theirs] * blocks + [s_a, s_b]
    specs = [whole(a) for a in pieces] + [pick(j) for j in range(blocks)] * 2 + [whole(s_a), whole(s_b)]
    if carried:
        ins.append(carry)
        specs.append(whole(carry))
    aliases = {}
    if not first:
        if not last:
            aliases = {1 + len(ins): 0}
        ins.append(acc)
        specs.append(whole(acc))
    outs = [
        jax.ShapeDtypeStruct((rows, width if last else 2 * width), F32),
        jax.ShapeDtypeStruct((blocks, chip, width), BF),
        jax.ShapeDtypeStruct((carried + blocks, chip, width), BF),
    ]
    if last:
        outs += [jax.ShapeDtypeStruct((rows, width), BF)] * 2 + [jax.ShapeDtypeStruct((2, rows), F32)]
    return pl.pallas_call(
        functools.partial(use_kernel, blocks, first, last, carried),
        grid_spec=pltpu.PrefetchScalarGridSpec(
            num_scalar_prefetch=1,
            grid=(1,),
            in_specs=specs,
            out_specs=[whole(o) for o in outs],
        ),
        out_shape=outs,
        input_output_aliases=aliases,
        compiler_params=pltpu.CompilerParams(vmem_limit_bytes=VMEM_LIMIT),
        cost_estimate=pl.CostEstimate(
            flops=8 * blocks * rows * chip * width, bytes_accessed=blocks * 4000000, transcendentals=0
        ),
    )(index, *ins)


def place_kernel(counts, index, *refs):
    n = sum(counts)
    k = len(counts)
    mine, theirs, out = refs[:k], refs[k:-1], refs[-1]
    where = [(a, j) for a in range(k) for j in range(counts[a])]
    spots = []
    for ref in theirs:
        spots += [(ref, j) for j in range(ref.shape[0])]
    for i in range(n):
        a, j = where[i]
        partner = i if i in (0, n - 1) else i + 1 - 2 * ((i - 1) % 2)
        ref, r = spots[partner]
        out[index[i]] = (mine[a][j].astype(F32) + ref[r].astype(F32)).astype(BF)


def place(index, mine, theirs):
    counts = tuple(a.shape[0] for a in mine)
    n = sum(counts)
    shape = (n,) + mine[0].shape[1:]
    return pl.pallas_call(
        functools.partial(place_kernel, counts),
        grid_spec=pltpu.PrefetchScalarGridSpec(
            num_scalar_prefetch=1,
            grid=(1,),
            in_specs=[pl.BlockSpec(a.shape, lambda i, idx: (0, 0, 0)) for a in (*mine, *theirs)],
            out_specs=pl.BlockSpec(shape, lambda i, idx: (0, 0, 0)),
        ),
        out_shape=jax.ShapeDtypeStruct(shape, BF),
        compiler_params=pltpu.CompilerParams(vmem_limit_bytes=VMEM_LIMIT),
        cost_estimate=pl.CostEstimate(flops=1000000, bytes_accessed=5000000, transcendentals=0),
    )(index, *mine, *theirs)


def make_local(ny):
    half_y = ny // 2
    swap = [(0, 1), (1, 0)]

    def flat4(y, x, c, d):
        return ((y * 2 + x) * 2 + c) * 2 + d

    def shift(h):
        return (4 * h - 2) % ny

    def token_moves(cross):
        pairs = []
        for y in range(ny):
            for x in range(2):
                for c in range(2):
                    for d in range(2):
                        to_y = ((y % half_y) * 2 + x + shift(y // half_y)) % ny
                        to_x = 1 - c if cross else c
                        pairs.append((flat4(y, x, c, d), flat4(to_y, to_x, d, y // half_y)))
        return pairs

    def flat2(c, d):
        return c * 2 + d

    scaled_a = [(flat2(c, k), flat2(k, c)) for c in range(2) for k in range(2)]
    scaled_b = [(flat2(c, k), flat2(k, 1 - c)) for c in range(2) for k in range(2)]
    sums_a = [(flat2(1 - g, g), flat2(1 - g, 1 - g)) for g in range(2)] + [
        (flat2(g, g), flat2(1 - g, g)) for g in range(2)
    ]
    sums_b = [(flat2(1 - g, g), flat2(g, 1 - g)) for g in range(2)]
    ring_a = [(y * 2 + c, ((y + 1 - 2 * c) % ny) * 2 + c) for y in range(ny) for c in range(2)]
    ring_b = [(y * 2 + c, ((y - 1 + 2 * c) % ny) * 2 + c) for y in range(ny) for c in range(2)]

    def local(cotangent, expert_ids, combine, gate_saved, up_saved, w_down):
        expert_count = lax.axis_size("expert")
        y = lax.axis_index("y")
        core = lax.axis_index("core")
        xlo = lax.axis_index("xlo")
        dp = lax.axis_index("dp")
        rows = gate_saved.shape[2]
        width = gate_saved.shape[3]
        capacity = rows // expert_count
        lanes = cotangent.shape[2]
        chip = 2 * lanes
        every = ("y", "xlo", "core", "dp")

        ids = expert_ids[0].astype(BF)
        moved = lax.ppermute(jnp.concatenate([cotangent[0], ids], axis=1), every, token_moves(False))
        across = lax.ppermute(cotangent[0], every, token_moves(True))
        mine = moved[:, :lanes]
        tokens = jnp.concatenate([jnp.where(xlo == 0, mine, across), jnp.where(xlo == 0, across, mine)], axis=1)
        table = one_hot_table(moved[:, lanes:].astype(jnp.int32), expert_count, capacity)
        outgoing = jnp.dot(table, tokens, preferred_element_type=F32).astype(BF)
        outgoing = outgoing.reshape(expert_count, capacity, chip)
        part = lax.all_to_all(outgoing, "expert", split_axis=0, concat_axis=0, tiled=True)

        gate = gate_saved[0, 0].astype(F32)
        upper = up_saved[0, 0].astype(F32)
        weight_rows = combine[0, 0][:, None]
        sigma = jax.nn.sigmoid(gate)
        active = gate * sigma
        scaled = (weight_rows * (active * upper)).astype(BF)
        s_a = lax.ppermute(scaled, ("core", "dp"), scaled_a)
        s_b = lax.ppermute(scaled, ("core", "dp"), scaled_b)
        w_moved = lax.ppermute(w_down[0], "core", swap)

        held_own = dp == core
        turn = jnp.where(core == 0, -1, 1)
        shift_here = jnp.where(dp == 0, shift(0), shift(1))
        order = [0] + [sign * step for step in range(1, half_y) for sign in (1, -1)] + [half_y]
        index = jnp.stack(
            [(y + turn * o + 2 * ny - shift_here) % ny for o in order] + [held_own.astype(jnp.int32), core]
        ).astype(jnp.int32)
        on_a = lambda v: lax.ppermute(v, ("y", "core"), ring_a)
        on_b = lambda v: lax.ppermute(v, ("y", "core"), ring_b)
        block = part.reshape(rows, chip)
        a = on_a(block)
        block_b, s_a, s_b = lax.optimization_barrier((block, s_a, s_b))
        b = on_b(block_b)
        args = (w_down[0].reshape(ny, chip, width), w_moved.reshape(ny, chip, width), s_a, s_b)
        waiting, start, acc, theirs = [block_b, a, b], 0, None, None
        g_mine, g_moved = [], []
        for step in range(2, half_y + 1):
            ready = theirs
            if step == half_y:
                a, acc, ready = lax.optimization_barrier((a, acc, ready))
                g_moved.append(lax.ppermute(ready, "core", swap))
            elif acc is not None:
                a, acc = lax.optimization_barrier((a, acc))
            a = on_a(a)
            acc, gm, theirs = use(waiting, index, start, *args, acc)
            g_mine.append(gm)
            start += len(waiting)
            waiting = [a]
            if step < half_y:
                if ready is None:
                    b, acc = lax.optimization_barrier((b, acc))
                else:
                    b, acc, ready = lax.optimization_barrier((b, acc, ready))
                    g_moved.append(lax.ppermute(ready, "core", swap))
                b = on_b(b)
                waiting.append(b)
        acc, *g_moved = lax.optimization_barrier((acc, *g_moved))
        acc, gm, theirs, sum_a, sum_b, mix = use(waiting, index, start, *args, acc, last=True, carry=theirs)
        g_mine.append(gm)

        got_a = lax.ppermute(sum_a, ("core", "dp"), sums_a)
        got_b = lax.ppermute(sum_b, ("core", "dp"), sums_b)
        members = 2 * ny * 4
        share = rows // (ny * 4)
        mix = lax.all_to_all(mix.reshape(members, share), ("dp", "y", "xlo", "core"), 0, 0, tiled=True)
        late = lax.ppermute(theirs, "core", swap)
        grad_weight = place(index, g_mine, [*g_moved, late]).reshape(ny * chip, width)
        grad_hidden = jnp.where(held_own, acc, got_b.astype(F32)) + got_a.astype(F32)
        weighted = weight_rows * grad_hidden
        grad_gate = (weighted * upper * sigma * (1.0 + gate * (1.0 - sigma))).astype(BF)
        grad_upper = (weighted * active).astype(BF)
        mix, grad_gate, grad_upper, grad_weight = lax.optimization_barrier((mix, grad_gate, grad_upper, grad_weight))
        mix = jnp.sum(mix, axis=0)
        blk = (y * 2 + xlo) * 2 + core
        mix = mix / lax.dynamic_slice_in_dim(combine[0, 0], blk * share, share, 0)
        return grad_gate[None, None], grad_upper[None, None], grad_weight[None], mix[None, None]

    return local


def solution(mesh):
    ne, nb, nd = mesh.devices.shape
    fine = Mesh(mesh.devices.reshape(ne, nb // 4, 2, 2, nd), ("expert", "y", "xlo", "core", "dp"))
    blk = ("y", "xlo", "core")
    return jax.shard_map(
        make_local(nb // 4),
        mesh=fine,
        in_specs=(
            P("dp", "expert", blk),
            P("dp", "expert", None),
            P("dp", "expert", None),
            P("dp", "expert", None, blk),
            P("dp", "expert", None, blk),
            P("expert", "dp", blk),
        ),
        out_specs=(
            P("dp", "expert", None, blk),
            P("dp", "expert", None, blk),
            P("expert", "dp", blk),
            P("dp", "expert", blk),
        ),
        check_vma=False,
    )
```

```python
import functools

import jax
import jax.numpy as jnp
from jax import lax
from jax.experimental import pallas as pl
from jax.experimental.pallas import tpu as pltpu
from jax.sharding import Mesh, PartitionSpec as P

BF = jnp.bfloat16
F32 = jnp.float32
VMEM_LIMIT = 60 * 1024 * 1024


def one_hot_table(ids, expert_count, capacity):
    experts = jnp.arange(expert_count, dtype=jnp.int32)
    chosen = (ids[:, :, None] == experts).astype(F32)
    per_token = jnp.sum(chosen, axis=1)
    count = ids.shape[0]
    before = (jnp.arange(count)[:, None] > jnp.arange(count)[None, :]).astype(BF)
    earlier = jnp.dot(before, per_token.astype(BF), preferred_element_type=F32)
    position = jnp.sum(chosen * earlier[:, None, :], axis=-1).astype(jnp.int32)
    target = ids * capacity + position
    columns = jnp.arange(expert_count * capacity, dtype=jnp.int32)
    hit = (target[:, 0][None, :] == columns[:, None]) | (target[:, 1][None, :] == columns[:, None])
    return hit.astype(BF)


def use_kernel(blocks, first, last, index, *refs):
    it = iter(refs)
    x_refs = [next(it) for _ in range(blocks)]
    w_mine = [next(it) for _ in range(blocks)]
    w_theirs = [next(it) for _ in range(blocks)]
    s_a, s_b = next(it), next(it)
    acc_in = None
    if not first:
        acc_in, _, _ = next(it), next(it), next(it)
    acc, g_mine, g_theirs = next(it), next(it), next(it)
    width = s_a.shape[1]
    flags = index.shape[0] - 2
    own = index[flags] == 1
    s_mine = jnp.where(own, s_a[...], s_b[...])
    s_theirs = jnp.where(own, s_b[...], s_a[...])
    s = jnp.concatenate([s_mine, s_theirs], axis=1)
    for b in range(blocks):
        x = x_refs[b][...]
        w = jnp.concatenate([w_mine[b][0], w_theirs[b][0]], axis=1)
        product = jnp.dot(x, w, preferred_element_type=F32)
        if last:
            total = product + acc_in[...]
        elif b == 0:
            acc[...] = product if first else product + acc_in[...]
        else:
            acc[...] += product
        outer = lax.dot_general(x, s, (((0,), (0,)), ((), ())), preferred_element_type=F32)
        g_mine[b] = outer[:, :width].astype(BF)
        g_theirs[b] = outer[:, width:].astype(BF)
    if last:
        sum_a, sum_b, mix = next(it), next(it), next(it)
        mine, theirs = total[:, :width], total[:, width:]
        acc[...] = mine
        sum_b[...] = theirs.astype(BF)
        sum_a[...] = jnp.where(own, theirs, mine).astype(BF)
        terms = s_mine.astype(F32) * mine + s_theirs.astype(F32) * theirs
        line = lax.dot_general(
            jnp.ones((8, width), F32),
            terms,
            (((1,), (1,)), ((), ())),
            precision=lax.Precision.HIGHEST,
            preferred_element_type=F32,
        )
        row = lax.broadcasted_iota(jnp.int32, (2, line.shape[1]), 0)
        mix[...] = jnp.where(row == index[flags + 1], line[:2], 0.0)


def use(pieces, index, start, w_mine, w_theirs, s_a, s_b, held, last=False):
    first = held is None
    blocks = len(pieces)
    rows, width = s_a.shape
    total, chip, _ = w_mine.shape
    assert start % blocks == 0

    def whole(a):
        return pl.BlockSpec(a.shape, lambda i, idx: (0,) * len(a.shape))

    def pick(j):
        return pl.BlockSpec((1, chip, width), lambda i, idx: (idx[start + j], 0, 0))

    ins = list(pieces) + [w_mine] * blocks + [w_theirs] * blocks + [s_a, s_b]
    specs = [whole(a) for a in pieces] + [pick(j) for j in range(blocks)] * 2 + [whole(s_a), whole(s_b)]
    aliases = {}
    if not first:
        n = 1 + len(ins)
        aliases = {n + 1: 1, n + 2: 2} if last else {n: 0, n + 1: 1, n + 2: 2}
        ins += list(held)
        specs += [whole(held[0]), pl.BlockSpec(memory_space=pl.ANY), pl.BlockSpec(memory_space=pl.ANY)]
    slot = pl.BlockSpec((blocks, chip, width), lambda i, idx: (start // blocks, 0, 0))
    outs = [jax.ShapeDtypeStruct((rows, width if last else 2 * width), F32)]
    outs += [jax.ShapeDtypeStruct((total, chip, width), BF)] * 2
    extra = []
    if last:
        extra = [jax.ShapeDtypeStruct((rows, width), BF)] * 2 + [jax.ShapeDtypeStruct((2, rows), F32)]
    return pl.pallas_call(
        functools.partial(use_kernel, blocks, first, last),
        grid_spec=pltpu.PrefetchScalarGridSpec(
            num_scalar_prefetch=1,
            grid=(1,),
            in_specs=specs,
            out_specs=[whole(outs[0]), slot, slot] + [whole(o) for o in extra],
        ),
        out_shape=outs + extra,
        input_output_aliases=aliases,
        compiler_params=pltpu.CompilerParams(vmem_limit_bytes=VMEM_LIMIT),
        cost_estimate=pl.CostEstimate(
            flops=8 * blocks * rows * chip * width, bytes_accessed=blocks * 4000000, transcendentals=0
        ),
    )(index, *ins)


def place_kernel(index, mine, theirs, out):
    out[...] = (mine[...].astype(F32) + theirs[...].astype(F32)).astype(BF)


def place(index, mine, theirs):
    total, chip, width = mine.shape

    def spec(which):
        return pl.BlockSpec((1, chip, width), lambda i, idx: (which(i, idx), 0, 0))

    return pl.pallas_call(
        place_kernel,
        grid_spec=pltpu.PrefetchScalarGridSpec(
            num_scalar_prefetch=1,
            grid=(total,),
            in_specs=[spec(lambda i, idx: i), spec(lambda i, idx: idx[total + i])],
            out_specs=spec(lambda i, idx: idx[i]),
        ),
        out_shape=jax.ShapeDtypeStruct(mine.shape, BF),
        compiler_params=pltpu.CompilerParams(vmem_limit_bytes=VMEM_LIMIT),
        cost_estimate=pl.CostEstimate(flops=1000000, bytes_accessed=5000000, transcendentals=0),
    )(index, mine, theirs)


def make_local(ny):
    half_y = ny // 2
    swap = [(0, 1), (1, 0)]

    def flat4(y, x, c, d):
        return ((y * 2 + x) * 2 + c) * 2 + d

    def shift(h):
        return (4 * h - 2) % ny

    def token_moves(cross):
        pairs = []
        for y in range(ny):
            for x in range(2):
                for c in range(2):
                    for d in range(2):
                        to_y = ((y % half_y) * 2 + x + shift(y // half_y)) % ny
                        to_x = 1 - c if cross else c
                        pairs.append((flat4(y, x, c, d), flat4(to_y, to_x, d, y // half_y)))
        return pairs

    def flat2(c, d):
        return c * 2 + d

    scaled_a = [(flat2(c, k), flat2(k, c)) for c in range(2) for k in range(2)]
    scaled_b = [(flat2(c, k), flat2(k, 1 - c)) for c in range(2) for k in range(2)]
    sums_a = [(flat2(1 - g, g), flat2(1 - g, 1 - g)) for g in range(2)] + [
        (flat2(g, g), flat2(1 - g, g)) for g in range(2)
    ]
    sums_b = [(flat2(1 - g, g), flat2(g, 1 - g)) for g in range(2)]
    ring_a = [(y * 2 + c, ((y + 1 - 2 * c) % ny) * 2 + c) for y in range(ny) for c in range(2)]
    ring_b = [(y * 2 + c, ((y - 1 + 2 * c) % ny) * 2 + c) for y in range(ny) for c in range(2)]

    def local(cotangent, expert_ids, combine, gate_saved, up_saved, w_down):
        expert_count = lax.axis_size("expert")
        y = lax.axis_index("y")
        core = lax.axis_index("core")
        xlo = lax.axis_index("xlo")
        dp = lax.axis_index("dp")
        rows = gate_saved.shape[2]
        width = gate_saved.shape[3]
        capacity = rows // expert_count
        lanes = cotangent.shape[2]
        chip = 2 * lanes
        every = ("y", "xlo", "core", "dp")

        ids = expert_ids[0].astype(BF)
        moved = lax.ppermute(jnp.concatenate([cotangent[0], ids], axis=1), every, token_moves(False))
        across = lax.ppermute(cotangent[0], every, token_moves(True))
        mine = moved[:, :lanes]
        tokens = jnp.concatenate([jnp.where(xlo == 0, mine, across), jnp.where(xlo == 0, across, mine)], axis=1)
        table = one_hot_table(moved[:, lanes:].astype(jnp.int32), expert_count, capacity)
        outgoing = jnp.dot(table, tokens, preferred_element_type=F32).astype(BF)
        outgoing = outgoing.reshape(expert_count, capacity, chip)
        part = lax.all_to_all(outgoing, "expert", split_axis=0, concat_axis=0, tiled=True)

        gate = gate_saved[0, 0].astype(F32)
        upper = up_saved[0, 0].astype(F32)
        weight_rows = combine[0, 0][:, None]
        sigma = jax.nn.sigmoid(gate)
        active = gate * sigma
        scaled = (weight_rows * (active * upper)).astype(BF)
        s_a = lax.ppermute(scaled, ("core", "dp"), scaled_a)
        s_b = lax.ppermute(scaled, ("core", "dp"), scaled_b)
        w_moved = lax.ppermute(w_down[0], "core", swap)

        held_own = dp == core
        turn = jnp.where(core == 0, -1, 1)
        shift_here = jnp.where(dp == 0, shift(0), shift(1))
        order = [0, 1]
        for step in range(2, half_y):
            order += [step, 1 - step]
        order += [1 - half_y, half_y]
        partner = [order.index(-o) if abs(o) < half_y else order.index(o) for o in order]
        spots = [(y + turn * o + 2 * ny - shift_here) % ny for o in order]
        index = jnp.stack(spots + [held_own.astype(jnp.int32), core]).astype(jnp.int32)
        place_index = jnp.stack(spots + [jnp.int32(p) for p in partner]).astype(jnp.int32)
        on_a = lambda v: lax.ppermute(v, ("y", "core"), ring_a)
        on_b = lambda v: lax.ppermute(v, ("y", "core"), ring_b)
        block = part.reshape(rows, chip)
        a = on_a(block)
        block_b, s_a, s_b = lax.optimization_barrier((block, s_a, s_b))
        b = on_b(block_b)
        args = (w_down[0].reshape(ny, chip, width), w_moved.reshape(ny, chip, width), s_a, s_b)
        waiting, start, held = [block_b, a], 0, None
        for step in range(2, half_y + 1):
            if held is not None:
                a, acc = lax.optimization_barrier((a, held[0]))
                held = (acc, *held[1:])
            a = on_a(a)
            held = use(waiting, index, start, *args, held)
            start += 2
            waiting = [a, b]
            if step < half_y:
                b, acc = lax.optimization_barrier((b, held[0]))
                held = (acc, *held[1:])
                b = on_b(b)
        held = use([b], index, start, *args, held)
        acc, mine, theirs, sum_a, sum_b, mix = use([a], index, start + 1, *args, held, last=True)

        got_a = lax.ppermute(sum_a, ("core", "dp"), sums_a)
        got_b = lax.ppermute(sum_b, ("core", "dp"), sums_b)
        members = 2 * ny * 4
        share = rows // (ny * 4)
        mix = lax.all_to_all(mix.reshape(members, share), ("dp", "y", "xlo", "core"), 0, 0, tiled=True)
        late = lax.ppermute(theirs, "core", swap)
        grad_weight = place(place_index, mine, late).reshape(ny * chip, width)
        grad_hidden = jnp.where(held_own, acc, got_b.astype(F32)) + got_a.astype(F32)
        weighted = weight_rows * grad_hidden
        grad_gate = (weighted * upper * sigma * (1.0 + gate * (1.0 - sigma))).astype(BF)
        grad_upper = (weighted * active).astype(BF)
        mix, grad_gate, grad_upper, grad_weight = lax.optimization_barrier((mix, grad_gate, grad_upper, grad_weight))
        mix = jnp.sum(mix, axis=0)
        blk = (y * 2 + xlo) * 2 + core
        mix = mix / lax.dynamic_slice_in_dim(combine[0, 0], blk * share, share, 0)
        return grad_gate[None, None], grad_upper[None, None], grad_weight[None], mix[None, None]

    return local


def solution(mesh):
    ne, nb, nd = mesh.devices.shape
    fine = Mesh(mesh.devices.reshape(ne, nb // 4, 2, 2, nd), ("expert", "y", "xlo", "core", "dp"))
    blk = ("y", "xlo", "core")
    return jax.shard_map(
        make_local(nb // 4),
        mesh=fine,
        in_specs=(
            P("dp", "expert", blk),
            P("dp", "expert", None),
            P("dp", "expert", None),
            P("dp", "expert", None, blk),
            P("dp", "expert", None, blk),
            P("expert", "dp", blk),
        ),
        out_specs=(
            P("dp", "expert", None, blk),
            P("dp", "expert", None, blk),
            P("expert", "dp", blk),
            P("dp", "expert", blk),
        ),
        check_vma=False,
    )
```

```python
import functools

import jax
import jax.numpy as jnp
from jax import lax
from jax.experimental import pallas as pl
from jax.experimental.pallas import tpu as pltpu
from jax.sharding import Mesh, PartitionSpec as P

BF = jnp.bfloat16
F32 = jnp.float32
VMEM_LIMIT = 60 * 1024 * 1024


def one_hot_table(ids, expert_count, capacity):
    experts = jnp.arange(expert_count, dtype=jnp.int32)
    chosen = (ids[:, :, None] == experts).astype(F32)
    per_token = jnp.sum(chosen, axis=1)
    count = ids.shape[0]
    before = (jnp.arange(count)[:, None] > jnp.arange(count)[None, :]).astype(BF)
    earlier = jnp.dot(before, per_token.astype(BF), preferred_element_type=F32)
    position = jnp.sum(chosen * earlier[:, None, :], axis=-1).astype(jnp.int32)
    target = ids * capacity + position
    columns = jnp.arange(expert_count * capacity, dtype=jnp.int32)
    hit = (target[:, 0][None, :] == columns[:, None]) | (target[:, 1][None, :] == columns[:, None])
    return hit.astype(BF)


def use_kernel(blocks, first, last, index, *refs):
    it = iter(refs)
    x_refs = [next(it) for _ in range(blocks)]
    w_mine = [next(it) for _ in range(blocks)]
    w_theirs = [next(it) for _ in range(blocks)]
    s_a, s_b = next(it), next(it)
    acc_in = None
    if not first:
        acc_in, _, _ = next(it), next(it), next(it)
    acc, g_mine, g_theirs = next(it), next(it), next(it)
    width = s_a.shape[1]
    flags = index.shape[0] - 2
    own = index[flags] == 1
    s_mine = jnp.where(own, s_a[...], s_b[...])
    s_theirs = jnp.where(own, s_b[...], s_a[...])
    s = jnp.concatenate([s_mine, s_theirs], axis=1)
    for b in range(blocks):
        x = x_refs[b][...]
        w = jnp.concatenate([w_mine[b][0], w_theirs[b][0]], axis=1)
        product = jnp.dot(x, w, preferred_element_type=F32)
        if last:
            total = product + acc_in[...]
        elif b == 0:
            acc[...] = product if first else product + acc_in[...]
        else:
            acc[...] += product
        outer = lax.dot_general(x, s, (((0,), (0,)), ((), ())), preferred_element_type=F32)
        g_mine[b] = outer[:, :width].astype(BF)
        g_theirs[b] = outer[:, width:].astype(BF)
    if last:
        sum_a, sum_b, mix = next(it), next(it), next(it)
        mine, theirs = total[:, :width], total[:, width:]
        acc[...] = mine
        sum_b[...] = theirs.astype(BF)
        sum_a[...] = jnp.where(own, theirs, mine).astype(BF)
        terms = s_mine.astype(F32) * mine + s_theirs.astype(F32) * theirs
        line = lax.dot_general(
            jnp.ones((8, width), F32),
            terms,
            (((1,), (1,)), ((), ())),
            precision=lax.Precision.HIGHEST,
            preferred_element_type=F32,
        )
        row = lax.broadcasted_iota(jnp.int32, (2, line.shape[1]), 0)
        mix[...] = jnp.where(row == index[flags + 1], line[:2], 0.0)


def use(pieces, index, start, w_mine, w_theirs, s_a, s_b, held, last=False):
    first = held is None
    blocks = len(pieces)
    rows, width = s_a.shape
    total, chip, _ = w_mine.shape
    assert start % blocks == 0

    def whole(a):
        return pl.BlockSpec(a.shape, lambda i, idx: (0,) * len(a.shape))

    def pick(j):
        return pl.BlockSpec((1, chip, width), lambda i, idx: (idx[start + j], 0, 0))

    ins = list(pieces) + [w_mine] * blocks + [w_theirs] * blocks + [s_a, s_b]
    specs = [whole(a) for a in pieces] + [pick(j) for j in range(blocks)] * 2 + [whole(s_a), whole(s_b)]
    aliases = {}
    if not first:
        n = 1 + len(ins)
        aliases = {n + 1: 1, n + 2: 2} if last else {n: 0, n + 1: 1, n + 2: 2}
        ins += list(held)
        specs += [whole(held[0]), pl.BlockSpec(memory_space=pl.ANY), pl.BlockSpec(memory_space=pl.ANY)]
    slot = pl.BlockSpec((blocks, chip, width), lambda i, idx: (start // blocks, 0, 0))
    outs = [jax.ShapeDtypeStruct((rows, width if last else 2 * width), F32)]
    outs += [jax.ShapeDtypeStruct((total, chip, width), BF)] * 2
    extra = []
    if last:
        extra = [jax.ShapeDtypeStruct((rows, width), BF)] * 2 + [jax.ShapeDtypeStruct((2, rows), F32)]
    return pl.pallas_call(
        functools.partial(use_kernel, blocks, first, last),
        grid_spec=pltpu.PrefetchScalarGridSpec(
            num_scalar_prefetch=1,
            grid=(1,),
            in_specs=specs,
            out_specs=[whole(outs[0]), slot, slot] + [whole(o) for o in extra],
        ),
        out_shape=outs + extra,
        input_output_aliases=aliases,
        compiler_params=pltpu.CompilerParams(vmem_limit_bytes=VMEM_LIMIT),
        cost_estimate=pl.CostEstimate(
            flops=8 * blocks * rows * chip * width, bytes_accessed=blocks * 4000000, transcendentals=0
        ),
    )(index, *ins)


def place_kernel(partner, index, mine, theirs, out):
    for i, p in enumerate(partner):
        out[index[i]] = (mine[i].astype(F32) + theirs[p].astype(F32)).astype(BF)


def place(index, partner, mine, theirs):
    def whole(a):
        return pl.BlockSpec(a.shape, lambda i, idx: (0, 0, 0))

    return pl.pallas_call(
        functools.partial(place_kernel, tuple(partner)),
        grid_spec=pltpu.PrefetchScalarGridSpec(
            num_scalar_prefetch=1,
            grid=(1,),
            in_specs=[whole(mine), whole(theirs)],
            out_specs=whole(mine),
        ),
        out_shape=jax.ShapeDtypeStruct(mine.shape, BF),
        compiler_params=pltpu.CompilerParams(vmem_limit_bytes=16 * 1024 * 1024),
        cost_estimate=pl.CostEstimate(flops=1000000, bytes_accessed=5000000, transcendentals=0),
    )(index, mine, theirs)


def make_local(ny):
    half_y = ny // 2
    swap = [(0, 1), (1, 0)]

    def flat4(y, x, c, d):
        return ((y * 2 + x) * 2 + c) * 2 + d

    def shift(h):
        return (4 * h - 2) % ny

    def token_moves(cross):
        pairs = []
        for y in range(ny):
            for x in range(2):
                for c in range(2):
                    for d in range(2):
                        to_y = ((y % half_y) * 2 + x + shift(y // half_y)) % ny
                        to_x = 1 - c if cross else c
                        pairs.append((flat4(y, x, c, d), flat4(to_y, to_x, d, y // half_y)))
        return pairs

    def flat2(c, d):
        return c * 2 + d

    scaled_a = [(flat2(c, k), flat2(k, c)) for c in range(2) for k in range(2)]
    scaled_b = [(flat2(c, k), flat2(k, 1 - c)) for c in range(2) for k in range(2)]
    sums_a = [(flat2(1 - g, g), flat2(1 - g, 1 - g)) for g in range(2)] + [
        (flat2(g, g), flat2(1 - g, g)) for g in range(2)
    ]
    sums_b = [(flat2(1 - g, g), flat2(g, 1 - g)) for g in range(2)]
    ring_a = [(y * 2 + c, ((y + 1 - 2 * c) % ny) * 2 + c) for y in range(ny) for c in range(2)]
    ring_b = [(y * 2 + c, ((y - 1 + 2 * c) % ny) * 2 + c) for y in range(ny) for c in range(2)]

    def local(cotangent, expert_ids, combine, gate_saved, up_saved, w_down):
        expert_count = lax.axis_size("expert")
        y = lax.axis_index("y")
        core = lax.axis_index("core")
        xlo = lax.axis_index("xlo")
        dp = lax.axis_index("dp")
        rows = gate_saved.shape[2]
        width = gate_saved.shape[3]
        capacity = rows // expert_count
        lanes = cotangent.shape[2]
        chip = 2 * lanes
        every = ("y", "xlo", "core", "dp")

        ids = expert_ids[0].astype(BF)
        moved = lax.ppermute(jnp.concatenate([cotangent[0], ids], axis=1), every, token_moves(False))
        across = lax.ppermute(cotangent[0], every, token_moves(True))
        mine = moved[:, :lanes]
        tokens = jnp.concatenate([jnp.where(xlo == 0, mine, across), jnp.where(xlo == 0, across, mine)], axis=1)
        table = one_hot_table(moved[:, lanes:].astype(jnp.int32), expert_count, capacity)
        outgoing = jnp.dot(table, tokens, preferred_element_type=F32).astype(BF)
        outgoing = outgoing.reshape(expert_count, capacity, chip)
        part = lax.all_to_all(outgoing, "expert", split_axis=0, concat_axis=0, tiled=True)

        gate = gate_saved[0, 0].astype(F32)
        upper = up_saved[0, 0].astype(F32)
        weight_rows = combine[0, 0][:, None]
        sigma = jax.nn.sigmoid(gate)
        active = gate * sigma
        scaled = (weight_rows * (active * upper)).astype(BF)
        s_a = lax.ppermute(scaled, ("core", "dp"), scaled_a)
        s_b = lax.ppermute(scaled, ("core", "dp"), scaled_b)
        w_moved = lax.ppermute(w_down[0], "core", swap)

        held_own = dp == core
        turn = jnp.where(core == 0, -1, 1)
        shift_here = jnp.where(dp == 0, shift(0), shift(1))
        order = [0, 1]
        for step in range(2, half_y):
            order += [step, 1 - step]
        order += [1 - half_y, half_y]
        partner = [order.index(-o) if abs(o) < half_y else order.index(o) for o in order]
        spots = [(y + turn * o + 2 * ny - shift_here) % ny for o in order]
        index = jnp.stack(spots + [held_own.astype(jnp.int32), core]).astype(jnp.int32)
        on_a = lambda v: lax.ppermute(v, ("y", "core"), ring_a)
        on_b = lambda v: lax.ppermute(v, ("y", "core"), ring_b)
        block = part.reshape(rows, chip)
        block, s_a, s_b = lax.optimization_barrier((block, s_a, s_b))
        a = on_a(block)
        args = (w_down[0].reshape(ny, chip, width), w_moved.reshape(ny, chip, width), s_a, s_b)
        held = use([block], index, 0, *args, None)
        block_b, acc = lax.optimization_barrier((block, held[0]))
        held = (acc, *held[1:])
        b = on_b(block_b)
        waiting, start = [a], 1
        for step in range(2, half_y + 1):
            a, acc = lax.optimization_barrier((a, held[0]))
            held = (acc, *held[1:])
            a = on_a(a)
            held = use(waiting, index, start, *args, held)
            start += len(waiting)
            waiting = [a, b]
            if step < half_y:
                b, acc = lax.optimization_barrier((b, held[0]))
                held = (acc, *held[1:])
                b = on_b(b)
        held = use([b], index, start, *args, held)
        acc, mine, theirs, sum_a, sum_b, mix = use([a], index, start + 1, *args, held, last=True)

        got_a = lax.ppermute(sum_a, ("core", "dp"), sums_a)
        got_b = lax.ppermute(sum_b, ("core", "dp"), sums_b)
        members = 2 * ny * 4
        share = rows // (ny * 4)
        mix = lax.all_to_all(mix.reshape(members, share), ("dp", "y", "xlo", "core"), 0, 0, tiled=True)
        late = lax.ppermute(theirs, "core", swap)
        grad_weight = place(index, partner, mine, late).reshape(ny * chip, width)
        grad_hidden = jnp.where(held_own, acc, got_b.astype(F32)) + got_a.astype(F32)
        weighted = weight_rows * grad_hidden
        grad_gate = (weighted * upper * sigma * (1.0 + gate * (1.0 - sigma))).astype(BF)
        grad_upper = (weighted * active).astype(BF)
        mix, grad_gate, grad_upper, grad_weight = lax.optimization_barrier((mix, grad_gate, grad_upper, grad_weight))
        mix = jnp.sum(mix, axis=0)
        blk = (y * 2 + xlo) * 2 + core
        mix = mix / lax.dynamic_slice_in_dim(combine[0, 0], blk * share, share, 0)
        return grad_gate[None, None], grad_upper[None, None], grad_weight[None], mix[None, None]

    return local


def solution(mesh):
    ne, nb, nd = mesh.devices.shape
    fine = Mesh(mesh.devices.reshape(ne, nb // 4, 2, 2, nd), ("expert", "y", "xlo", "core", "dp"))
    blk = ("y", "xlo", "core")
    return jax.shard_map(
        make_local(nb // 4),
        mesh=fine,
        in_specs=(
            P("dp", "expert", blk),
            P("dp", "expert", None),
            P("dp", "expert", None),
            P("dp", "expert", None, blk),
            P("dp", "expert", None, blk),
            P("expert", "dp", blk),
        ),
        out_specs=(
            P("dp", "expert", None, blk),
            P("dp", "expert", None, blk),
            P("expert", "dp", blk),
            P("dp", "expert", blk),
        ),
        check_vma=False,
    )
```

```python
import functools

import jax
import jax.numpy as jnp
from jax import lax
from jax.experimental import pallas as pl
from jax.experimental.pallas import tpu as pltpu
from jax.sharding import Mesh, PartitionSpec as P

BF = jnp.bfloat16
F32 = jnp.float32
VMEM_LIMIT = 24 * 1024 * 1024


def one_hot_table(ids, expert_count, capacity):
    experts = jnp.arange(expert_count, dtype=jnp.int32)
    chosen = (ids[:, :, None] == experts).astype(F32)
    per_token = jnp.sum(chosen, axis=1)
    count = ids.shape[0]
    before = (jnp.arange(count)[:, None] > jnp.arange(count)[None, :]).astype(BF)
    earlier = jnp.dot(before, per_token.astype(BF), preferred_element_type=F32)
    position = jnp.sum(chosen * earlier[:, None, :], axis=-1).astype(jnp.int32)
    target = ids * capacity + position
    columns = jnp.arange(expert_count * capacity, dtype=jnp.int32)
    hit = (target[:, 0][None, :] == columns[:, None]) | (target[:, 1][None, :] == columns[:, None])
    return hit.astype(BF)


def use_kernel(blocks, first, last, index, *refs):
    it = iter(refs)
    x_refs = [next(it) for _ in range(blocks)]
    w_mine = [next(it) for _ in range(blocks)]
    w_theirs = [next(it) for _ in range(blocks)]
    s_a, s_b = next(it), next(it)
    acc_in = None
    if not first:
        acc_in, _, _ = next(it), next(it), next(it)
    acc, g_mine, g_theirs = next(it), next(it), next(it)
    width = s_a.shape[1]
    flags = index.shape[0] - 2
    own = index[flags] == 1
    s_mine = jnp.where(own, s_a[...], s_b[...])
    s_theirs = jnp.where(own, s_b[...], s_a[...])
    s = jnp.concatenate([s_mine, s_theirs], axis=1)
    for b in range(blocks):
        x = x_refs[b][...]
        w = jnp.concatenate([w_mine[b][0], w_theirs[b][0]], axis=1)
        product = jnp.dot(x, w, preferred_element_type=F32)
        if last:
            total = product + acc_in[...]
        elif b == 0:
            acc[...] = product if first else product + acc_in[...]
        else:
            acc[...] += product
        outer = lax.dot_general(x, s, (((0,), (0,)), ((), ())), preferred_element_type=F32)
        g_mine[b] = outer[:, :width].astype(BF)
        g_theirs[b] = outer[:, width:].astype(BF)
    if last:
        sum_a, sum_b, mix = next(it), next(it), next(it)
        mine, theirs = total[:, :width], total[:, width:]
        acc[...] = mine
        sum_b[...] = theirs.astype(BF)
        sum_a[...] = jnp.where(own, theirs, mine).astype(BF)
        terms = s_mine.astype(F32) * mine + s_theirs.astype(F32) * theirs
        line = lax.dot_general(
            jnp.ones((8, width), F32),
            terms,
            (((1,), (1,)), ((), ())),
            precision=lax.Precision.HIGHEST,
            preferred_element_type=F32,
        )
        row = lax.broadcasted_iota(jnp.int32, (2, line.shape[1]), 0)
        mix[...] = jnp.where(row == index[flags + 1], line[:2], 0.0)


def use(pieces, index, start, w_mine, w_theirs, s_a, s_b, held, last=False):
    first = held is None
    blocks = len(pieces)
    rows, width = s_a.shape
    total, chip, _ = w_mine.shape
    assert start % blocks == 0

    def whole(a):
        return pl.BlockSpec(a.shape, lambda i, idx: (0,) * len(a.shape))

    def pick(j):
        return pl.BlockSpec((1, chip, width), lambda i, idx: (idx[start + j], 0, 0))

    ins = list(pieces) + [w_mine] * blocks + [w_theirs] * blocks + [s_a, s_b]
    specs = [whole(a) for a in pieces] + [pick(j) for j in range(blocks)] * 2 + [whole(s_a), whole(s_b)]
    aliases = {}
    if not first:
        n = 1 + len(ins)
        aliases = {n + 1: 1, n + 2: 2} if last else {n: 0, n + 1: 1, n + 2: 2}
        ins += list(held)
        specs += [whole(held[0]), pl.BlockSpec(memory_space=pl.ANY), pl.BlockSpec(memory_space=pl.ANY)]
    slot = pl.BlockSpec((blocks, chip, width), lambda i, idx: (start // blocks, 0, 0))
    outs = [jax.ShapeDtypeStruct((rows, width if last else 2 * width), F32)]
    outs += [jax.ShapeDtypeStruct((total, chip, width), BF)] * 2
    extra = []
    if last:
        extra = [jax.ShapeDtypeStruct((rows, width), BF)] * 2 + [jax.ShapeDtypeStruct((2, rows), F32)]
    return pl.pallas_call(
        functools.partial(use_kernel, blocks, first, last),
        grid_spec=pltpu.PrefetchScalarGridSpec(
            num_scalar_prefetch=1,
            grid=(1,),
            in_specs=specs,
            out_specs=[whole(outs[0]), slot, slot] + [whole(o) for o in extra],
        ),
        out_shape=outs + extra,
        input_output_aliases=aliases,
        compiler_params=pltpu.CompilerParams(vmem_limit_bytes=VMEM_LIMIT),
        cost_estimate=pl.CostEstimate(
            flops=8 * blocks * rows * chip * width, bytes_accessed=blocks * 4000000, transcendentals=0
        ),
    )(index, *ins)


def place_kernel(partner, index, mine, theirs, out):
    for i, p in enumerate(partner):
        out[index[i]] = (mine[i].astype(F32) + theirs[p].astype(F32)).astype(BF)


def place(index, partner, mine, theirs):
    def whole(a):
        return pl.BlockSpec(a.shape, lambda i, idx: (0, 0, 0))

    return pl.pallas_call(
        functools.partial(place_kernel, tuple(partner)),
        grid_spec=pltpu.PrefetchScalarGridSpec(
            num_scalar_prefetch=1,
            grid=(1,),
            in_specs=[whole(mine), whole(theirs)],
            out_specs=whole(mine),
        ),
        out_shape=jax.ShapeDtypeStruct(mine.shape, BF),
        compiler_params=pltpu.CompilerParams(vmem_limit_bytes=16 * 1024 * 1024),
        cost_estimate=pl.CostEstimate(flops=1000000, bytes_accessed=5000000, transcendentals=0),
    )(index, mine, theirs)


def make_local(ny):
    half_y = ny // 2
    swap = [(0, 1), (1, 0)]

    def flat4(y, x, c, d):
        return ((y * 2 + x) * 2 + c) * 2 + d

    def shift(h):
        return (4 * h - 2) % ny

    def token_moves(cross):
        pairs = []
        for y in range(ny):
            for x in range(2):
                for c in range(2):
                    for d in range(2):
                        to_y = ((y % half_y) * 2 + x + shift(y // half_y)) % ny
                        to_x = 1 - c if cross else c
                        pairs.append((flat4(y, x, c, d), flat4(to_y, to_x, d, y // half_y)))
        return pairs

    def flat2(c, d):
        return c * 2 + d

    scaled_a = [(flat2(c, k), flat2(k, c)) for c in range(2) for k in range(2)]
    scaled_b = [(flat2(c, k), flat2(k, 1 - c)) for c in range(2) for k in range(2)]
    sums_a = [(flat2(1 - g, g), flat2(1 - g, 1 - g)) for g in range(2)] + [
        (flat2(g, g), flat2(1 - g, g)) for g in range(2)
    ]
    sums_b = [(flat2(1 - g, g), flat2(g, 1 - g)) for g in range(2)]
    ring_a = [(y * 2 + c, ((y + 1 - 2 * c) % ny) * 2 + c) for y in range(ny) for c in range(2)]
    ring_b = [(y * 2 + c, ((y - 1 + 2 * c) % ny) * 2 + c) for y in range(ny) for c in range(2)]

    def local(cotangent, expert_ids, combine, gate_saved, up_saved, w_down):
        expert_count = lax.axis_size("expert")
        y = lax.axis_index("y")
        core = lax.axis_index("core")
        xlo = lax.axis_index("xlo")
        dp = lax.axis_index("dp")
        rows = gate_saved.shape[2]
        width = gate_saved.shape[3]
        capacity = rows // expert_count
        lanes = cotangent.shape[2]
        chip = 2 * lanes
        every = ("y", "xlo", "core", "dp")

        ids = expert_ids[0].astype(BF)
        moved = lax.ppermute(jnp.concatenate([cotangent[0], ids], axis=1), every, token_moves(False))
        across = lax.ppermute(cotangent[0], every, token_moves(True))
        mine = moved[:, :lanes]
        tokens = jnp.concatenate([jnp.where(xlo == 0, mine, across), jnp.where(xlo == 0, across, mine)], axis=1)
        table = one_hot_table(moved[:, lanes:].astype(jnp.int32), expert_count, capacity)
        outgoing = jnp.dot(table, tokens, preferred_element_type=F32).astype(BF)
        outgoing = outgoing.reshape(expert_count, capacity, chip)
        part = lax.all_to_all(outgoing, "expert", split_axis=0, concat_axis=0, tiled=True)

        gate = gate_saved[0, 0].astype(F32)
        upper = up_saved[0, 0].astype(F32)
        weight_rows = combine[0, 0][:, None]
        sigma = jax.nn.sigmoid(gate)
        active = gate * sigma
        scaled = (weight_rows * (active * upper)).astype(BF)
        s_a = lax.ppermute(scaled, ("core", "dp"), scaled_a)
        s_b = lax.ppermute(scaled, ("core", "dp"), scaled_b)
        w_moved = lax.ppermute(w_down[0], "core", swap)

        held_own = dp == core
        turn = jnp.where(core == 0, -1, 1)
        shift_here = jnp.where(dp == 0, shift(0), shift(1))
        order = [0, 1]
        for step in range(2, half_y):
            order += [step, 1 - step]
        order += [1 - half_y, half_y]
        partner = [order.index(-o) if abs(o) < half_y else order.index(o) for o in order]
        spots = [(y + turn * o + 2 * ny - shift_here) % ny for o in order]
        index = jnp.stack(spots + [held_own.astype(jnp.int32), core]).astype(jnp.int32)
        on_a = lambda v: lax.ppermute(v, ("y", "core"), ring_a)
        on_b = lambda v: lax.ppermute(v, ("y", "core"), ring_b)
        block = part.reshape(rows, chip)
        block, s_a, s_b = lax.optimization_barrier((block, s_a, s_b))
        a = on_a(block)
        args = (w_down[0].reshape(ny, chip, width), w_moved.reshape(ny, chip, width), s_a, s_b)
        held = use([block], index, 0, *args, None)
        block_b, acc = lax.optimization_barrier((block, held[0]))
        held = (acc, *held[1:])
        b = on_b(block_b)
        waiting, start = [a], 1
        for step in range(2, half_y + 1):
            a, acc = lax.optimization_barrier((a, held[0]))
            held = (acc, *held[1:])
            a = on_a(a)
            held = use(waiting, index, start, *args, held)
            start += len(waiting)
            waiting = [a, b]
            if step < half_y:
                b, acc = lax.optimization_barrier((b, held[0]))
                held = (acc, *held[1:])
                b = on_b(b)
        held = use([b], index, start, *args, held)
        acc, mine, theirs, sum_a, sum_b, mix = use([a], index, start + 1, *args, held, last=True)

        got_a = lax.ppermute(sum_a, ("core", "dp"), sums_a)
        got_b = lax.ppermute(sum_b, ("core", "dp"), sums_b)
        members = 2 * ny * 4
        share = rows // (ny * 4)
        mix = lax.all_to_all(mix.reshape(members, share), ("dp", "y", "xlo", "core"), 0, 0, tiled=True)
        late = lax.ppermute(theirs, "core", swap)
        grad_weight = place(index, partner, mine, late).reshape(ny * chip, width)
        grad_hidden = jnp.where(held_own, acc, got_b.astype(F32)) + got_a.astype(F32)
        weighted = weight_rows * grad_hidden
        grad_gate = (weighted * upper * sigma * (1.0 + gate * (1.0 - sigma))).astype(BF)
        grad_upper = (weighted * active).astype(BF)
        mix, grad_gate, grad_upper, grad_weight = lax.optimization_barrier((mix, grad_gate, grad_upper, grad_weight))
        mix = jnp.sum(mix, axis=0)
        blk = (y * 2 + xlo) * 2 + core
        mix = mix / lax.dynamic_slice_in_dim(combine[0, 0], blk * share, share, 0)
        return grad_gate[None, None], grad_upper[None, None], grad_weight[None], mix[None, None]

    return local


def solution(mesh):
    ne, nb, nd = mesh.devices.shape
    fine = Mesh(mesh.devices.reshape(ne, nb // 4, 2, 2, nd), ("expert", "y", "xlo", "core", "dp"))
    blk = ("y", "xlo", "core")
    return jax.shard_map(
        make_local(nb // 4),
        mesh=fine,
        in_specs=(
            P("dp", "expert", blk),
            P("dp", "expert", None),
            P("dp", "expert", None),
            P("dp", "expert", None, blk),
            P("dp", "expert", None, blk),
            P("expert", "dp", blk),
        ),
        out_specs=(
            P("dp", "expert", None, blk),
            P("dp", "expert", None, blk),
            P("expert", "dp", blk),
            P("dp", "expert", blk),
        ),
        check_vma=False,
    )
```

```python
import functools

import jax
import jax.numpy as jnp
from jax import lax
from jax.experimental import pallas as pl
from jax.experimental.pallas import tpu as pltpu
from jax.sharding import Mesh, PartitionSpec as P

BF = jnp.bfloat16
F32 = jnp.float32
VMEM_LIMIT = 24 * 1024 * 1024


def one_hot_table(ids, expert_count, capacity):
    experts = jnp.arange(expert_count, dtype=jnp.int32)
    chosen = (ids[:, :, None] == experts).astype(F32)
    per_token = jnp.sum(chosen, axis=1)
    count = ids.shape[0]
    before = (jnp.arange(count)[:, None] > jnp.arange(count)[None, :]).astype(BF)
    earlier = jnp.dot(before, per_token.astype(BF), preferred_element_type=F32)
    position = jnp.sum(chosen * earlier[:, None, :], axis=-1).astype(jnp.int32)
    target = ids * capacity + position
    columns = jnp.arange(expert_count * capacity, dtype=jnp.int32)
    hit = (target[:, 0][None, :] == columns[:, None]) | (target[:, 1][None, :] == columns[:, None])
    return hit.astype(BF)


def use_kernel(blocks, first, last, index, *refs):
    it = iter(refs)
    x_refs = [next(it) for _ in range(blocks)]
    w_mine = [next(it) for _ in range(blocks)]
    w_theirs = [next(it) for _ in range(blocks)]
    s_a, s_b = next(it), next(it)
    acc_in = None
    if not first:
        acc_in, _, _ = next(it), next(it), next(it)
    acc, g_mine, g_theirs = next(it), next(it), next(it)
    width = s_a.shape[1]
    flags = index.shape[0] - 2
    own = index[flags] == 1
    s_mine = jnp.where(own, s_a[...], s_b[...])
    s_theirs = jnp.where(own, s_b[...], s_a[...])
    s = jnp.concatenate([s_mine, s_theirs], axis=1)
    for b in range(blocks):
        x = x_refs[b][...]
        w = jnp.concatenate([w_mine[b][0], w_theirs[b][0]], axis=1)
        product = jnp.dot(x, w, preferred_element_type=F32)
        if last:
            total = product + acc_in[...]
        elif b == 0:
            acc[...] = product if first else product + acc_in[...]
        else:
            acc[...] += product
        outer = lax.dot_general(x, s, (((0,), (0,)), ((), ())), preferred_element_type=F32)
        g_mine[b] = outer[:, :width].astype(BF)
        g_theirs[b] = outer[:, width:].astype(BF)
    if last:
        sum_a, sum_b, mix = next(it), next(it), next(it)
        mine, theirs = total[:, :width], total[:, width:]
        acc[...] = mine
        sum_b[...] = theirs.astype(BF)
        sum_a[...] = jnp.where(own, theirs, mine).astype(BF)
        terms = s_mine.astype(F32) * mine + s_theirs.astype(F32) * theirs
        line = lax.dot_general(
            jnp.ones((8, width), F32),
            terms,
            (((1,), (1,)), ((), ())),
            precision=lax.Precision.HIGHEST,
            preferred_element_type=F32,
        )
        row = lax.broadcasted_iota(jnp.int32, (2, line.shape[1]), 0)
        mix[...] = jnp.where(row == index[flags + 1], line[:2], 0.0)


def use(pieces, index, start, w_mine, w_theirs, s_a, s_b, held, last=False):
    first = held is None
    blocks = len(pieces)
    rows, width = s_a.shape
    total, chip, _ = w_mine.shape
    assert start % blocks == 0

    def whole(a):
        return pl.BlockSpec(a.shape, lambda i, idx: (0,) * len(a.shape))

    def pick(j):
        return pl.BlockSpec((1, chip, width), lambda i, idx: (idx[start + j], 0, 0))

    ins = list(pieces) + [w_mine] * blocks + [w_theirs] * blocks + [s_a, s_b]
    specs = [whole(a) for a in pieces] + [pick(j) for j in range(blocks)] * 2 + [whole(s_a), whole(s_b)]
    aliases = {}
    if not first:
        n = 1 + len(ins)
        aliases = {n + 1: 1, n + 2: 2} if last else {n: 0, n + 1: 1, n + 2: 2}
        ins += list(held)
        specs += [whole(held[0]), pl.BlockSpec(memory_space=pl.ANY), pl.BlockSpec(memory_space=pl.ANY)]
    slot = pl.BlockSpec((blocks, chip, width), lambda i, idx: (start // blocks, 0, 0))
    sums = (rows, width if last else 2 * width)
    outs = [pltpu.HBM(sums, F32) if last else jax.ShapeDtypeStruct(sums, F32)]
    outs += [pltpu.HBM((total, chip, width), BF)] * 2
    extra = []
    if last:
        extra = [jax.ShapeDtypeStruct((rows, width), BF)] * 2 + [jax.ShapeDtypeStruct((2, rows), F32)]
    return pl.pallas_call(
        functools.partial(use_kernel, blocks, first, last),
        grid_spec=pltpu.PrefetchScalarGridSpec(
            num_scalar_prefetch=1,
            grid=(1,),
            in_specs=specs,
            out_specs=[pl.BlockSpec(sums, lambda i, idx: (0, 0)), slot, slot] + [whole(o) for o in extra],
        ),
        out_shape=outs + extra,
        input_output_aliases=aliases,
        compiler_params=pltpu.CompilerParams(vmem_limit_bytes=VMEM_LIMIT),
        cost_estimate=pl.CostEstimate(
            flops=8 * blocks * rows * chip * width, bytes_accessed=blocks * 4000000, transcendentals=0
        ),
    )(index, *ins)


def place_kernel(partner, index, mine, theirs, out):
    for i, p in enumerate(partner):
        out[index[i]] = (mine[i].astype(F32) + theirs[p].astype(F32)).astype(BF)


def place(index, partner, mine, theirs):
    def whole(a):
        return pl.BlockSpec(a.shape, lambda i, idx: (0, 0, 0))

    return pl.pallas_call(
        functools.partial(place_kernel, tuple(partner)),
        grid_spec=pltpu.PrefetchScalarGridSpec(
            num_scalar_prefetch=1,
            grid=(1,),
            in_specs=[whole(mine), whole(theirs)],
            out_specs=whole(mine),
        ),
        out_shape=jax.ShapeDtypeStruct(mine.shape, BF),
        compiler_params=pltpu.CompilerParams(vmem_limit_bytes=16 * 1024 * 1024),
        cost_estimate=pl.CostEstimate(flops=1000000, bytes_accessed=5000000, transcendentals=0),
    )(index, mine, theirs)


def finish_kernel(index, own, got_a, got_b, gate_ref, up_ref, combine_ref, out_gate, out_up):
    flags = index.shape[0] - 2
    total = jnp.where(index[flags] == 1, own[...], got_b[...].astype(F32)) + got_a[...].astype(F32)
    gate = gate_ref[...].astype(F32)
    sigma = jax.nn.sigmoid(gate)
    weighted = combine_ref[:, :1] * total
    out_gate[...] = (weighted * up_ref[...].astype(F32) * sigma * (1.0 + gate * (1.0 - sigma))).astype(BF)
    out_up[...] = (weighted * (gate * sigma)).astype(BF)


def finish(index, own, got_a, got_b, gate, up, combine_wide):
    ins = (own, got_a, got_b, gate, up, combine_wide)

    def whole(a):
        return pl.BlockSpec(a.shape, lambda i, idx: (0, 0))

    return pl.pallas_call(
        finish_kernel,
        grid_spec=pltpu.PrefetchScalarGridSpec(
            num_scalar_prefetch=1,
            grid=(1,),
            in_specs=[whole(a) for a in ins],
            out_specs=[whole(gate), whole(up)],
        ),
        out_shape=[pltpu.HBM(gate.shape, BF)] * 2,
        compiler_params=pltpu.CompilerParams(vmem_limit_bytes=16 * 1024 * 1024),
        cost_estimate=pl.CostEstimate(flops=3000000, bytes_accessed=3500000, transcendentals=200000),
    )(index, *ins)


def make_local(ny):
    half_y = ny // 2
    swap = [(0, 1), (1, 0)]

    def flat4(y, x, c, d):
        return ((y * 2 + x) * 2 + c) * 2 + d

    def shift(h):
        return (4 * h - 2) % ny

    def token_moves(cross):
        pairs = []
        for y in range(ny):
            for x in range(2):
                for c in range(2):
                    for d in range(2):
                        to_y = ((y % half_y) * 2 + x + shift(y // half_y)) % ny
                        to_x = 1 - c if cross else c
                        pairs.append((flat4(y, x, c, d), flat4(to_y, to_x, d, y // half_y)))
        return pairs

    def flat2(c, d):
        return c * 2 + d

    scaled_a = [(flat2(c, k), flat2(k, c)) for c in range(2) for k in range(2)]
    scaled_b = [(flat2(c, k), flat2(k, 1 - c)) for c in range(2) for k in range(2)]
    sums_a = [(flat2(1 - g, g), flat2(1 - g, 1 - g)) for g in range(2)] + [
        (flat2(g, g), flat2(1 - g, g)) for g in range(2)
    ]
    sums_b = [(flat2(1 - g, g), flat2(g, 1 - g)) for g in range(2)]
    ring_a = [(y * 2 + c, ((y + 1 - 2 * c) % ny) * 2 + c) for y in range(ny) for c in range(2)]
    ring_b = [(y * 2 + c, ((y - 1 + 2 * c) % ny) * 2 + c) for y in range(ny) for c in range(2)]

    def local(cotangent, expert_ids, combine, gate_saved, up_saved, w_down):
        expert_count = lax.axis_size("expert")
        y = lax.axis_index("y")
        core = lax.axis_index("core")
        xlo = lax.axis_index("xlo")
        dp = lax.axis_index("dp")
        rows = gate_saved.shape[2]
        width = gate_saved.shape[3]
        capacity = rows // expert_count
        lanes = cotangent.shape[2]
        chip = 2 * lanes
        every = ("y", "xlo", "core", "dp")

        ids = expert_ids[0].astype(BF)
        moved = lax.ppermute(jnp.concatenate([cotangent[0], ids], axis=1), every, token_moves(False))
        across = lax.ppermute(cotangent[0], every, token_moves(True))
        mine = moved[:, :lanes]
        tokens = jnp.concatenate([jnp.where(xlo == 0, mine, across), jnp.where(xlo == 0, across, mine)], axis=1)
        table = one_hot_table(moved[:, lanes:].astype(jnp.int32), expert_count, capacity)
        outgoing = jnp.dot(table, tokens, preferred_element_type=F32).astype(BF)
        outgoing = outgoing.reshape(expert_count, capacity, chip)
        part = lax.all_to_all(outgoing, "expert", split_axis=0, concat_axis=0, tiled=True)

        gate = gate_saved[0, 0].astype(F32)
        upper = up_saved[0, 0].astype(F32)
        weight_rows = combine[0, 0][:, None]
        sigma = jax.nn.sigmoid(gate)
        active = gate * sigma
        combine_wide = jnp.broadcast_to(weight_rows, (rows, 128))
        scaled = (weight_rows * (active * upper)).astype(BF)
        w_moved = lax.ppermute(w_down[0], "core", swap)

        held_own = dp == core
        share = rows // (ny * 4)
        blk = (y * 2 + xlo) * 2 + core
        combine_share = lax.dynamic_slice_in_dim(combine[0, 0], blk * share, share, 0)
        combine_share, combine_wide, scaled = lax.optimization_barrier((combine_share, combine_wide, scaled))
        s_a = lax.ppermute(scaled, ("core", "dp"), scaled_a)
        s_b = lax.ppermute(scaled, ("core", "dp"), scaled_b)
        turn = jnp.where(core == 0, -1, 1)
        shift_here = jnp.where(dp == 0, shift(0), shift(1))
        order = [0, 1]
        for step in range(2, half_y):
            order += [step, 1 - step]
        order += [1 - half_y, half_y]
        partner = [order.index(-o) if abs(o) < half_y else order.index(o) for o in order]
        spots = [(y + turn * o + 2 * ny - shift_here) % ny for o in order]
        index = jnp.stack(spots + [held_own.astype(jnp.int32), core]).astype(jnp.int32)
        on_a = lambda v: lax.ppermute(v, ("y", "core"), ring_a)
        on_b = lambda v: lax.ppermute(v, ("y", "core"), ring_b)
        block = part.reshape(rows, chip)
        block, s_a, s_b = lax.optimization_barrier((block, s_a, s_b))
        a = on_a(block)
        args = (w_down[0].reshape(ny, chip, width), w_moved.reshape(ny, chip, width), s_a, s_b)
        held = use([block], index, 0, *args, None)
        block_b, acc = lax.optimization_barrier((block, held[0]))
        held = (acc, *held[1:])
        b = on_b(block_b)
        waiting, start = [a], 1
        for step in range(2, half_y + 1):
            a, acc = lax.optimization_barrier((a, held[0]))
            held = (acc, *held[1:])
            a = on_a(a)
            held = use(waiting, index, start, *args, held)
            start += len(waiting)
            waiting = [a, b]
            if step < half_y:
                b, acc = lax.optimization_barrier((b, held[0]))
                held = (acc, *held[1:])
                b = on_b(b)
        held = use([b], index, start, *args, held)
        acc, mine, theirs, sum_a, sum_b, mix = use([a], index, start + 1, *args, held, last=True)

        got_a = lax.ppermute(sum_a, ("core", "dp"), sums_a)
        got_b = lax.ppermute(sum_b, ("core", "dp"), sums_b)
        members = 2 * ny * 4
        mix = lax.all_to_all(mix.reshape(members, share), ("dp", "y", "xlo", "core"), 0, 0, tiled=True)
        late = lax.ppermute(theirs, "core", swap)
        grad_weight = place(index, partner, mine, late).reshape(ny * chip, width)
        grad_gate, grad_upper = finish(index, acc, got_a, got_b, gate_saved[0, 0], up_saved[0, 0], combine_wide)
        mix, grad_gate, grad_upper, grad_weight = lax.optimization_barrier((mix, grad_gate, grad_upper, grad_weight))
        mix = jnp.sum(mix, axis=0)
        mix = mix / combine_share
        return grad_gate[None, None], grad_upper[None, None], grad_weight[None], mix[None, None]

    return local


def solution(mesh):
    ne, nb, nd = mesh.devices.shape
    fine = Mesh(mesh.devices.reshape(ne, nb // 4, 2, 2, nd), ("expert", "y", "xlo", "core", "dp"))
    blk = ("y", "xlo", "core")
    return jax.shard_map(
        make_local(nb // 4),
        mesh=fine,
        in_specs=(
            P("dp", "expert", blk),
            P("dp", "expert", None),
            P("dp", "expert", None),
            P("dp", "expert", None, blk),
            P("dp", "expert", None, blk),
            P("expert", "dp", blk),
        ),
        out_specs=(
            P("dp", "expert", None, blk),
            P("dp", "expert", None, blk),
            P("expert", "dp", blk),
            P("dp", "expert", blk),
        ),
        check_vma=False,
    )
```

```python
import functools

import jax
import jax.numpy as jnp
from jax import lax
from jax.experimental import pallas as pl
from jax.experimental.pallas import tpu as pltpu
from jax.sharding import Mesh, PartitionSpec as P

BF = jnp.bfloat16
F32 = jnp.float32
VMEM_LIMIT = 24 * 1024 * 1024


def one_hot_table(ids, expert_count, capacity):
    experts = jnp.arange(expert_count, dtype=jnp.int32)
    chosen = (ids[:, :, None] == experts).astype(F32)
    per_token = jnp.sum(chosen, axis=1)
    count = ids.shape[0]
    before = (jnp.arange(count)[:, None] > jnp.arange(count)[None, :]).astype(BF)
    earlier = jnp.dot(before, per_token.astype(BF), preferred_element_type=F32)
    position = jnp.sum(chosen * earlier[:, None, :], axis=-1).astype(jnp.int32)
    target = ids * capacity + position
    columns = jnp.arange(expert_count * capacity, dtype=jnp.int32)
    hit = (target[:, 0][None, :] == columns[:, None]) | (target[:, 1][None, :] == columns[:, None])
    return hit.astype(BF)


def use_kernel(blocks, first, last, index, *refs):
    it = iter(refs)
    x_refs = [next(it) for _ in range(blocks)]
    w_mine = [next(it) for _ in range(blocks)]
    w_theirs = [next(it) for _ in range(blocks)]
    s_a, s_b = next(it), next(it)
    acc_in = None
    if not first:
        acc_in, _, _ = next(it), next(it), next(it)
    acc, g_mine, g_theirs = next(it), next(it), next(it)
    width = s_a.shape[1]
    flags = index.shape[0] - 2
    own = index[flags] == 1
    s_mine = jnp.where(own, s_a[...], s_b[...])
    s_theirs = jnp.where(own, s_b[...], s_a[...])
    s = jnp.concatenate([s_mine, s_theirs], axis=1)
    for b in range(blocks):
        x = x_refs[b][...]
        w = jnp.concatenate([w_mine[b][0], w_theirs[b][0]], axis=1)
        product = jnp.dot(x, w, preferred_element_type=F32)
        if last:
            total = product + acc_in[...]
        elif b == 0:
            acc[...] = product if first else product + acc_in[...]
        else:
            acc[...] += product
        outer = lax.dot_general(x, s, (((0,), (0,)), ((), ())), preferred_element_type=F32)
        g_mine[b] = outer[:, :width].astype(BF)
        g_theirs[b] = outer[:, width:].astype(BF)
    if last:
        sum_a, sum_b, mix = next(it), next(it), next(it)
        mine, theirs = total[:, :width], total[:, width:]
        acc[...] = mine
        sum_b[...] = theirs.astype(BF)
        sum_a[...] = jnp.where(own, theirs, mine).astype(BF)
        terms = s_mine.astype(F32) * mine + s_theirs.astype(F32) * theirs
        line = lax.dot_general(
            jnp.ones((8, width), F32),
            terms,
            (((1,), (1,)), ((), ())),
            precision=lax.Precision.HIGHEST,
            preferred_element_type=F32,
        )
        row = lax.broadcasted_iota(jnp.int32, (2, line.shape[1]), 0)
        mix[...] = jnp.where(row == index[flags + 1], line[:2], 0.0)


def use(pieces, index, start, w_mine, w_theirs, s_a, s_b, held, last=False):
    first = held is None
    blocks = len(pieces)
    rows, width = s_a.shape
    total, chip, _ = w_mine.shape
    assert start % blocks == 0

    def whole(a):
        return pl.BlockSpec(a.shape, lambda i, idx: (0,) * len(a.shape))

    def pick(j):
        return pl.BlockSpec((1, chip, width), lambda i, idx: (idx[start + j], 0, 0))

    ins = list(pieces) + [w_mine] * blocks + [w_theirs] * blocks + [s_a, s_b]
    specs = [whole(a) for a in pieces] + [pick(j) for j in range(blocks)] * 2 + [whole(s_a), whole(s_b)]
    aliases = {}
    if not first:
        n = 1 + len(ins)
        aliases = {n + 1: 1, n + 2: 2} if last else {n: 0, n + 1: 1, n + 2: 2}
        ins += list(held)
        specs += [whole(held[0]), pl.BlockSpec(memory_space=pl.ANY), pl.BlockSpec(memory_space=pl.ANY)]
    slot = pl.BlockSpec((blocks, chip, width), lambda i, idx: (start // blocks, 0, 0))
    sums = (rows, width if last else 2 * width)
    outs = [pltpu.HBM(sums, F32) if last else jax.ShapeDtypeStruct(sums, F32)]
    outs += [pltpu.HBM((total, chip, width), BF)] * 2
    extra = []
    if last:
        extra = [jax.ShapeDtypeStruct((rows, width), BF)] * 2 + [jax.ShapeDtypeStruct((2, rows), F32)]
    return pl.pallas_call(
        functools.partial(use_kernel, blocks, first, last),
        grid_spec=pltpu.PrefetchScalarGridSpec(
            num_scalar_prefetch=1,
            grid=(1,),
            in_specs=specs,
            out_specs=[pl.BlockSpec(sums, lambda i, idx: (0, 0)), slot, slot] + [whole(o) for o in extra],
        ),
        out_shape=outs + extra,
        input_output_aliases=aliases,
        compiler_params=pltpu.CompilerParams(vmem_limit_bytes=VMEM_LIMIT),
        cost_estimate=pl.CostEstimate(
            flops=8 * blocks * rows * chip * width, bytes_accessed=blocks * 4000000, transcendentals=0
        ),
    )(index, *ins)


def place_kernel(partner, index, mine, theirs, out):
    for i, p in enumerate(partner):
        out[index[i]] = (mine[i].astype(F32) + theirs[p].astype(F32)).astype(BF)


def place(index, partner, mine, theirs):
    def whole(a):
        return pl.BlockSpec(a.shape, lambda i, idx: (0, 0, 0))

    mine = pltpu.with_memory_space_constraint(mine, pltpu.HBM)
    return pl.pallas_call(
        functools.partial(place_kernel, tuple(partner)),
        grid_spec=pltpu.PrefetchScalarGridSpec(
            num_scalar_prefetch=1,
            grid=(1,),
            in_specs=[whole(mine), whole(theirs)],
            out_specs=whole(mine),
        ),
        out_shape=jax.ShapeDtypeStruct(mine.shape, BF),
        compiler_params=pltpu.CompilerParams(vmem_limit_bytes=16 * 1024 * 1024),
        cost_estimate=pl.CostEstimate(flops=1000000, bytes_accessed=5000000, transcendentals=0),
    )(index, mine, theirs)


def finish_kernel(index, own, got_a, got_b, gate_ref, up_ref, combine_ref, out_gate, out_up):
    flags = index.shape[0] - 2
    total = jnp.where(index[flags] == 1, own[...], got_b[...].astype(F32)) + got_a[...].astype(F32)
    gate = gate_ref[...].astype(F32)
    sigma = jax.nn.sigmoid(gate)
    weighted = combine_ref[:, :1] * total
    out_gate[...] = (weighted * up_ref[...].astype(F32) * sigma * (1.0 + gate * (1.0 - sigma))).astype(BF)
    out_up[...] = (weighted * (gate * sigma)).astype(BF)


def finish(index, own, got_a, got_b, gate, up, combine_wide):
    in_hbm = lambda a: pltpu.with_memory_space_constraint(a, pltpu.HBM)
    ins = (in_hbm(own), got_a, got_b, in_hbm(gate), in_hbm(up), in_hbm(combine_wide))

    def whole(a):
        return pl.BlockSpec(a.shape, lambda i, idx: (0, 0))

    return pl.pallas_call(
        finish_kernel,
        grid_spec=pltpu.PrefetchScalarGridSpec(
            num_scalar_prefetch=1,
            grid=(1,),
            in_specs=[whole(a) for a in ins],
            out_specs=[whole(gate), whole(up)],
        ),
        out_shape=[pltpu.HBM(gate.shape, BF)] * 2,
        compiler_params=pltpu.CompilerParams(vmem_limit_bytes=16 * 1024 * 1024),
        cost_estimate=pl.CostEstimate(flops=3000000, bytes_accessed=3500000, transcendentals=200000),
    )(index, *ins)


def make_local(ny):
    half_y = ny // 2
    swap = [(0, 1), (1, 0)]

    def flat4(y, x, c, d):
        return ((y * 2 + x) * 2 + c) * 2 + d

    def shift(h):
        return (4 * h - 2) % ny

    def token_moves(cross):
        pairs = []
        for y in range(ny):
            for x in range(2):
                for c in range(2):
                    for d in range(2):
                        to_y = ((y % half_y) * 2 + x + shift(y // half_y)) % ny
                        to_x = 1 - c if cross else c
                        pairs.append((flat4(y, x, c, d), flat4(to_y, to_x, d, y // half_y)))
        return pairs

    def flat2(c, d):
        return c * 2 + d

    scaled_a = [(flat2(c, k), flat2(k, c)) for c in range(2) for k in range(2)]
    scaled_b = [(flat2(c, k), flat2(k, 1 - c)) for c in range(2) for k in range(2)]
    sums_a = [(flat2(1 - g, g), flat2(1 - g, 1 - g)) for g in range(2)] + [
        (flat2(g, g), flat2(1 - g, g)) for g in range(2)
    ]
    sums_b = [(flat2(1 - g, g), flat2(g, 1 - g)) for g in range(2)]
    ring_a = [(y * 2 + c, ((y + 1 - 2 * c) % ny) * 2 + c) for y in range(ny) for c in range(2)]
    ring_b = [(y * 2 + c, ((y - 1 + 2 * c) % ny) * 2 + c) for y in range(ny) for c in range(2)]

    def local(cotangent, expert_ids, combine, gate_saved, up_saved, w_down):
        expert_count = lax.axis_size("expert")
        y = lax.axis_index("y")
        core = lax.axis_index("core")
        xlo = lax.axis_index("xlo")
        dp = lax.axis_index("dp")
        rows = gate_saved.shape[2]
        width = gate_saved.shape[3]
        capacity = rows // expert_count
        lanes = cotangent.shape[2]
        chip = 2 * lanes
        every = ("y", "xlo", "core", "dp")

        ids = expert_ids[0].astype(BF)
        moved = lax.ppermute(jnp.concatenate([cotangent[0], ids], axis=1), every, token_moves(False))
        across = lax.ppermute(cotangent[0], every, token_moves(True))
        mine = moved[:, :lanes]
        tokens = jnp.concatenate([jnp.where(xlo == 0, mine, across), jnp.where(xlo == 0, across, mine)], axis=1)
        table = one_hot_table(moved[:, lanes:].astype(jnp.int32), expert_count, capacity)
        outgoing = jnp.dot(table, tokens, preferred_element_type=F32).astype(BF)
        outgoing = outgoing.reshape(expert_count, capacity, chip)
        part = lax.all_to_all(outgoing, "expert", split_axis=0, concat_axis=0, tiled=True)

        gate = gate_saved[0, 0].astype(F32)
        upper = up_saved[0, 0].astype(F32)
        weight_rows = combine[0, 0][:, None]
        sigma = jax.nn.sigmoid(gate)
        active = gate * sigma
        combine_wide = jnp.broadcast_to(weight_rows, (rows, 128))
        scaled = (weight_rows * (active * upper)).astype(BF)
        w_moved = lax.ppermute(w_down[0], "core", swap)

        held_own = dp == core
        share = rows // (ny * 4)
        blk = (y * 2 + xlo) * 2 + core
        combine_share = lax.dynamic_slice_in_dim(combine[0, 0], blk * share, share, 0)
        combine_share, combine_wide, scaled = lax.optimization_barrier((combine_share, combine_wide, scaled))
        s_a = lax.ppermute(scaled, ("core", "dp"), scaled_a)
        s_b = lax.ppermute(scaled, ("core", "dp"), scaled_b)
        turn = jnp.where(core == 0, -1, 1)
        shift_here = jnp.where(dp == 0, shift(0), shift(1))
        order = []
        for step in range(1, half_y):
            order += [step, -step]
        order += [0, half_y]
        partner = [order.index(-o) if abs(o) < half_y else order.index(o) for o in order]
        spots = [(y + turn * o + 2 * ny - shift_here) % ny for o in order]
        index = jnp.stack(spots + [held_own.astype(jnp.int32), core]).astype(jnp.int32)
        on_a = lambda v: lax.ppermute(v, ("y", "core"), ring_a)
        on_b = lambda v: lax.ppermute(v, ("y", "core"), ring_b)
        block = part.reshape(rows, chip)
        block, s_a, s_b = lax.optimization_barrier((block, s_a, s_b))
        a = on_a(block)
        args = (w_down[0].reshape(ny, chip, width), w_moved.reshape(ny, chip, width), s_a, s_b)
        held = use([block], index, ny - 2, *args, None)
        block_b, acc = lax.optimization_barrier((block, held[0]))
        held = (acc, *held[1:])
        b = on_b(block_b)
        a_next = on_a(a)
        for step in range(1, half_y):
            blocks = [a, b]
            a = a_next
            if step < half_y - 1:
                b = on_b(b)
            held = use(blocks, index, 2 * (step - 1), *args, held)
            if step < half_y - 1:
                a, acc = lax.optimization_barrier((a, held[0]))
                held = (acc, *held[1:])
                a_next = on_a(a)
        acc, mine, theirs, sum_a, sum_b, mix = use([a], index, ny - 1, *args, held, last=True)

        got_a = lax.ppermute(sum_a, ("core", "dp"), sums_a)
        got_b = lax.ppermute(sum_b, ("core", "dp"), sums_b)
        members = 2 * ny * 4
        mix = lax.all_to_all(mix.reshape(members, share), ("dp", "y", "xlo", "core"), 0, 0, tiled=True)
        late = lax.ppermute(theirs, "core", swap)
        grad_weight = place(index, partner, mine, late).reshape(ny * chip, width)
        grad_gate, grad_upper = finish(index, acc, got_a, got_b, gate_saved[0, 0], up_saved[0, 0], combine_wide)
        mix, grad_gate, grad_upper, grad_weight = lax.optimization_barrier((mix, grad_gate, grad_upper, grad_weight))
        mix = jnp.sum(mix, axis=0)
        mix = mix / combine_share
        return grad_gate[None, None], grad_upper[None, None], grad_weight[None], mix[None, None]

    return local


def solution(mesh):
    ne, nb, nd = mesh.devices.shape
    fine = Mesh(mesh.devices.reshape(ne, nb // 4, 2, 2, nd), ("expert", "y", "xlo", "core", "dp"))
    blk = ("y", "xlo", "core")
    return jax.shard_map(
        make_local(nb // 4),
        mesh=fine,
        in_specs=(
            P("dp", "expert", blk),
            P("dp", "expert", None),
            P("dp", "expert", None),
            P("dp", "expert", None, blk),
            P("dp", "expert", None, blk),
            P("expert", "dp", blk),
        ),
        out_specs=(
            P("dp", "expert", None, blk),
            P("dp", "expert", None, blk),
            P("expert", "dp", blk),
            P("dp", "expert", blk),
        ),
        check_vma=False,
    )
```

```python
import functools

import jax
import jax.numpy as jnp
from jax import lax
from jax.experimental import pallas as pl
from jax.experimental.pallas import tpu as pltpu
from jax.sharding import Mesh, PartitionSpec as P

BF = jnp.bfloat16
F32 = jnp.float32
VMEM_LIMIT = 24 * 1024 * 1024


def one_hot_table(ids, expert_count, capacity):
    experts = jnp.arange(expert_count, dtype=jnp.int32)
    chosen = (ids[:, :, None] == experts).astype(F32)
    per_token = jnp.sum(chosen, axis=1)
    count = ids.shape[0]
    before = (jnp.arange(count)[:, None] > jnp.arange(count)[None, :]).astype(BF)
    earlier = jnp.dot(before, per_token.astype(BF), preferred_element_type=F32)
    position = jnp.sum(chosen * earlier[:, None, :], axis=-1).astype(jnp.int32)
    target = ids * capacity + position
    columns = jnp.arange(expert_count * capacity, dtype=jnp.int32)
    hit = (target[:, 0][None, :] == columns[:, None]) | (target[:, 1][None, :] == columns[:, None])
    return hit.astype(BF)


def use_kernel(blocks, first, last, index, *refs):
    it = iter(refs)
    x_refs = [next(it) for _ in range(blocks)]
    w_mine = [next(it) for _ in range(blocks)]
    w_theirs = [next(it) for _ in range(blocks)]
    s_a, s_b = next(it), next(it)
    acc_in = None
    if not first:
        acc_in, _, _ = next(it), next(it), next(it)
    acc, g_mine, g_theirs = next(it), next(it), next(it)
    width = s_a.shape[1]
    flags = index.shape[0] - 2
    own = index[flags] == 1
    s_mine = jnp.where(own, s_a[...], s_b[...])
    s_theirs = jnp.where(own, s_b[...], s_a[...])
    s = jnp.concatenate([s_mine, s_theirs], axis=1)
    for b in range(blocks):
        x = x_refs[b][...]
        w = jnp.concatenate([w_mine[b][0], w_theirs[b][0]], axis=1)
        product = jnp.dot(x, w, preferred_element_type=F32)
        if last:
            total = product + acc_in[...]
        elif b == 0:
            acc[...] = product if first else product + acc_in[...]
        else:
            acc[...] += product
        outer = lax.dot_general(x, s, (((0,), (0,)), ((), ())), preferred_element_type=F32)
        g_mine[b] = outer[:, :width].astype(BF)
        g_theirs[b] = outer[:, width:].astype(BF)
    if last:
        sum_a, sum_b, mix = next(it), next(it), next(it)
        mine, theirs = total[:, :width], total[:, width:]
        acc[...] = mine
        sum_b[...] = theirs.astype(BF)
        sum_a[...] = jnp.where(own, theirs, mine).astype(BF)
        terms = s_mine.astype(F32) * mine + s_theirs.astype(F32) * theirs
        line = lax.dot_general(
            jnp.ones((8, width), F32),
            terms,
            (((1,), (1,)), ((), ())),
            precision=lax.Precision.HIGHEST,
            preferred_element_type=F32,
        )
        row = lax.broadcasted_iota(jnp.int32, (2, line.shape[1]), 0)
        mix[...] = jnp.where(row == index[flags + 1], line[:2], 0.0)


def use(pieces, index, start, w_mine, w_theirs, s_a, s_b, held, last=False):
    first = held is None
    blocks = len(pieces)
    rows, width = s_a.shape
    total, chip, _ = w_mine.shape
    assert start % blocks == 0

    def whole(a):
        return pl.BlockSpec(a.shape, lambda i, idx: (0,) * len(a.shape))

    def pick(j):
        return pl.BlockSpec((1, chip, width), lambda i, idx: (idx[start + j], 0, 0))

    ins = list(pieces) + [w_mine] * blocks + [w_theirs] * blocks + [s_a, s_b]
    specs = [whole(a) for a in pieces] + [pick(j) for j in range(blocks)] * 2 + [whole(s_a), whole(s_b)]
    aliases = {}
    if not first:
        n = 1 + len(ins)
        aliases = {n + 1: 1, n + 2: 2} if last else {n: 0, n + 1: 1, n + 2: 2}
        ins += list(held)
        specs += [whole(held[0]), pl.BlockSpec(memory_space=pl.ANY), pl.BlockSpec(memory_space=pl.ANY)]
    slot = pl.BlockSpec((blocks, chip, width), lambda i, idx: (start // blocks, 0, 0))
    sums = (rows, width if last else 2 * width)
    outs = [pltpu.HBM(sums, F32) if last else jax.ShapeDtypeStruct(sums, F32)]
    outs += [pltpu.HBM((total, chip, width), BF)] * 2
    extra = []
    if last:
        extra = [jax.ShapeDtypeStruct((rows, width), BF)] * 2 + [jax.ShapeDtypeStruct((2, rows), F32)]
    return pl.pallas_call(
        functools.partial(use_kernel, blocks, first, last),
        grid_spec=pltpu.PrefetchScalarGridSpec(
            num_scalar_prefetch=1,
            grid=(1,),
            in_specs=specs,
            out_specs=[pl.BlockSpec(sums, lambda i, idx: (0, 0)), slot, slot] + [whole(o) for o in extra],
        ),
        out_shape=outs + extra,
        input_output_aliases=aliases,
        compiler_params=pltpu.CompilerParams(vmem_limit_bytes=VMEM_LIMIT),
        cost_estimate=pl.CostEstimate(
            flops=8 * blocks * rows * chip * width, bytes_accessed=blocks * 4000000, transcendentals=0
        ),
    )(index, *ins)


def place_kernel(partner, index, mine, theirs, out):
    for i, p in enumerate(partner):
        out[index[i]] = (mine[i].astype(F32) + theirs[p].astype(F32)).astype(BF)


def place(index, partner, mine, theirs):
    def whole(a):
        return pl.BlockSpec(a.shape, lambda i, idx: (0, 0, 0))

    return pl.pallas_call(
        functools.partial(place_kernel, tuple(partner)),
        grid_spec=pltpu.PrefetchScalarGridSpec(
            num_scalar_prefetch=1,
            grid=(1,),
            in_specs=[whole(mine), whole(theirs)],
            out_specs=whole(mine),
        ),
        out_shape=jax.ShapeDtypeStruct(mine.shape, BF),
        compiler_params=pltpu.CompilerParams(vmem_limit_bytes=16 * 1024 * 1024),
        cost_estimate=pl.CostEstimate(flops=1000000, bytes_accessed=5000000, transcendentals=0),
    )(index, mine, theirs)


def finish_kernel(index, own, got_a, got_b, gate_ref, up_ref, combine_ref, out_gate, out_up):
    flags = index.shape[0] - 2
    total = jnp.where(index[flags] == 1, own[...], got_b[...].astype(F32)) + got_a[...].astype(F32)
    gate = gate_ref[...].astype(F32)
    sigma = jax.nn.sigmoid(gate)
    scale = combine_ref[...]
    weighted = jnp.concatenate([scale] * (gate.shape[1] // scale.shape[1]), axis=1) * total
    out_gate[...] = (weighted * up_ref[...].astype(F32) * sigma * (1.0 + gate * (1.0 - sigma))).astype(BF)
    out_up[...] = (weighted * (gate * sigma)).astype(BF)


def finish(index, own, got_a, got_b, gate, up, combine_wide):
    in_hbm = lambda a: pltpu.with_memory_space_constraint(a, pltpu.HBM)
    ins = (in_hbm(own), got_a, got_b, in_hbm(gate), in_hbm(up), in_hbm(combine_wide))

    def whole(a):
        return pl.BlockSpec(a.shape, lambda i, idx: (0, 0))

    return pl.pallas_call(
        finish_kernel,
        grid_spec=pltpu.PrefetchScalarGridSpec(
            num_scalar_prefetch=1,
            grid=(1,),
            in_specs=[whole(a) for a in ins],
            out_specs=[whole(gate), whole(up)],
        ),
        out_shape=[pltpu.HBM(gate.shape, BF)] * 2,
        compiler_params=pltpu.CompilerParams(vmem_limit_bytes=16 * 1024 * 1024),
        cost_estimate=pl.CostEstimate(flops=3000000, bytes_accessed=3500000, transcendentals=200000),
    )(index, *ins)


def make_local(ny):
    half_y = ny // 2
    swap = [(0, 1), (1, 0)]

    def flat4(y, x, c, d):
        return ((y * 2 + x) * 2 + c) * 2 + d

    def shift(h):
        return (4 * h - 2) % ny

    def token_moves(cross):
        pairs = []
        for y in range(ny):
            for x in range(2):
                for c in range(2):
                    for d in range(2):
                        to_y = ((y % half_y) * 2 + x + shift(y // half_y)) % ny
                        to_x = 1 - c if cross else c
                        pairs.append((flat4(y, x, c, d), flat4(to_y, to_x, d, y // half_y)))
        return pairs

    def flat2(c, d):
        return c * 2 + d

    scaled_a = [(flat2(c, k), flat2(k, c)) for c in range(2) for k in range(2)]
    scaled_b = [(flat2(c, k), flat2(k, 1 - c)) for c in range(2) for k in range(2)]
    sums_a = [(flat2(1 - g, g), flat2(1 - g, 1 - g)) for g in range(2)] + [
        (flat2(g, g), flat2(1 - g, g)) for g in range(2)
    ]
    sums_b = [(flat2(1 - g, g), flat2(g, 1 - g)) for g in range(2)]
    ring_a = [(y * 2 + c, ((y + 1 - 2 * c) % ny) * 2 + c) for y in range(ny) for c in range(2)]
    ring_b = [(y * 2 + c, ((y - 1 + 2 * c) % ny) * 2 + c) for y in range(ny) for c in range(2)]

    def local(cotangent, expert_ids, combine, gate_saved, up_saved, w_down):
        expert_count = lax.axis_size("expert")
        y = lax.axis_index("y")
        core = lax.axis_index("core")
        xlo = lax.axis_index("xlo")
        dp = lax.axis_index("dp")
        rows = gate_saved.shape[2]
        width = gate_saved.shape[3]
        capacity = rows // expert_count
        lanes = cotangent.shape[2]
        chip = 2 * lanes
        every = ("y", "xlo", "core", "dp")

        ids = expert_ids[0].astype(BF)
        moved = lax.ppermute(jnp.concatenate([cotangent[0], ids], axis=1), every, token_moves(False))
        across = lax.ppermute(cotangent[0], every, token_moves(True))
        mine = moved[:, :lanes]
        tokens = jnp.concatenate([jnp.where(xlo == 0, mine, across), jnp.where(xlo == 0, across, mine)], axis=1)
        table = one_hot_table(moved[:, lanes:].astype(jnp.int32), expert_count, capacity)
        outgoing = jnp.dot(table, tokens, preferred_element_type=F32).astype(BF)
        outgoing = outgoing.reshape(expert_count, capacity, chip)
        part = lax.all_to_all(outgoing, "expert", split_axis=0, concat_axis=0, tiled=True)

        gate = gate_saved[0, 0].astype(F32)
        upper = up_saved[0, 0].astype(F32)
        weight_rows = combine[0, 0][:, None]
        sigma = jax.nn.sigmoid(gate)
        active = gate * sigma
        combine_wide = jnp.broadcast_to(weight_rows, (rows, 128))
        scaled = (weight_rows * (active * upper)).astype(BF)
        w_moved = lax.ppermute(w_down[0], "core", swap)

        held_own = dp == core
        share = rows // (ny * 4)
        blk = (y * 2 + xlo) * 2 + core
        combine_share = lax.dynamic_slice_in_dim(combine[0, 0], blk * share, share, 0)
        combine_share, scaled = lax.optimization_barrier((combine_share, scaled))
        s_a = lax.ppermute(scaled, ("core", "dp"), scaled_a)
        s_b = lax.ppermute(scaled, ("core", "dp"), scaled_b)
        turn = jnp.where(core == 0, -1, 1)
        shift_here = jnp.where(dp == 0, shift(0), shift(1))
        order = []
        for step in range(1, half_y):
            order += [step, -step]
        order += [0, half_y]
        partner = [order.index(-o) if abs(o) < half_y else order.index(o) for o in order]
        spots = [(y + turn * o + 2 * ny - shift_here) % ny for o in order]
        index = jnp.stack(spots + [held_own.astype(jnp.int32), core]).astype(jnp.int32)
        on_a = lambda v: lax.ppermute(v, ("y", "core"), ring_a)
        on_b = lambda v: lax.ppermute(v, ("y", "core"), ring_b)
        block = part.reshape(rows, chip)
        block, s_a, s_b = lax.optimization_barrier((block, s_a, s_b))
        a = on_a(block)
        args = (w_down[0].reshape(ny, chip, width), w_moved.reshape(ny, chip, width), s_a, s_b)
        held = use([block], index, ny - 2, *args, None)
        block_b, acc = lax.optimization_barrier((block, held[0]))
        held = (acc, *held[1:])
        b = on_b(block_b)
        a_next = on_a(a)
        for step in range(1, half_y):
            blocks = [a, b]
            a = a_next
            if step < half_y - 1:
                b = on_b(b)
            held = use(blocks, index, 2 * (step - 1), *args, held)
            if step < half_y - 1:
                a, acc = lax.optimization_barrier((a, held[0]))
                held = (acc, *held[1:])
                a_next = on_a(a)
        acc, combine_wide = lax.optimization_barrier((held[0], combine_wide))
        held = (acc, *held[1:])
        acc, mine, theirs, sum_a, sum_b, mix = use([a], index, ny - 1, *args, held, last=True)

        got_a = lax.ppermute(sum_a, ("core", "dp"), sums_a)
        got_b = lax.ppermute(sum_b, ("core", "dp"), sums_b)
        members = 2 * ny * 4
        mix = lax.all_to_all(mix.reshape(members, share), ("dp", "y", "xlo", "core"), 0, 0, tiled=True)
        late = lax.ppermute(theirs, "core", swap)
        grad_weight = place(index, partner, mine, late).reshape(ny * chip, width)
        grad_gate, grad_upper = finish(index, acc, got_a, got_b, gate_saved[0, 0], up_saved[0, 0], combine_wide)
        mix, grad_gate, grad_upper, grad_weight = lax.optimization_barrier((mix, grad_gate, grad_upper, grad_weight))
        mix = jnp.sum(mix, axis=0)
        mix = mix / combine_share
        return grad_gate[None, None], grad_upper[None, None], grad_weight[None], mix[None, None]

    return local


def solution(mesh):
    ne, nb, nd = mesh.devices.shape
    fine = Mesh(mesh.devices.reshape(ne, nb // 4, 2, 2, nd), ("expert", "y", "xlo", "core", "dp"))
    blk = ("y", "xlo", "core")
    return jax.shard_map(
        make_local(nb // 4),
        mesh=fine,
        in_specs=(
            P("dp", "expert", blk),
            P("dp", "expert", None),
            P("dp", "expert", None),
            P("dp", "expert", None, blk),
            P("dp", "expert", None, blk),
            P("expert", "dp", blk),
        ),
        out_specs=(
            P("dp", "expert", None, blk),
            P("dp", "expert", None, blk),
            P("expert", "dp", blk),
            P("dp", "expert", blk),
        ),
        check_vma=False,
    )
```

```python
import functools

import jax
import jax.numpy as jnp
from jax import lax
from jax.experimental import pallas as pl
from jax.experimental.pallas import tpu as pltpu
from jax.sharding import Mesh, PartitionSpec as P

BF = jnp.bfloat16
F32 = jnp.float32
VMEM_LIMIT = 24 * 1024 * 1024


def one_hot_table(ids, expert_count, capacity):
    experts = jnp.arange(expert_count, dtype=jnp.int32)
    chosen = (ids[:, :, None] == experts).astype(F32)
    per_token = jnp.sum(chosen, axis=1)
    count = ids.shape[0]
    before = (jnp.arange(count)[:, None] > jnp.arange(count)[None, :]).astype(BF)
    earlier = jnp.dot(before, per_token.astype(BF), preferred_element_type=F32)
    position = jnp.sum(chosen * earlier[:, None, :], axis=-1).astype(jnp.int32)
    target = ids * capacity + position
    columns = jnp.arange(expert_count * capacity, dtype=jnp.int32)
    hit = (target[:, 0][None, :] == columns[:, None]) | (target[:, 1][None, :] == columns[:, None])
    return hit.astype(BF)


def use_kernel(blocks, first, last, carries, index, *refs):
    it = iter(refs)
    x_refs = [next(it) for _ in range(blocks)]
    w_mine = [next(it) for _ in range(blocks)]
    w_theirs = [next(it) for _ in range(blocks)]
    s_a, s_b = next(it), next(it)
    acc_in = None
    if not first:
        acc_in, _ = next(it), next(it)
    carry_refs = [next(it) for _ in carries]
    carried = sum(carries)
    acc, g_mine, g_theirs = next(it), next(it), next(it)
    width = s_a.shape[1]
    flags = index.shape[0] - 2
    own = index[flags] == 1
    s_mine = jnp.where(own, s_a[...], s_b[...])
    s_theirs = jnp.where(own, s_b[...], s_a[...])
    s = jnp.concatenate([s_mine, s_theirs], axis=1)
    for b in range(blocks):
        x = x_refs[b][...]
        w = jnp.concatenate([w_mine[b][0], w_theirs[b][0]], axis=1)
        product = jnp.dot(x, w, preferred_element_type=F32)
        if last:
            total = product + acc_in[...]
        elif b == 0:
            acc[...] = product if first else product + acc_in[...]
        else:
            acc[...] += product
        outer = lax.dot_general(x, s, (((0,), (0,)), ((), ())), preferred_element_type=F32)
        g_mine[b] = outer[:, :width].astype(BF)
        g_theirs[carried + b] = outer[:, width:].astype(BF)
    at = 0
    for ref, n in zip(carry_refs, carries):
        g_theirs[at : at + n] = ref[...]
        at += n
    if last:
        sum_a, sum_b, mix = next(it), next(it), next(it)
        mine, theirs = total[:, :width], total[:, width:]
        acc[...] = mine
        sum_b[...] = theirs.astype(BF)
        sum_a[...] = jnp.where(own, theirs, mine).astype(BF)
        terms = s_mine.astype(F32) * mine + s_theirs.astype(F32) * theirs
        line = lax.dot_general(
            jnp.ones((8, width), F32),
            terms,
            (((1,), (1,)), ((), ())),
            precision=lax.Precision.HIGHEST,
            preferred_element_type=F32,
        )
        row = lax.broadcasted_iota(jnp.int32, (2, line.shape[1]), 0)
        mix[...] = jnp.where(row == index[flags + 1], line[:2], 0.0)


def use(pieces, index, start, w_mine, w_theirs, s_a, s_b, held, last=False, carry=()):
    first = held is None
    blocks = len(pieces)
    rows, width = s_a.shape
    total, chip, _ = w_mine.shape
    assert start % blocks == 0

    def whole(a):
        return pl.BlockSpec(a.shape, lambda i, idx: (0,) * len(a.shape))

    def pick(j):
        return pl.BlockSpec((1, chip, width), lambda i, idx: (idx[start + j], 0, 0))

    ins = list(pieces) + [w_mine] * blocks + [w_theirs] * blocks + [s_a, s_b]
    specs = [whole(a) for a in pieces] + [pick(j) for j in range(blocks)] * 2 + [whole(s_a), whole(s_b)]
    aliases = {}
    if not first:
        n = 1 + len(ins)
        aliases = {n + 1: 1} if last else {n: 0, n + 1: 1}
        ins += list(held)
        specs += [whole(held[0]), pl.BlockSpec(memory_space=pl.ANY)]
    carries = tuple(c.shape[0] for c in carry)
    ins += list(carry)
    specs += [whole(c) for c in carry]
    slot = pl.BlockSpec((blocks, chip, width), lambda i, idx: (start // blocks, 0, 0))
    sums = (rows, width if last else 2 * width)
    outs = [pltpu.HBM(sums, F32) if last else jax.ShapeDtypeStruct(sums, F32)]
    sent = (sum(carries) + blocks, chip, width)
    outs += [pltpu.HBM((total, chip, width), BF), jax.ShapeDtypeStruct(sent, BF)]
    extra = []
    if last:
        extra = [jax.ShapeDtypeStruct((rows, width), BF)] * 2 + [jax.ShapeDtypeStruct((2, rows), F32)]
    return pl.pallas_call(
        functools.partial(use_kernel, blocks, first, last, carries),
        grid_spec=pltpu.PrefetchScalarGridSpec(
            num_scalar_prefetch=1,
            grid=(1,),
            in_specs=specs,
            out_specs=[pl.BlockSpec(sums, lambda i, idx: (0, 0)), slot, pl.BlockSpec(sent, lambda i, idx: (0, 0, 0))] + [whole(o) for o in extra],
        ),
        out_shape=outs + extra,
        input_output_aliases=aliases,
        compiler_params=pltpu.CompilerParams(vmem_limit_bytes=VMEM_LIMIT),
        cost_estimate=pl.CostEstimate(
            flops=8 * blocks * rows * chip * width, bytes_accessed=blocks * 4000000, transcendentals=0
        ),
    )(index, *ins)


def place_kernel(partner, index, mine, *refs):
    theirs, out = refs[:-1], refs[-1]
    for i, (a, j) in enumerate(partner):
        out[index[i]] = (mine[i].astype(F32) + theirs[a][j].astype(F32)).astype(BF)


def place(index, partner, mine, theirs):
    def whole(a):
        return pl.BlockSpec(a.shape, lambda i, idx: (0, 0, 0))

    return pl.pallas_call(
        functools.partial(place_kernel, tuple(partner)),
        grid_spec=pltpu.PrefetchScalarGridSpec(
            num_scalar_prefetch=1,
            grid=(1,),
            in_specs=[whole(mine)] + [whole(t) for t in theirs],
            out_specs=whole(mine),
        ),
        out_shape=jax.ShapeDtypeStruct(mine.shape, BF),
        compiler_params=pltpu.CompilerParams(vmem_limit_bytes=16 * 1024 * 1024),
        cost_estimate=pl.CostEstimate(flops=1000000, bytes_accessed=5000000, transcendentals=0),
    )(index, mine, *theirs)


def finish_kernel(index, own, got_a, got_b, gate_ref, up_ref, combine_ref, out_gate, out_up):
    flags = index.shape[0] - 2
    total = jnp.where(index[flags] == 1, own[...], got_b[...].astype(F32)) + got_a[...].astype(F32)
    gate = gate_ref[...].astype(F32)
    sigma = jax.nn.sigmoid(gate)
    scale = combine_ref[...]
    weighted = jnp.concatenate([scale] * (gate.shape[1] // scale.shape[1]), axis=1) * total
    out_gate[...] = (weighted * up_ref[...].astype(F32) * sigma * (1.0 + gate * (1.0 - sigma))).astype(BF)
    out_up[...] = (weighted * (gate * sigma)).astype(BF)


def finish(index, own, got_a, got_b, gate, up, combine_wide):
    in_hbm = lambda a: pltpu.with_memory_space_constraint(a, pltpu.HBM)
    ins = (in_hbm(own), got_a, got_b, in_hbm(gate), in_hbm(up), in_hbm(combine_wide))

    def whole(a):
        return pl.BlockSpec(a.shape, lambda i, idx: (0, 0))

    return pl.pallas_call(
        finish_kernel,
        grid_spec=pltpu.PrefetchScalarGridSpec(
            num_scalar_prefetch=1,
            grid=(1,),
            in_specs=[whole(a) for a in ins],
            out_specs=[whole(gate), whole(up)],
        ),
        out_shape=[pltpu.HBM(gate.shape, BF)] * 2,
        compiler_params=pltpu.CompilerParams(vmem_limit_bytes=16 * 1024 * 1024),
        cost_estimate=pl.CostEstimate(flops=3000000, bytes_accessed=3500000, transcendentals=200000),
    )(index, *ins)


def make_local(ny):
    half_y = ny // 2
    swap = [(0, 1), (1, 0)]

    def flat4(y, x, c, d):
        return ((y * 2 + x) * 2 + c) * 2 + d

    def shift(h):
        return (4 * h - 2) % ny

    def token_moves(cross):
        pairs = []
        for y in range(ny):
            for x in range(2):
                for c in range(2):
                    for d in range(2):
                        to_y = ((y % half_y) * 2 + x + shift(y // half_y)) % ny
                        to_x = 1 - c if cross else c
                        pairs.append((flat4(y, x, c, d), flat4(to_y, to_x, d, y // half_y)))
        return pairs

    def flat2(c, d):
        return c * 2 + d

    scaled_a = [(flat2(c, k), flat2(k, c)) for c in range(2) for k in range(2)]
    scaled_b = [(flat2(c, k), flat2(k, 1 - c)) for c in range(2) for k in range(2)]
    sums_a = [(flat2(1 - g, g), flat2(1 - g, 1 - g)) for g in range(2)] + [
        (flat2(g, g), flat2(1 - g, g)) for g in range(2)
    ]
    sums_b = [(flat2(1 - g, g), flat2(g, 1 - g)) for g in range(2)]
    ring_a = [(y * 2 + c, ((y + 1 - 2 * c) % ny) * 2 + c) for y in range(ny) for c in range(2)]
    ring_b = [(y * 2 + c, ((y - 1 + 2 * c) % ny) * 2 + c) for y in range(ny) for c in range(2)]

    def local(cotangent, expert_ids, combine, gate_saved, up_saved, w_down):
        expert_count = lax.axis_size("expert")
        y = lax.axis_index("y")
        core = lax.axis_index("core")
        xlo = lax.axis_index("xlo")
        dp = lax.axis_index("dp")
        rows = gate_saved.shape[2]
        width = gate_saved.shape[3]
        capacity = rows // expert_count
        lanes = cotangent.shape[2]
        chip = 2 * lanes
        every = ("y", "xlo", "core", "dp")

        ids = expert_ids[0].astype(BF)
        moved = lax.ppermute(jnp.concatenate([cotangent[0], ids], axis=1), every, token_moves(False))
        across = lax.ppermute(cotangent[0], every, token_moves(True))
        mine = moved[:, :lanes]
        tokens = jnp.concatenate([jnp.where(xlo == 0, mine, across), jnp.where(xlo == 0, across, mine)], axis=1)
        table = one_hot_table(moved[:, lanes:].astype(jnp.int32), expert_count, capacity)
        outgoing = jnp.dot(table, tokens, preferred_element_type=F32).astype(BF)
        outgoing = outgoing.reshape(expert_count, capacity, chip)
        part = lax.all_to_all(outgoing, "expert", split_axis=0, concat_axis=0, tiled=True)

        gate = gate_saved[0, 0].astype(F32)
        upper = up_saved[0, 0].astype(F32)
        weight_rows = combine[0, 0][:, None]
        sigma = jax.nn.sigmoid(gate)
        active = gate * sigma
        combine_wide = jnp.broadcast_to(weight_rows, (rows, 128))
        scaled = (weight_rows * (active * upper)).astype(BF)
        w_moved = lax.ppermute(w_down[0], "core", swap)

        held_own = dp == core
        share = rows // (ny * 4)
        blk = (y * 2 + xlo) * 2 + core
        combine_share = lax.dynamic_slice_in_dim(combine[0, 0], blk * share, share, 0)
        combine_share, scaled = lax.optimization_barrier((combine_share, scaled))
        s_a = lax.ppermute(scaled, ("core", "dp"), scaled_a)
        s_b = lax.ppermute(scaled, ("core", "dp"), scaled_b)
        turn = jnp.where(core == 0, -1, 1)
        shift_here = jnp.where(dp == 0, shift(0), shift(1))
        order = []
        for step in range(1, half_y):
            order += [step, -step]
        order += [0, half_y]
        slots = [order.index(-o) if abs(o) < half_y else order.index(o) for o in order]
        late_slots = [ny - 2, ny - 4, ny - 3, ny - 1]
        partner = [
            (half_y - 2, late_slots.index(p)) if p in late_slots else (p // 2, p % 2) for p in slots
        ]
        spots = [(y + turn * o + 2 * ny - shift_here) % ny for o in order]
        index = jnp.stack(spots + [held_own.astype(jnp.int32), core]).astype(jnp.int32)
        on_a = lambda v: lax.ppermute(v, ("y", "core"), ring_a)
        on_b = lambda v: lax.ppermute(v, ("y", "core"), ring_b)
        block = part.reshape(rows, chip)
        block, s_a, s_b = lax.optimization_barrier((block, s_a, s_b))
        a = on_a(block)
        args = (w_down[0].reshape(ny, chip, width), w_moved.reshape(ny, chip, width), s_a, s_b)
        acc, mine, own_part = use([block], index, ny - 2, *args, None)
        block_b, acc = lax.optimization_barrier((block, acc))
        b = on_b(block_b)
        a_next = on_a(a)
        swapped = []
        for step in range(1, half_y):
            blocks = [a, b]
            a = a_next
            if step < half_y - 1:
                b = on_b(b)
            acc, mine, theirs = use(blocks, index, 2 * (step - 1), *args, (acc, mine))
            if step < half_y - 1:
                got = lax.ppermute(theirs, "core", swap)
                a, acc, got = lax.optimization_barrier((a, acc, got))
                swapped.append(got)
                a_next = on_a(a)
        acc, combine_wide = lax.optimization_barrier((acc, combine_wide))
        acc, mine, theirs, sum_a, sum_b, mix = use(
            [a], index, ny - 1, *args, (acc, mine), last=True, carry=(own_part, theirs)
        )

        got_a = lax.ppermute(sum_a, ("core", "dp"), sums_a)
        got_b = lax.ppermute(sum_b, ("core", "dp"), sums_b)
        members = 2 * ny * 4
        mix = lax.all_to_all(mix.reshape(members, share), ("dp", "y", "xlo", "core"), 0, 0, tiled=True)
        late = lax.ppermute(theirs, "core", swap)
        grad_weight = place(index, partner, mine, (*swapped, late)).reshape(ny * chip, width)
        grad_gate, grad_upper = finish(index, acc, got_a, got_b, gate_saved[0, 0], up_saved[0, 0], combine_wide)
        mix, grad_gate, grad_upper, grad_weight = lax.optimization_barrier((mix, grad_gate, grad_upper, grad_weight))
        mix = jnp.sum(mix, axis=0)
        mix = mix / combine_share
        return grad_gate[None, None], grad_upper[None, None], grad_weight[None], mix[None, None]

    return local


def solution(mesh):
    ne, nb, nd = mesh.devices.shape
    fine = Mesh(mesh.devices.reshape(ne, nb // 4, 2, 2, nd), ("expert", "y", "xlo", "core", "dp"))
    blk = ("y", "xlo", "core")
    return jax.shard_map(
        make_local(nb // 4),
        mesh=fine,
        in_specs=(
            P("dp", "expert", blk),
            P("dp", "expert", None),
            P("dp", "expert", None),
            P("dp", "expert", None, blk),
            P("dp", "expert", None, blk),
            P("expert", "dp", blk),
        ),
        out_specs=(
            P("dp", "expert", None, blk),
            P("dp", "expert", None, blk),
            P("expert", "dp", blk),
            P("dp", "expert", blk),
        ),
        check_vma=False,
    )
```

```python
import functools

import jax
import jax.numpy as jnp
from jax import lax
from jax.experimental import pallas as pl
from jax.experimental.pallas import tpu as pltpu
from jax.sharding import Mesh, PartitionSpec as P

BF = jnp.bfloat16
F32 = jnp.float32
VMEM_LIMIT = 24 * 1024 * 1024


def one_hot_table(ids, expert_count, capacity):
    experts = jnp.arange(expert_count, dtype=jnp.int32)
    chosen = (ids[:, :, None] == experts).astype(F32)
    per_token = jnp.sum(chosen, axis=1)
    count = ids.shape[0]
    before = (jnp.arange(count)[:, None] > jnp.arange(count)[None, :]).astype(BF)
    earlier = jnp.dot(before, per_token.astype(BF), preferred_element_type=F32)
    position = jnp.sum(chosen * earlier[:, None, :], axis=-1).astype(jnp.int32)
    target = ids * capacity + position
    columns = jnp.arange(expert_count * capacity, dtype=jnp.int32)
    hit = (target[:, 0][None, :] == columns[:, None]) | (target[:, 1][None, :] == columns[:, None])
    return hit.astype(BF)


def use_kernel(blocks, first, last, carries, index, *refs):
    it = iter(refs)
    x_refs = [next(it) for _ in range(blocks)]
    w_mine = [next(it) for _ in range(blocks)]
    w_theirs = [next(it) for _ in range(blocks)]
    s_a, s_b = next(it), next(it)
    acc_in = None
    if not first:
        acc_in, _ = next(it), next(it)
    carry_refs = [next(it) for _ in carries]
    carried = sum(carries)
    acc, g_mine, g_theirs = next(it), next(it), next(it)
    width = s_a.shape[1]
    flags = index.shape[0] - 2
    own = index[flags] == 1
    s_mine = jnp.where(own, s_a[...], s_b[...])
    s_theirs = jnp.where(own, s_b[...], s_a[...])
    s = jnp.concatenate([s_mine, s_theirs], axis=1)
    for b in range(blocks):
        x = x_refs[b][...]
        w = jnp.concatenate([w_mine[b][0], w_theirs[b][0]], axis=1)
        product = jnp.dot(x, w, preferred_element_type=F32)
        if last:
            total = product + acc_in[...]
        elif b == 0:
            acc[...] = product if first else product + acc_in[...]
        else:
            acc[...] += product
        outer = lax.dot_general(x, s, (((0,), (0,)), ((), ())), preferred_element_type=F32)
        g_mine[b] = outer[:, :width].astype(BF)
        g_theirs[carried + b] = outer[:, width:].astype(BF)
    at = 0
    for ref, n in zip(carry_refs, carries):
        g_theirs[at : at + n] = ref[...]
        at += n
    if last:
        sum_a, sum_b, mix = next(it), next(it), next(it)
        mine, theirs = total[:, :width], total[:, width:]
        acc[...] = mine
        sum_b[...] = theirs.astype(BF)
        sum_a[...] = jnp.where(own, theirs, mine).astype(BF)
        terms = s_mine.astype(F32) * mine + s_theirs.astype(F32) * theirs
        line = lax.dot_general(
            jnp.ones((8, width), F32),
            terms,
            (((1,), (1,)), ((), ())),
            precision=lax.Precision.HIGHEST,
            preferred_element_type=F32,
        )
        row = lax.broadcasted_iota(jnp.int32, (2, line.shape[1]), 0)
        mix[...] = jnp.where(row == index[flags + 1], line[:2], 0.0)


def use(pieces, index, start, w_mine, w_theirs, s_a, s_b, held, last=False, carry=()):
    first = held is None
    blocks = len(pieces)
    rows, width = s_a.shape
    total, chip, _ = w_mine.shape
    assert start % blocks == 0

    def whole(a):
        return pl.BlockSpec(a.shape, lambda i, idx: (0,) * len(a.shape))

    def pick(j):
        return pl.BlockSpec((1, chip, width), lambda i, idx: (idx[start + j], 0, 0))

    ins = list(pieces) + [w_mine] * blocks + [w_theirs] * blocks + [s_a, s_b]
    specs = [whole(a) for a in pieces] + [pick(j) for j in range(blocks)] * 2 + [whole(s_a), whole(s_b)]
    aliases = {}
    if not first:
        n = 1 + len(ins)
        aliases = {n + 1: 1} if last else {n: 0, n + 1: 1}
        ins += list(held)
        specs += [whole(held[0]), pl.BlockSpec(memory_space=pl.ANY)]
    carries = tuple(c.shape[0] for c in carry)
    ins += list(carry)
    specs += [whole(c) for c in carry]
    slot = pl.BlockSpec((blocks, chip, width), lambda i, idx: (start // blocks, 0, 0))
    sums = (rows, width if last else 2 * width)
    outs = [pltpu.HBM(sums, F32) if last else jax.ShapeDtypeStruct(sums, F32)]
    sent = (sum(carries) + blocks, chip, width)
    outs += [pltpu.HBM((total, chip, width), BF), jax.ShapeDtypeStruct(sent, BF)]
    extra = []
    if last:
        extra = [jax.ShapeDtypeStruct((rows, width), BF)] * 2 + [jax.ShapeDtypeStruct((2, rows), F32)]
    return pl.pallas_call(
        functools.partial(use_kernel, blocks, first, last, carries),
        grid_spec=pltpu.PrefetchScalarGridSpec(
            num_scalar_prefetch=1,
            grid=(1,),
            in_specs=specs,
            out_specs=[pl.BlockSpec(sums, lambda i, idx: (0, 0)), slot, pl.BlockSpec(sent, lambda i, idx: (0, 0, 0))] + [whole(o) for o in extra],
        ),
        out_shape=outs + extra,
        input_output_aliases=aliases,
        compiler_params=pltpu.CompilerParams(vmem_limit_bytes=VMEM_LIMIT),
        cost_estimate=pl.CostEstimate(
            flops=8 * blocks * rows * chip * width, bytes_accessed=blocks * 4000000, transcendentals=0
        ),
    )(index, *ins)


def place_kernel(partner, index, mine, *refs):
    theirs, out = refs[:-1], refs[-1]
    for i, (a, j) in enumerate(partner):
        out[index[i]] = (mine[i].astype(F32) + theirs[a][j].astype(F32)).astype(BF)


def place(index, partner, mine, theirs):
    def whole(a):
        return pl.BlockSpec(a.shape, lambda i, idx: (0, 0, 0))

    return pl.pallas_call(
        functools.partial(place_kernel, tuple(partner)),
        grid_spec=pltpu.PrefetchScalarGridSpec(
            num_scalar_prefetch=1,
            grid=(1,),
            in_specs=[whole(mine)] + [whole(t) for t in theirs],
            out_specs=whole(mine),
        ),
        out_shape=jax.ShapeDtypeStruct(mine.shape, BF),
        compiler_params=pltpu.CompilerParams(vmem_limit_bytes=16 * 1024 * 1024),
        cost_estimate=pl.CostEstimate(flops=1000000, bytes_accessed=5000000, transcendentals=0),
    )(index, mine, *theirs)


def finish_kernel(index, own, got_a, got_b, gate_ref, up_ref, combine_ref, out_gate, out_up):
    flags = index.shape[0] - 2
    total = jnp.where(index[flags] == 1, own[...], got_b[...].astype(F32)) + got_a[...].astype(F32)
    gate = gate_ref[...].astype(F32)
    sigma = jax.nn.sigmoid(gate)
    scale = combine_ref[...]
    weighted = jnp.concatenate([scale] * (gate.shape[1] // scale.shape[1]), axis=1) * total
    out_gate[...] = (weighted * up_ref[...].astype(F32) * sigma * (1.0 + gate * (1.0 - sigma))).astype(BF)
    out_up[...] = (weighted * (gate * sigma)).astype(BF)


def finish(index, own, got_a, got_b, gate, up, combine_wide):
    in_hbm = lambda a: pltpu.with_memory_space_constraint(a, pltpu.HBM)
    ins = (in_hbm(own), got_a, got_b, in_hbm(gate), in_hbm(up), in_hbm(combine_wide))

    def whole(a):
        return pl.BlockSpec(a.shape, lambda i, idx: (0, 0))

    return pl.pallas_call(
        finish_kernel,
        grid_spec=pltpu.PrefetchScalarGridSpec(
            num_scalar_prefetch=1,
            grid=(1,),
            in_specs=[whole(a) for a in ins],
            out_specs=[whole(gate), whole(up)],
        ),
        out_shape=[pltpu.HBM(gate.shape, BF)] * 2,
        compiler_params=pltpu.CompilerParams(vmem_limit_bytes=16 * 1024 * 1024),
        cost_estimate=pl.CostEstimate(flops=3000000, bytes_accessed=3500000, transcendentals=200000),
    )(index, *ins)


def make_local(ny):
    half_y = ny // 2
    swap = [(0, 1), (1, 0)]

    def flat4(y, x, c, d):
        return ((y * 2 + x) * 2 + c) * 2 + d

    def shift(h):
        return (4 * h - 2) % ny

    def token_moves(cross):
        pairs = []
        for y in range(ny):
            for x in range(2):
                for c in range(2):
                    for d in range(2):
                        to_y = ((y % half_y) * 2 + x + shift(y // half_y)) % ny
                        to_x = 1 - c if cross else c
                        pairs.append((flat4(y, x, c, d), flat4(to_y, to_x, d, y // half_y)))
        return pairs

    def flat2(c, d):
        return c * 2 + d

    scaled_a = [(flat2(c, k), flat2(k, c)) for c in range(2) for k in range(2)]
    scaled_b = [(flat2(c, k), flat2(k, 1 - c)) for c in range(2) for k in range(2)]
    sums_a = [(flat2(1 - g, g), flat2(1 - g, 1 - g)) for g in range(2)] + [
        (flat2(g, g), flat2(1 - g, g)) for g in range(2)
    ]
    sums_b = [(flat2(1 - g, g), flat2(g, 1 - g)) for g in range(2)]
    ring_a = [(y * 2 + c, ((y + 1 - 2 * c) % ny) * 2 + c) for y in range(ny) for c in range(2)]
    ring_b = [(y * 2 + c, ((y - 1 + 2 * c) % ny) * 2 + c) for y in range(ny) for c in range(2)]

    def local(cotangent, expert_ids, combine, gate_saved, up_saved, w_down):
        expert_count = lax.axis_size("expert")
        y = lax.axis_index("y")
        core = lax.axis_index("core")
        xlo = lax.axis_index("xlo")
        dp = lax.axis_index("dp")
        rows = gate_saved.shape[2]
        width = gate_saved.shape[3]
        capacity = rows // expert_count
        lanes = cotangent.shape[2]
        chip = 2 * lanes
        every = ("y", "xlo", "core", "dp")

        ids = expert_ids[0].astype(BF)
        moved = lax.ppermute(jnp.concatenate([cotangent[0], ids], axis=1), every, token_moves(False))
        across = lax.ppermute(cotangent[0], every, token_moves(True))
        mine = moved[:, :lanes]
        tokens = jnp.concatenate([jnp.where(xlo == 0, mine, across), jnp.where(xlo == 0, across, mine)], axis=1)
        table = one_hot_table(moved[:, lanes:].astype(jnp.int32), expert_count, capacity)
        outgoing = jnp.dot(table, tokens, preferred_element_type=F32).astype(BF)
        outgoing = outgoing.reshape(expert_count, capacity, chip)
        part = lax.all_to_all(outgoing, "expert", split_axis=0, concat_axis=0, tiled=True)

        gate = gate_saved[0, 0].astype(F32)
        upper = up_saved[0, 0].astype(F32)
        weight_rows = combine[0, 0][:, None]
        sigma = jax.nn.sigmoid(gate)
        active = gate * sigma
        combine_wide = jnp.broadcast_to(weight_rows, (rows, 128))
        scaled = (weight_rows * (active * upper)).astype(BF)
        w_moved = lax.ppermute(w_down[0], "core", swap)

        held_own = dp == core
        share = rows // (ny * 4)
        blk = (y * 2 + xlo) * 2 + core
        combine_share = lax.dynamic_slice_in_dim(combine[0, 0], blk * share, share, 0)
        combine_share, scaled = lax.optimization_barrier((combine_share, scaled))
        s_a = lax.ppermute(scaled, ("core", "dp"), scaled_a)
        s_b = lax.ppermute(scaled, ("core", "dp"), scaled_b)
        turn = jnp.where(core == 0, -1, 1)
        shift_here = jnp.where(dp == 0, shift(0), shift(1))
        order = []
        for step in range(1, half_y):
            order += [step, -step]
        order += [0, half_y]
        slots = [order.index(-o) if abs(o) < half_y else order.index(o) for o in order]
        late_slots = [ny - 2, ny - 4, ny - 3, ny - 1]
        partner = [
            (half_y - 2, late_slots.index(p)) if p in late_slots else (p // 2, p % 2) for p in slots
        ]
        spots = [(y + turn * o + 2 * ny - shift_here) % ny for o in order]
        index = jnp.stack(spots + [held_own.astype(jnp.int32), core]).astype(jnp.int32)
        on_a = lambda v: lax.ppermute(v, ("y", "core"), ring_a)
        on_b = lambda v: lax.ppermute(v, ("y", "core"), ring_b)
        block = part.reshape(rows, chip)
        block, s_a, s_b = lax.optimization_barrier((block, s_a, s_b))
        a = on_a(block)
        args = (w_down[0].reshape(ny, chip, width), w_moved.reshape(ny, chip, width), s_a, s_b)
        acc, mine, own_part = use([block], index, ny - 2, *args, None)
        block_b, acc = lax.optimization_barrier((block, acc))
        b = on_b(block_b)
        a_next = on_a(a)
        swapped = []
        for step in range(1, half_y):
            blocks = [a, b]
            a = a_next
            if step < half_y - 1:
                b = on_b(b)
            acc, mine, theirs = use(blocks, index, 2 * (step - 1), *args, (acc, mine))
            if step < half_y - 1:
                got = lax.ppermute(theirs, "core", swap)
                a, acc, *swapped = lax.optimization_barrier((a, acc, *swapped))
                swapped.append(got)
                a_next = on_a(a)
        acc, combine_wide, *swapped = lax.optimization_barrier((acc, combine_wide, *swapped))
        acc, mine, theirs, sum_a, sum_b, mix = use(
            [a], index, ny - 1, *args, (acc, mine), last=True, carry=(own_part, theirs)
        )

        got_a = lax.ppermute(sum_a, ("core", "dp"), sums_a)
        got_b = lax.ppermute(sum_b, ("core", "dp"), sums_b)
        members = 2 * ny * 4
        mix = lax.all_to_all(mix.reshape(members, share), ("dp", "y", "xlo", "core"), 0, 0, tiled=True)
        late = lax.ppermute(theirs, "core", swap)
        grad_weight = place(index, partner, mine, (*swapped, late)).reshape(ny * chip, width)
        grad_gate, grad_upper = finish(index, acc, got_a, got_b, gate_saved[0, 0], up_saved[0, 0], combine_wide)
        mix, grad_gate, grad_upper, grad_weight = lax.optimization_barrier((mix, grad_gate, grad_upper, grad_weight))
        mix = jnp.sum(mix, axis=0)
        mix = mix / combine_share
        return grad_gate[None, None], grad_upper[None, None], grad_weight[None], mix[None, None]

    return local


def solution(mesh):
    ne, nb, nd = mesh.devices.shape
    fine = Mesh(mesh.devices.reshape(ne, nb // 4, 2, 2, nd), ("expert", "y", "xlo", "core", "dp"))
    blk = ("y", "xlo", "core")
    return jax.shard_map(
        make_local(nb // 4),
        mesh=fine,
        in_specs=(
            P("dp", "expert", blk),
            P("dp", "expert", None),
            P("dp", "expert", None),
            P("dp", "expert", None, blk),
            P("dp", "expert", None, blk),
            P("expert", "dp", blk),
        ),
        out_specs=(
            P("dp", "expert", None, blk),
            P("dp", "expert", None, blk),
            P("expert", "dp", blk),
            P("dp", "expert", blk),
        ),
        check_vma=False,
    )
```

```python
import functools

import jax
import jax.numpy as jnp
from jax import lax
from jax.experimental import pallas as pl
from jax.experimental.pallas import tpu as pltpu
from jax.sharding import Mesh, PartitionSpec as P

BF = jnp.bfloat16
F32 = jnp.float32
VMEM_LIMIT = 24 * 1024 * 1024


def one_hot_table(ids, expert_count, capacity):
    experts = jnp.arange(expert_count, dtype=jnp.int32)
    chosen = (ids[:, :, None] == experts).astype(F32)
    per_token = jnp.sum(chosen, axis=1)
    count = ids.shape[0]
    before = (jnp.arange(count)[:, None] > jnp.arange(count)[None, :]).astype(BF)
    earlier = jnp.dot(before, per_token.astype(BF), preferred_element_type=F32)
    position = jnp.sum(chosen * earlier[:, None, :], axis=-1).astype(jnp.int32)
    target = ids * capacity + position
    columns = jnp.arange(expert_count * capacity, dtype=jnp.int32)
    hit = (target[:, 0][None, :] == columns[:, None]) | (target[:, 1][None, :] == columns[:, None])
    return hit.astype(BF)


def use_kernel(blocks, first, last, index, *refs):
    it = iter(refs)
    x_refs = [next(it) for _ in range(blocks)]
    w_mine = [next(it) for _ in range(blocks)]
    w_theirs = [next(it) for _ in range(blocks)]
    s_a, s_b = next(it), next(it)
    acc_in = None
    if not first:
        acc_in, _, _ = next(it), next(it), next(it)
    acc, g_mine, g_theirs = next(it), next(it), next(it)
    width = s_a.shape[1]
    flags = index.shape[0] - 2
    own = index[flags] == 1
    s_mine = jnp.where(own, s_a[...], s_b[...])
    s_theirs = jnp.where(own, s_b[...], s_a[...])
    s = jnp.concatenate([s_mine, s_theirs], axis=1)
    for b in range(blocks):
        x = x_refs[b][...]
        w = jnp.concatenate([w_mine[b][0], w_theirs[b][0]], axis=1)
        product = jnp.dot(x, w, preferred_element_type=F32)
        if last:
            total = product + acc_in[...]
        elif b == 0:
            acc[...] = product if first else product + acc_in[...]
        else:
            acc[...] += product
        outer = lax.dot_general(x, s, (((0,), (0,)), ((), ())), preferred_element_type=F32)
        g_mine[b] = outer[:, :width].astype(BF)
        g_theirs[b] = outer[:, width:].astype(BF)
    if last:
        sum_a, sum_b, mix = next(it), next(it), next(it)
        mine, theirs = total[:, :width], total[:, width:]
        acc[...] = mine
        sum_b[...] = theirs.astype(BF)
        sum_a[...] = jnp.where(own, theirs, mine).astype(BF)
        terms = s_mine.astype(F32) * mine + s_theirs.astype(F32) * theirs
        line = lax.dot_general(
            jnp.ones((8, width), F32),
            terms,
            (((1,), (1,)), ((), ())),
            precision=lax.Precision.HIGHEST,
            preferred_element_type=F32,
        )
        row = lax.broadcasted_iota(jnp.int32, (2, line.shape[1]), 0)
        mix[...] = jnp.where(row == index[flags + 1], line[:2], 0.0)


def use(pieces, index, start, w_mine, w_theirs, s_a, s_b, held, last=False):
    first = held is None
    blocks = len(pieces)
    rows, width = s_a.shape
    total, chip, _ = w_mine.shape
    assert start % blocks == 0

    def whole(a):
        return pl.BlockSpec(a.shape, lambda i, idx: (0,) * len(a.shape))

    def pick(j):
        return pl.BlockSpec((1, chip, width), lambda i, idx: (idx[start + j], 0, 0))

    ins = list(pieces) + [w_mine] * blocks + [w_theirs] * blocks + [s_a, s_b]
    specs = [whole(a) for a in pieces] + [pick(j) for j in range(blocks)] * 2 + [whole(s_a), whole(s_b)]
    aliases = {}
    if not first:
        n = 1 + len(ins)
        aliases = {n + 1: 1, n + 2: 2} if last else {n: 0, n + 1: 1, n + 2: 2}
        ins += list(held)
        specs += [whole(held[0]), pl.BlockSpec(memory_space=pl.ANY), pl.BlockSpec(memory_space=pl.ANY)]
    slot = pl.BlockSpec((blocks, chip, width), lambda i, idx: (start // blocks, 0, 0))
    sums = (rows, width if last else 2 * width)
    outs = [pltpu.HBM(sums, F32) if last else jax.ShapeDtypeStruct(sums, F32)]
    outs += [pltpu.HBM((total, chip, width), BF)] * 2
    extra = []
    if last:
        extra = [jax.ShapeDtypeStruct((rows, width), BF)] * 2 + [jax.ShapeDtypeStruct((2, rows), F32)]
    return pl.pallas_call(
        functools.partial(use_kernel, blocks, first, last),
        grid_spec=pltpu.PrefetchScalarGridSpec(
            num_scalar_prefetch=1,
            grid=(1,),
            in_specs=specs,
            out_specs=[pl.BlockSpec(sums, lambda i, idx: (0, 0)), slot, slot] + [whole(o) for o in extra],
        ),
        out_shape=outs + extra,
        input_output_aliases=aliases,
        compiler_params=pltpu.CompilerParams(vmem_limit_bytes=VMEM_LIMIT),
        cost_estimate=pl.CostEstimate(
            flops=8 * blocks * rows * chip * width, bytes_accessed=blocks * 4000000, transcendentals=0
        ),
    )(index, *ins)


def place_kernel(partner, index, mine, theirs, out):
    for i, p in enumerate(partner):
        out[index[i]] = (mine[i].astype(F32) + theirs[p].astype(F32)).astype(BF)


def place(index, partner, mine, theirs):
    def whole(a):
        return pl.BlockSpec(a.shape, lambda i, idx: (0, 0, 0))

    mine = pltpu.with_memory_space_constraint(mine, pltpu.HBM)
    return pl.pallas_call(
        functools.partial(place_kernel, tuple(partner)),
        grid_spec=pltpu.PrefetchScalarGridSpec(
            num_scalar_prefetch=1,
            grid=(1,),
            in_specs=[whole(mine), whole(theirs)],
            out_specs=whole(mine),
        ),
        out_shape=jax.ShapeDtypeStruct(mine.shape, BF),
        compiler_params=pltpu.CompilerParams(vmem_limit_bytes=16 * 1024 * 1024),
        cost_estimate=pl.CostEstimate(flops=1000000, bytes_accessed=5000000, transcendentals=0),
    )(index, mine, theirs)


def finish_kernel(index, own, got_a, got_b, gate_ref, up_ref, combine_ref, out_gate, out_up):
    flags = index.shape[0] - 2
    total = jnp.where(index[flags] == 1, own[...], got_b[...].astype(F32)) + got_a[...].astype(F32)
    gate = gate_ref[...].astype(F32)
    sigma = jax.nn.sigmoid(gate)
    scale = combine_ref[...]
    weighted = jnp.concatenate([scale] * (gate.shape[1] // scale.shape[1]), axis=1) * total
    out_gate[...] = (weighted * up_ref[...].astype(F32) * sigma * (1.0 + gate * (1.0 - sigma))).astype(BF)
    out_up[...] = (weighted * (gate * sigma)).astype(BF)


def finish(index, own, got_a, got_b, gate, up, combine_wide):
    in_hbm = lambda a: pltpu.with_memory_space_constraint(a, pltpu.HBM)
    ins = (in_hbm(own), got_a, got_b, in_hbm(gate), in_hbm(up), in_hbm(combine_wide))

    def whole(a):
        return pl.BlockSpec(a.shape, lambda i, idx: (0, 0))

    return pl.pallas_call(
        finish_kernel,
        grid_spec=pltpu.PrefetchScalarGridSpec(
            num_scalar_prefetch=1,
            grid=(1,),
            in_specs=[whole(a) for a in ins],
            out_specs=[whole(gate), whole(up)],
        ),
        out_shape=[pltpu.HBM(gate.shape, BF)] * 2,
        compiler_params=pltpu.CompilerParams(vmem_limit_bytes=16 * 1024 * 1024),
        cost_estimate=pl.CostEstimate(flops=3000000, bytes_accessed=3500000, transcendentals=200000),
    )(index, *ins)


def make_local(ny):
    half_y = ny // 2
    swap = [(0, 1), (1, 0)]

    def flat4(y, x, c, d):
        return ((y * 2 + x) * 2 + c) * 2 + d

    def shift(h):
        return (4 * h - 2) % ny

    def token_moves(cross):
        pairs = []
        for y in range(ny):
            for x in range(2):
                for c in range(2):
                    for d in range(2):
                        to_y = ((y % half_y) * 2 + x + shift(y // half_y)) % ny
                        to_x = 1 - c if cross else c
                        pairs.append((flat4(y, x, c, d), flat4(to_y, to_x, d, y // half_y)))
        return pairs

    def flat2(c, d):
        return c * 2 + d

    scaled_a = [(flat2(c, k), flat2(k, c)) for c in range(2) for k in range(2)]
    scaled_b = [(flat2(c, k), flat2(k, 1 - c)) for c in range(2) for k in range(2)]
    sums_a = [(flat2(1 - g, g), flat2(1 - g, 1 - g)) for g in range(2)] + [
        (flat2(g, g), flat2(1 - g, g)) for g in range(2)
    ]
    sums_b = [(flat2(1 - g, g), flat2(g, 1 - g)) for g in range(2)]
    ring_a = [(y * 2 + c, ((y + 1 - 2 * c) % ny) * 2 + c) for y in range(ny) for c in range(2)]
    ring_b = [(y * 2 + c, ((y - 1 + 2 * c) % ny) * 2 + c) for y in range(ny) for c in range(2)]

    def local(cotangent, expert_ids, combine, gate_saved, up_saved, w_down):
        expert_count = lax.axis_size("expert")
        y = lax.axis_index("y")
        core = lax.axis_index("core")
        xlo = lax.axis_index("xlo")
        dp = lax.axis_index("dp")
        rows = gate_saved.shape[2]
        width = gate_saved.shape[3]
        capacity = rows // expert_count
        lanes = cotangent.shape[2]
        chip = 2 * lanes
        every = ("y", "xlo", "core", "dp")

        ids = expert_ids[0].astype(BF)
        moved = lax.ppermute(jnp.concatenate([cotangent[0], ids], axis=1), every, token_moves(False))
        across = lax.ppermute(cotangent[0], every, token_moves(True))
        mine = moved[:, :lanes]
        tokens = jnp.concatenate([jnp.where(xlo == 0, mine, across), jnp.where(xlo == 0, across, mine)], axis=1)
        table = one_hot_table(moved[:, lanes:].astype(jnp.int32), expert_count, capacity)
        outgoing = jnp.dot(table, tokens, preferred_element_type=F32).astype(BF)
        outgoing = outgoing.reshape(expert_count, capacity, chip)
        part = lax.all_to_all(outgoing, "expert", split_axis=0, concat_axis=0, tiled=True)

        gate = gate_saved[0, 0].astype(F32)
        upper = up_saved[0, 0].astype(F32)
        weight_rows = combine[0, 0][:, None]
        sigma = jax.nn.sigmoid(gate)
        active = gate * sigma
        combine_wide = jnp.broadcast_to(weight_rows, (rows, 128))
        scaled = (weight_rows * (active * upper)).astype(BF)
        w_moved = lax.ppermute(w_down[0], "core", swap)

        held_own = dp == core
        share = rows // (ny * 4)
        blk = (y * 2 + xlo) * 2 + core
        combine_share = lax.dynamic_slice_in_dim(combine[0, 0], blk * share, share, 0)
        combine_share, scaled = lax.optimization_barrier((combine_share, scaled))
        s_a = lax.ppermute(scaled, ("core", "dp"), scaled_a)
        s_b = lax.ppermute(scaled, ("core", "dp"), scaled_b)
        turn = jnp.where(core == 0, -1, 1)
        shift_here = jnp.where(dp == 0, shift(0), shift(1))
        order = []
        for step in range(1, half_y):
            order += [step, -step]
        order += [0, half_y]
        partner = [order.index(-o) if abs(o) < half_y else order.index(o) for o in order]
        spots = [(y + turn * o + 2 * ny - shift_here) % ny for o in order]
        index = jnp.stack(spots + [held_own.astype(jnp.int32), core]).astype(jnp.int32)
        on_a = lambda v: lax.ppermute(v, ("y", "core"), ring_a)
        on_b = lambda v: lax.ppermute(v, ("y", "core"), ring_b)
        block = part.reshape(rows, chip)
        block, s_a, s_b = lax.optimization_barrier((block, s_a, s_b))
        a = on_a(block)
        args = (w_down[0].reshape(ny, chip, width), w_moved.reshape(ny, chip, width), s_a, s_b)
        held = use([block], index, ny - 2, *args, None)
        block_b, acc = lax.optimization_barrier((block, held[0]))
        held = (acc, *held[1:])
        b = on_b(block_b)
        a_next = on_a(a)
        for step in range(1, half_y):
            blocks = [a, b]
            a = a_next
            if step < half_y - 1:
                b = on_b(b)
            held = use(blocks, index, 2 * (step - 1), *args, held)
            if step < half_y - 1:
                a, acc = lax.optimization_barrier((a, held[0]))
                held = (acc, *held[1:])
                a_next = on_a(a)
        acc, combine_wide = lax.optimization_barrier((held[0], combine_wide))
        held = (acc, *held[1:])
        acc, mine, theirs, sum_a, sum_b, mix = use([a], index, ny - 1, *args, held, last=True)

        got_a = lax.ppermute(sum_a, ("core", "dp"), sums_a)
        got_b = lax.ppermute(sum_b, ("core", "dp"), sums_b)
        members = 2 * ny * 4
        mix = lax.all_to_all(mix.reshape(members, share), ("dp", "y", "xlo", "core"), 0, 0, tiled=True)
        late = lax.ppermute(theirs, "core", swap)
        grad_weight = place(index, partner, mine, late).reshape(ny * chip, width)
        grad_gate, grad_upper = finish(index, acc, got_a, got_b, gate_saved[0, 0], up_saved[0, 0], combine_wide)
        mix, grad_gate, grad_upper, grad_weight = lax.optimization_barrier((mix, grad_gate, grad_upper, grad_weight))
        mix = jnp.sum(mix, axis=0)
        mix = mix / combine_share
        return grad_gate[None, None], grad_upper[None, None], grad_weight[None], mix[None, None]

    return local


def solution(mesh):
    ne, nb, nd = mesh.devices.shape
    fine = Mesh(mesh.devices.reshape(ne, nb // 4, 2, 2, nd), ("expert", "y", "xlo", "core", "dp"))
    blk = ("y", "xlo", "core")
    return jax.shard_map(
        make_local(nb // 4),
        mesh=fine,
        in_specs=(
            P("dp", "expert", blk),
            P("dp", "expert", None),
            P("dp", "expert", None),
            P("dp", "expert", None, blk),
            P("dp", "expert", None, blk),
            P("expert", "dp", blk),
        ),
        out_specs=(
            P("dp", "expert", None, blk),
            P("dp", "expert", None, blk),
            P("expert", "dp", blk),
            P("dp", "expert", blk),
        ),
        check_vma=False,
    )
```
